32 devices in a mesh: dp: 8 (over y, x, core), seq: 4 (over z).
Axes of the slice: x: 2, y: 2, z: 4, core: 2. Of those that a mesh axis runs over, the one named last changes fastest.
Arguments:
- frames: bfloat16 [8, 2, 1024, 1024], P('dp', None, 'seq'), may hold values from -6 to 6
- cotangent: bfloat16 [8, 2, 1024, 1024], P('dp', None, 'seq'), may hold values from -6 to 6
- lengths: int32 [8, 2], replicated, may hold values from 50 to 1024, as said below
- assignment: int32 [8], replicated, may hold values from 0 to 7, each once
- norm_gains: bfloat16 [6, 1024], P(None, 'seq'), may hold values from 0.5 to 1.5
- norm_biases: bfloat16 [6, 1024], P(None, 'seq'), may hold values from -2 to 2
- expand_one: bfloat16 [1024, 4096], P('seq'), may hold values from -0.1875 to 0.1875
- shrink_one: bfloat16 [4096, 1024], P('seq'), may hold values from -0.09375 to 0.09375
- qkv_weight: bfloat16 [1024, 3072], P('seq'), may hold values from -0.25 to 0.25
- pos_weight: bfloat16 [1024, 1024], P(None, 'seq'), may hold values from -0.1875 to 0.1875
- pos_biases: bfloat16 [2, 1024], P(None, 'seq'), may hold values from -3 to 3
- attn_out: bfloat16 [1024, 1024], P('seq'), may hold values from -0.25 to 0.25
- conv_in: bfloat16 [1024, 2048], P('seq'), may hold values from -0.1875 to 0.1875
- conv_depth: bfloat16 [5, 1024], P(None, 'seq'), may hold values from -2.5 to 2.5
- conv_out: bfloat16 [1024, 1024], P('seq'), may hold values from -0.1875 to 0.1875
- expand_two: bfloat16 [1024, 4096], P('seq'), may hold values from -0.1875 to 0.1875
- shrink_two: bfloat16 [4096, 1024], P('seq'), may hold values from -0.25 to 0.25
Outputs:
- encoded: bfloat16 [8, 2, 1024, 1024], P('dp', None, 'seq')
- grad_input: float32 [8, 2, 1024, 1024], P('dp', None, 'seq')
- grad_norm_gains: float32 [6, 1024], P(None, 'seq')
- grad_norm_biases: float32 [6, 1024], P(None, 'seq')
- grad_expand_one: float32 [1024, 4096], P('seq')
- grad_shrink_one: float32 [4096, 1024], P('seq')
- grad_qkv_weight: float32 [1024, 3072], P('seq')
- grad_pos_weight: float32 [1024, 1024], P(None, 'seq')
- grad_pos_biases: float32 [2, 1024], P(None, 'seq')
- grad_attn_out: float32 [1024, 1024], P('seq')
- grad_conv_in: float32 [1024, 2048], P('seq')
- grad_conv_depth: float32 [5, 1024], P(None, 'seq')
- grad_conv_out: float32 [1024, 1024], P('seq')
- grad_expand_two: float32 [1024, 4096], P('seq')
- grad_shrink_two: float32 [4096, 1024], P('seq')
The draws below stay inside these ranges and needn't reach their ends.
Inputs may be any that keep to these rules, and one draw needn't show every extreme that they name: lengths[b, u] is the number of real frames of utterance u of batch b; in every batch one utterance, which one drawn from the seed, has 1024 frames. A permutation: row g of frames and cotangent is batch assignment[g], whose lengths are row assignment[g] of lengths.
All inputs are finite; a program needn't handle non-finite values.
Results may differ from the reference program's by a relative error of at most 0.024.
Values may be sent and summed in bfloat16 or wider, within the bound.
A program may use at most 320 MiB of HBM per device.

```python
import math
import jax
import jax.numpy as jnp
from jax import lax

D = 1024
FF = 4096
HEADS = 8
HEAD_DIM = 128
KERNEL = 5
UTT = 2
LEN = 1024
QUERY_BLOCK = 512
BATCHES = 8


def draw_lengths(key, part):
    key = jax.random.fold_in(key, 11)
    length_key, chooser_key = jax.random.split(key)
    shortest = min(50, LEN // 2)
    drawn = jax.random.randint(length_key, (BATCHES, UTT), shortest, LEN + 1, dtype=jnp.int32)
    chosen = jax.random.randint(chooser_key, (BATCHES, 1), 0, UTT, dtype=jnp.int32)
    column = jnp.arange(UTT, dtype=jnp.int32)[None, :]
    return jnp.where(column == chosen, LEN, drawn).astype(jnp.int32)


def levels(own_key, shape, cuts, low, top_value):
    level, own = 1.0, jax.random.fold_in(own_key, 6)
    for position, shards_of in cuts:
        heights = jnp.exp(jax.random.uniform(jax.random.fold_in(own, position), (shards_of,), jnp.float32, low / len(cuts), top_value / len(cuts)))
        level = level * jnp.repeat(heights, shape[position] // shards_of).reshape([-1 if axis == position else 1 for axis in range(len(shape))])
    return level


def normal_values(stream_key, shape, width, limit, cuts=(), held_as=jnp.bfloat16):
    result = jax.random.normal(stream_key, shape, jnp.float32) * width
    if len(cuts) > 0:
        result = levels(stream_key, shape, cuts, -0.22, 0.18) * result
    return jnp.clip(result, min=-limit, max=limit).astype(held_as)


def setup_inputs(seed: int = 0) -> dict:
    arg_keys = jax.random.split(jax.random.key(seed), 18)
    return {
        "frames": normal_values(arg_keys[0], (BATCHES, UTT, LEN, D), 1.0, 6.0, ((0, 8), (2, 4))),
        "cotangent": normal_values(arg_keys[1], (BATCHES, UTT, LEN, D), 1.0, 6.0, ((0, 8), (2, 4))),
        "lengths": draw_lengths(jax.random.fold_in(arg_keys[17], 71), 0),
        "assignment": jax.random.permutation(arg_keys[3], BATCHES).astype(jnp.int32),
        "norm_gains": jnp.clip(1.0 + 0.1 * jax.random.normal(arg_keys[4], (6, D), jnp.float32), 0.5, 1.5).astype(jnp.bfloat16),
        "norm_biases": normal_values(arg_keys[5], (6, D), 0.3, 2.0, ((1, 4),)),
        "expand_one": normal_values(arg_keys[6], (D, FF), D ** -0.5, 0.1875, ((0, 4),)),
        "shrink_one": normal_values(arg_keys[7], (FF, D), FF ** -0.5, 0.09375, ((0, 4),)),
        "qkv_weight": normal_values(arg_keys[8], (D, 3 * D), (D // 2) ** -0.5, 0.25, ((0, 4),)),
        "pos_weight": normal_values(arg_keys[9], (D, D), D ** -0.5, 0.1875, ((1, 4),)),
        "pos_biases": normal_values(arg_keys[10], (2, D), 0.5, 3.0, ((1, 4),)),
        "attn_out": normal_values(arg_keys[11], (D, D), (D // 2) ** -0.5, 0.25, ((0, 4),)),
        "conv_in": normal_values(arg_keys[12], (D, 2 * D), D ** -0.5, 0.1875, ((0, 4),)),
        "conv_depth": normal_values(arg_keys[13], (KERNEL, D), KERNEL ** -0.5, 2.5, ((1, 4),)),
        "conv_out": normal_values(arg_keys[14], (D, D), D ** -0.5, 0.1875, ((0, 4),)),
        "expand_two": normal_values(arg_keys[15], (D, FF), D ** -0.5, 0.1875, ((0, 4),)),
        "shrink_two": normal_values(arg_keys[16], (FF, D), (FF // 8) ** -0.5, 0.25, ((0, 4),)),
    }


EPSILON = 1e-05
HIGHEST = lax.Precision.HIGHEST

@jax.custom_vjp
def low(v):
    return lax.optimization_barrier(v.astype(jnp.bfloat16)).astype(jnp.float32)

@jax.custom_vjp
def low_back(v):
    return v

def low_keep(v):
    return (low(v), None)

def low_pass(kept, grad):
    return (grad,)

def back_keep(v):
    return (v, None)

def back_low(kept, grad):
    return (low(grad),)
low.defvjp(low_keep, low_pass)
low_back.defvjp(back_keep, back_low)

def layer_norm(stream, norm_gain, offset):
    average = lax.optimization_barrier(jnp.mean(stream, axis=-1, keepdims=True))
    centred = stream - average
    spread = lax.optimization_barrier(jnp.mean(centred * centred, axis=-1, keepdims=True))
    return centred * lax.rsqrt(spread + EPSILON) * norm_gain + offset

def swish(stream):
    return stream * jax.nn.sigmoid(stream)

def position_table(length, features):
    indices = jnp.arange(2 * length, dtype=jnp.int32)
    distance = (length - 1 - indices).astype(jnp.float32)
    halves = jnp.arange(features // 2, dtype=jnp.int32).astype(jnp.float32)
    frequency = jnp.exp(halves * (-2.0 * math.log(10000.0) / features))
    angles = distance[:, None] * frequency[None, :]
    return jnp.stack([jnp.sin(angles), jnp.cos(angles)], axis=-1).reshape(2 * length, features)

def skew(placed, block_rows, length):
    leading = placed.shape[:-2]
    span_width = placed.shape[-1]
    flattened = placed.reshape(leading + (block_rows * span_width,))
    flattened = flattened[..., block_rows - 1:block_rows - 1 + block_rows * (span_width - 1)]
    return flattened.reshape(leading + (block_rows, span_width - 1))[..., :length]

def product(left, right, form):
    return jnp.einsum(form, left, right, precision=HIGHEST)

def feed_forward(stream, norm_gain, offset, expand_weight, shrink_weight):
    normed = low(layer_norm(stream, norm_gain, offset))
    hidden = low_back(product(normed, expand_weight, 'utd,df->utf'))
    active = low(swish(hidden))
    return low_back(product(active, shrink_weight, 'utf,fd->utd'))

def attention(stream, norm_gain, offset, qkv_weight, pos_weight, pos_biases, out_weight, lengths_row):
    utterances = stream.shape[0]
    normed = low(layer_norm(stream, norm_gain, offset))
    packed = low_back(low(product(normed, qkv_weight, 'utd,de->ute')))
    packed = packed.reshape(utterances, LEN, 3, HEADS, HEAD_DIM)
    queries = packed[:, :, 0]
    keys_all = packed[:, :, 1]
    values_all = packed[:, :, 2]
    sinusoid = low(position_table(LEN, D))
    projected = low_back(low(product(sinusoid, pos_weight, 'rd,de->re'))).reshape(2 * LEN, HEADS, HEAD_DIM)
    content_query = low(queries + pos_biases[0].reshape(HEADS, HEAD_DIM))
    position_query = low(queries + pos_biases[1].reshape(HEADS, HEAD_DIM))
    keeping = (jnp.arange(LEN, dtype=jnp.int32)[None, :] < lengths_row[:, None])[:, None, None, :]
    span_width = LEN + QUERY_BLOCK
    scaling = 1.0 / math.sqrt(HEAD_DIM)

    def one_block(block_index):
        starting = (block_index * QUERY_BLOCK).astype(jnp.int32)
        content_block = lax.dynamic_slice_in_dim(content_query, starting, QUERY_BLOCK, 1)
        position_block = lax.dynamic_slice_in_dim(position_query, starting, QUERY_BLOCK, 1)
        lowest = (LEN - QUERY_BLOCK - starting).astype(jnp.int32)
        window = lax.dynamic_slice_in_dim(projected, lowest, span_width, 0)
        content = product(content_block, keys_all, 'uahe,ujhe->uhaj')
        placed = product(position_block, window, 'uahe,mhe->uham')
        scores = low_back(content + skew(placed, QUERY_BLOCK, LEN))
        logits = jnp.where(keeping, scores * scaling, -1000000000.0)
        maximum = lax.optimization_barrier(jnp.max(logits, axis=-1, keepdims=True))
        exponent = jnp.exp(logits - maximum)
        weights = low(exponent / lax.optimization_barrier(jnp.sum(exponent, axis=-1, keepdims=True)))
        return product(weights, values_all, 'uhaj,ujhe->uahe')
    blocks = lax.map(jax.checkpoint(one_block), jnp.arange(LEN // QUERY_BLOCK, dtype=jnp.int32))
    mixture = jnp.moveaxis(blocks, 0, 1).reshape(utterances, LEN, D)
    mixture = low_back(low(mixture))
    return low_back(product(mixture, out_weight, 'ute,ed->utd'))

def convolution(stream, norm_gain, offset, in_weight, depth_weight, inner_gain, inner_offset, out_weight, validity):
    normed = low(layer_norm(stream, norm_gain, offset))
    doubled = low_back(product(normed, in_weight, 'utd,de->ute'))
    gated_rows = low(doubled[..., :D] * jax.nn.sigmoid(doubled[..., D:]) * validity[..., None])
    margin = (KERNEL - 1) // 2
    padded = jnp.pad(gated_rows, ((0, 0), (margin, margin), (0, 0)))
    depthwise = depth_weight[0] * padded[:, 0:LEN]
    for shift_index in range(1, KERNEL):
        depthwise = depthwise + depth_weight[shift_index] * padded[:, shift_index:shift_index + LEN]
    depthwise = low_back(depthwise)
    active = low(swish(layer_norm(depthwise, inner_gain, inner_offset)))
    return low_back(product(active, out_weight, 'utd,de->ute'))

def forward(params, frames_batch, lengths_row):
    gains, offsets, expand_one, shrink_one, qkv_weight, pos_weight, pos_biases, attn_out, conv_in, conv_depth, conv_out, expand_two, shrink_two = params
    validity = (jnp.arange(LEN, dtype=jnp.int32)[None, :] < lengths_row[:, None]).astype(jnp.float32)
    section_one = frames_batch + 0.5 * feed_forward(frames_batch, gains[0], offsets[0], expand_one, shrink_one)
    section_two = section_one + attention(section_one, gains[1], offsets[1], qkv_weight, pos_weight, pos_biases, attn_out, lengths_row)
    section_three = section_two + convolution(section_two, gains[2], offsets[2], conv_in, conv_depth, gains[3], offsets[3], conv_out, validity)
    section_four = section_three + 0.5 * feed_forward(section_three, gains[4], offsets[4], expand_two, shrink_two)
    return layer_norm(section_four, gains[5], offsets[5])

def reference(frames, cotangent, lengths, assignment, norm_gains, norm_biases, expand_one, shrink_one, qkv_weight, pos_weight, pos_biases, attn_out, conv_in, conv_depth, conv_out, expand_two, shrink_two):
    params = tuple((weight.astype(jnp.float32) for weight in (norm_gains, norm_biases, expand_one, shrink_one, qkv_weight, pos_weight, pos_biases, attn_out, conv_in, conv_depth, conv_out, expand_two, shrink_two)))
    batch_lengths = lengths[assignment]

    def one_batch(running, inputs):
        frames_batch, cot_batch, lengths_row = inputs

        def apply_layer(weights, stream):
            return forward(weights, stream, lengths_row)
        encoded_batch, pullback = jax.vjp(apply_layer, params, frames_batch.astype(jnp.float32))
        grad_params, grad_frames = pullback(cot_batch.astype(jnp.float32))
        running = jax.tree.map(jnp.add, running, grad_params)
        return (running, (encoded_batch.astype(jnp.bfloat16), grad_frames))
    starting_sums = jax.tree.map(jnp.zeros_like, params)
    totals, (encoded, grad_input) = lax.scan(one_batch, starting_sums, (frames, cotangent, batch_lengths))
    return (encoded, grad_input, totals[0], totals[1], totals[2], totals[3], totals[4], totals[5], totals[6], totals[7], totals[8], totals[9], totals[10], totals[11], totals[12])
```

```python
import functools
import math

import jax
import jax.numpy as jnp
from jax import lax
from jax.experimental import pallas as pl
from jax.experimental.pallas import tpu as pltpu
from jax.sharding import PartitionSpec as P

D = 1024
KERNEL = 5
EPSILON = 1e-05
MESH=pl.DeviceIdType.MESH

def place():
    dp=lax.axis_index("dp"); z=lax.axis_index("seq")
    c=dp%2; p=(dp//2)%4
    bx=p%2; by=p//2
    return dict(dp=dp,z=z,c=c,p=p,px=p+1-2*bx,py=p+2-4*by,
                core=dp+1-2*c, xn=dp+2-4*bx, yn=dp+4-8*by)

def gather_kernel(nw, nz, *refs):
    ins=refs[:nw]; small,fr,ct=refs[nw:nw+3]
    outs=refs[nw+3:2*nw+3]; small_o,fr_o,ct_o=refs[2*nw+3:2*nw+6]
    (zr,xr,yr,ar,br,cr,zsr,zsl,xs,ys,as_,bs,cs,loc,fs,frv)=refs[2*nw+6:]
    k=place(); dp,z,c,p=k["dp"],k["z"],k["c"],k["p"]
    here=lambda zz:(dp,zz)
    tcore=z//2; tdp=dp-c+tcore
    bar=pltpu.get_barrier_semaphore()
    def sig(dev): pl.semaphore_signal(bar,inc=1,device_id=dev,device_id_type=MESH)
    for n in ("core","xn","yn"): sig((k[n],z))
    for ok,zz in ((z>0,z-1),(z<nz-1,z+1)):
        @pl.when(ok)
        def _(): sig((dp,zz))
    for u in range(2):
        @pl.when(jnp.logical_or(tcore!=c, 2*c+u!=z))
        def _(): sig((tdp,2*c+u))
    one=lambda b: jnp.where(b,1,0)
    pl.semaphore_wait(bar,3+one(z>0)+one(z<nz-1)+2-one(tcore==c))
    def rc(src,dst,s,r,dev):
        return pltpu.make_async_remote_copy(src_ref=src,dst_ref=dst,send_sem=s,recv_sem=r,device_id=dev,device_id_type=MESH)
    allin=list(ins)+[small]; allout=list(outs)+[small_o]
    def piece(w,t,pp=None,half=None):
        if w==nw: return small_o.at[t]
        r=outs[w].at[t,p if pp is None else pp,c]
        if half is None: return r
        h=outs[w].shape[3]//2
        return r.at[pl.ds(half*h,h)]
    def own(w):
        return small if w==nw else ins[w].at[p,c]
    def zright(w,t,src=None): return rc(piece(w,t) if src is None else src,piece(w,t),zsr.at[w,t],zr.at[w,t],(dp,z+1))
    def zleft(w,t,src=None): return rc(piece(w,t) if src is None else src,piece(w,t),zsl.at[w,t],zr.at[w,t],(dp,z-1))
    def xsend(w,t): return rc(piece(w,t),piece(w,t),xs.at[w,t],xr.at[w,t],(k["xn"],z))
    def ysend(w,t): return rc(piece(w,t),piece(w,t),ys.at[w,t],yr.at[w,t],(k["yn"],z))
    def asend(w,t): return rc(piece(w,t,k["px"],0),piece(w,t,k["px"],0),as_.at[w,t],ar.at[w,t],(k["yn"],z))
    def bsend(w,t): return rc(piece(w,t,k["py"],1),piece(w,t,k["py"],1),bs.at[w,t],br.at[w,t],(k["xn"],z))
    def csend(w,t): return rc(outs[w].at[t,:,c],outs[w].at[t,:,c],cs.at[w,t],cr.at[w,t],(k["core"],z))
    def local(w): return pltpu.make_async_copy(allin[w],allout[w].at[z],loc.at[w])
    redo=[(fr,fr_o,0),(ct,ct_o,1)]
    def move(a,u):
        s,d,i=redo[a]
        return rc(s.at[u],d.at[z%2],fs.at[i,u],frv.at[i,z%2],(tdp,2*c+u))
    def keep(a):
        s,d,i=redo[a]
        return pltpu.make_async_copy(s.at[z%2],d.at[z%2],loc.at[nw+1+i])
    def moves(a,f_remote,f_local):
        for u in range(2):
            @pl.when(jnp.logical_or(tcore!=c,2*c+u!=z))
            def _(): f_remote(a,u)
        @pl.when(tcore==c)
        def _(): f_local(a)
    def away(f):
        for d in range(1,nz):
            @pl.when(z-d>=0)
            def _(): f(z-d,True)
            @pl.when(z+d<nz)
            def _(): f(z+d,False)
    moves(0,lambda a,u:move(a,u).start(),lambda a:keep(a).start())
    def go(w):
        @pl.when(z<nz-1)
        def _(): zright(w,z,own(w)).start()
        @pl.when(z>0)
        def _(): zleft(w,z,own(w)).start()
    def f1(w,t,fromleft):
        zright(w,t).wait_recv()
        if fromleft:
            @pl.when(z<nz-1)
            def _(): zright(w,t).start()
        else:
            @pl.when(z>0)
            def _(): zleft(w,t).start()
        if w<nw:
            xsend(w,t).start(); ysend(w,t).start()
    def f2(w,t,_):
        xsend(w,t).wait_recv(); asend(w,t).start()
        ysend(w,t).wait_recv(); bsend(w,t).start()
    def f3(w,t,_):
        asend(w,t).wait_recv(); bsend(w,t).wait_recv(); csend(w,t).start()
    def at(f,w,d):
        @pl.when(z-d>=0)
        def _(): f(w,z-d,True)
        @pl.when(z+d<nz)
        def _(): f(w,z+d,False)
    if True:
        for w in ([nw]+list(range(nw)))[:2]: go(w)
        for w in range(nw+1): local(w).start()
        for d in range(1,nz): at(f1,nw,d)
        for s in range(nw+2):
            for ww in (s+1,):
                if ww<nw: go(ww)
            if s==4: moves(1,lambda a,u:move(a,u).start(),lambda a:keep(a).start())
            for f,ww in ((f1,s),(f2,s-1),(f3,s-2)):
                if 0<=ww<nw:
                    for d in range(1,nz): at(f,ww,d)
    def away(f):
        for d in range(1,nz):
            @pl.when(z-d>=0)
            def _(): f(z-d,True)
            @pl.when(z+d<nz)
            def _(): f(z+d,False)
    for w in range(nw+1):
        local(w).wait()
        @pl.when(z<nz-1)
        def _(): zright(w,z,own(w)).wait_send()
        @pl.when(z>0)
        def _(): zleft(w,z,own(w)).wait_send()
        def f(t,fromleft):
            if fromleft:
                @pl.when(z<nz-1)
                def _(): zright(w,t).wait_send()
            else:
                @pl.when(z>0)
                def _(): zleft(w,t).wait_send()
            if w<nw:
                for g in (xsend,ysend,asend,bsend): g(w,t).wait_send()
                csend(w,t).wait()
        away(f)
    for a in range(2):
        moves(a,lambda a,u:move(a,u).wait_send(),lambda a:keep(a).wait())
        for pos in range(2):
            @pl.when(jnp.logical_or(tcore!=c,2*c+pos!=z))
            def _():
                s,d,i=redo[a]
                rc(s.at[pos],d.at[pos],fs.at[i,pos],frv.at[i,pos],(tdp,2*c+pos)).wait_recv()

def gather(ws,small,fr,ct,nz,cid=0):
    nw=len(ws)
    ins=[w.reshape(4,2,w.shape[0]//8,w.shape[1]) for w in ws]
    any_=pl.BlockSpec(memory_space=pl.ANY)
    shp=[jax.ShapeDtypeStruct((nz,)+w.shape,w.dtype) for w in ins]+[jax.ShapeDtypeStruct((nz,)+small.shape,small.dtype),jax.ShapeDtypeStruct(fr.shape,fr.dtype),jax.ShapeDtypeStruct(ct.shape,ct.dtype)]
    S=pltpu.SemaphoreType.DMA
    o=pl.pallas_call(functools.partial(gather_kernel,nw,nz),out_shape=shp,in_specs=[any_]*(nw+3),out_specs=[any_]*(nw+3),
        scratch_shapes=[S((nw+1,nz))]+[S((nw,nz))]*5+[S((nw+1,nz))]*2+[S((nw,nz))]*5+[S((nw+3,)),S((2,2)),S((2,2))],
        compiler_params=pltpu.CompilerParams(collective_id=cid,has_side_effects=True,vmem_limit_bytes=2**20),
        cost_estimate=pl.CostEstimate(flops=0,bytes_accessed=2*48*2**20,transcendentals=0),
    )(*ins,small,fr,ct)
    full=[x.reshape(nz*w.shape[0],w.shape[1]) for x,w in zip(o[:nw],ws)]
    return full,o[nw],o[nw+1],o[nw+2]

HD=128; SCALE=1.0/math.sqrt(128)
BLK=256
NT=(((1,),(1,)),((),()))
TN=(((0,),(0,)),((),()))
def dot(a,b,dims=(((1,),(0,)),((),()))):
    return lax.dot_general(a,b,dims,preferred_element_type=jnp.float32)

def order(first, own, oth):
    return jnp.concatenate([jnp.where(first, own, oth), jnp.where(first, oth, own)], axis=0)

def attn_fwd_kernel(sc_ref, q_ref, k_ref, v_ref, ko_ref, vo_ref, pt_ref, pb_ref, o_ref, p_ref):
    T=q_ref.shape[0]; L2=2*T
    first=sc_ref[0]==0; length=sc_ref[1]
    q=q_ref[...].astype(jnp.float32)
    pb=pb_ref[...].astype(jnp.float32)
    qu=(q+pb[0:1]).astype(jnp.bfloat16); qv=(q+pb[1:2]).astype(jnp.bfloat16)
    k=order(first,k_ref[...],ko_ref[...]); v=order(first,v_ref[...],vo_ref[...])
    W=BLK+L2
    keep=lax.broadcasted_iota(jnp.int32,(BLK,L2),1)<length
    for b in range(T//BLK):
        i0=b*BLK; w0=T-i0-BLK
        s=dot(qu[i0:i0+BLK],k,NT)
        pl_=dot(qv[i0:i0+BLK],pt_ref[w0:w0+W,:],NT)
        s=s+pltpu.roll(pl_,W-(BLK-1),1,stride=1,stride_axis=0)[:,:L2]
        s=jnp.where(keep,s*SCALE,-1e9)
        m=jnp.max(s,axis=-1,keepdims=True)
        e=jnp.exp(s-m)
        p=(e*(1.0/jnp.sum(e,axis=-1,keepdims=True))).astype(jnp.bfloat16)
        p_ref[0,i0:i0+BLK,:]=p
        o_ref[i0:i0+BLK,:]=dot(p,v).astype(jnp.bfloat16)

def attn_bwd_kernel(sc_ref, q_ref, k_ref, v_ref, ko_ref, vo_ref, pt_ref, pb_ref, g_ref, p_ref,
                    gq_ref, gk_ref, gv_ref, gko_ref, gvo_ref, gpt_ref, gb_ref, gpt_acc):
    T=q_ref.shape[0]; L2=2*T
    first=sc_ref[0]==0
    q=q_ref[...].astype(jnp.float32)
    pb=pb_ref[...].astype(jnp.float32)
    qu=(q+pb[0:1]).astype(jnp.bfloat16); qv=(q+pb[1:2]).astype(jnp.bfloat16)
    k=order(first,k_ref[...],ko_ref[...]); v=order(first,v_ref[...],vo_ref[...])
    W=BLK+L2
    flip=(lax.broadcasted_iota(jnp.int32,(BLK,BLK),0)+lax.broadcasted_iota(jnp.int32,(BLK,BLK),1)==BLK-1).astype(jnp.float32).astype(jnp.bfloat16)
    gpt_acc[...]=jnp.zeros_like(gpt_acc)
    gk=gv=None; su=sv=None
    for b in range(T//BLK):
        i0=b*BLK; w0=T-i0-BLK
        g=g_ref[i0:i0+BLK,:]
        pbf=p_ref[0,i0:i0+BLK,:]
        p=pbf.astype(jnp.float32)
        t=p*dot(g,v,NT)
        gl=t-p*jnp.sum(t,axis=-1,keepdims=True)
        gr=gl*SCALE
        grb=gr.astype(jnp.bfloat16)
        gvb=dot(pbf,g,TN); gkb=dot(grb,qu[i0:i0+BLK],TN)
        gv=gvb if gv is None else gv+gvb
        gk=gkb if gk is None else gk+gkb
        gqu=dot(grb,k)
        pad=jnp.concatenate([dot(flip,grb),jnp.zeros((BLK,BLK),jnp.float32)],axis=1)
        gp=pltpu.roll(pad,0,1,stride=1,stride_axis=0).astype(jnp.bfloat16)
        gpt_acc[w0:w0+W,:]+=dot(gp,dot(flip,qv[i0:i0+BLK]).astype(jnp.bfloat16),TN)
        gqv=lax.dot_general(flip.astype(jnp.float32),dot(gp,pt_ref[w0:w0+W,:]),(((1,),(0,)),((),())),precision=lax.Precision.HIGHEST,preferred_element_type=jnp.float32)
        gq_ref[i0:i0+BLK,:]=(gqu+gqv).astype(jnp.bfloat16)
        a=jnp.sum(gqu,axis=0,keepdims=True); c=jnp.sum(gqv,axis=0,keepdims=True)
        su=a if su is None else su+a; sv=c if sv is None else sv+c
    gpt_ref[...]=gpt_acc[...].astype(jnp.bfloat16)
    gk_ref[...]=jnp.where(first,gk[:T],gk[T:]); gv_ref[...]=jnp.where(first,gv[:T],gv[T:])
    gko_ref[...]=jnp.where(first,gk[T:],gk[:T]).astype(jnp.bfloat16); gvo_ref[...]=jnp.where(first,gv[T:],gv[:T]).astype(jnp.bfloat16)
    gb_ref[...]=jnp.concatenate([su,sv,jnp.zeros((6,su.shape[1]),jnp.float32)],axis=0)

def col(rows,off=0): return pl.BlockSpec((rows,HD),lambda h,off=off:(0,h+off))
def attn_fwd(sc,qkv,kvo,pt,pb):
    T=qkv.shape[0]; D=qkv.shape[1]//3; H=D//HD
    return pl.pallas_call(attn_fwd_kernel,grid=(H,),
        in_specs=[pl.BlockSpec(memory_space=pltpu.SMEM),col(T),col(T,H),col(T,2*H),col(T),col(T,H),col(3*T),col(pb.shape[0])],
        out_specs=[col(T),pl.BlockSpec((1,T,2*T),lambda h:(h,0,0))],
        out_shape=[jax.ShapeDtypeStruct((T,D),jnp.bfloat16),jax.ShapeDtypeStruct((H,T,2*T),jnp.bfloat16)],
        compiler_params=pltpu.CompilerParams(vmem_limit_bytes=48*2**20),
        cost_estimate=pl.CostEstimate(flops=H*T*2*T*HD*2*3,bytes_accessed=20*2**20,transcendentals=H*T*2*T),
    )(sc,qkv,qkv,qkv,kvo,kvo,pt,pb)
def attn_bwd(sc,qkv,kvo,pt,pb,g,p):
    T=qkv.shape[0]; D=qkv.shape[1]//3; H=D//HD
    f32=jnp.float32; bf=jnp.bfloat16
    return pl.pallas_call(attn_bwd_kernel,grid=(H,),
        in_specs=[pl.BlockSpec(memory_space=pltpu.SMEM),col(T),col(T,H),col(T,2*H),col(T),col(T,H),col(3*T),col(pb.shape[0]),col(T),pl.BlockSpec((1,T,2*T),lambda h:(h,0,0))],
        out_specs=[col(T)]*5+[col(3*T),col(8)],
        out_shape=[jax.ShapeDtypeStruct((T,D),bf),jax.ShapeDtypeStruct((T,D),f32),jax.ShapeDtypeStruct((T,D),f32),jax.ShapeDtypeStruct((T,D),bf),jax.ShapeDtypeStruct((T,D),bf),jax.ShapeDtypeStruct((3*T,D),bf),jax.ShapeDtypeStruct((8,D),f32)],
        scratch_shapes=[pltpu.VMEM((3*T,HD),f32)],
        compiler_params=pltpu.CompilerParams(vmem_limit_bytes=48*2**20),
        cost_estimate=pl.CostEstimate(flops=H*T*2*T*HD*2*6,bytes_accessed=30*2**20,transcendentals=0),
    )(sc,qkv,qkv,qkv,kvo,kvo,pt,pb,g,p)

def reduce_all(grads, g_small):
    outs = []
    for g in grads:
        part = lax.psum_scatter(g, ("seq", "dp"), scatter_dimension=0, tiled=True)
        outs.append(lax.all_gather(part, "dp", axis=0, tiled=True).astype(jnp.float32))
    width = g_small.shape[1] // lax.axis_size("seq")
    total = lax.psum(g_small.astype(jnp.bfloat16), ("dp", "seq")).astype(jnp.float32)
    return (*outs, lax.dynamic_slice_in_dim(total, lax.axis_index("seq") * width, width, axis=1))

def layer_norm(stream, gain, offset):
    average = jnp.mean(stream, axis=-1, keepdims=True)
    centred = stream - average
    spread = jnp.mean(centred * centred, axis=-1, keepdims=True)
    return centred * lax.rsqrt(spread + EPSILON) * gain + offset


def layer_norm_back(stream, gain, grad):
    average = jnp.mean(stream, axis=-1, keepdims=True)
    centred = stream - average
    spread = jnp.mean(centred * centred, axis=-1, keepdims=True)
    inverse = lax.rsqrt(spread + EPSILON)
    unit = centred * inverse
    scaled = grad * gain
    grad_stream = inverse * (
        scaled
        - jnp.mean(scaled, axis=-1, keepdims=True)
        - unit * jnp.mean(scaled * unit, axis=-1, keepdims=True)
    )
    return grad_stream, jnp.sum(grad * unit, axis=0), jnp.sum(grad, axis=0)


def swish(value):
    return value * jax.nn.sigmoid(value)


def swish_back(value, grad):
    gate = jax.nn.sigmoid(value)
    return grad * gate * (1.0 + value * (1.0 - gate))


def position_rows(first_row, rows, length, features):
    fine = 32
    column = lax.broadcasted_iota(jnp.int32, (1, features), 1)
    odd = column % 2 == 1
    frequency = jnp.exp((column // 2).astype(jnp.float32) * (-2.0 * math.log(10000.0) / features))
    coarse_at = (length - 1 - first_row - fine * jnp.arange(rows // fine, dtype=jnp.int32)).astype(jnp.float32)
    fine_at = jnp.arange(fine, dtype=jnp.int32).astype(jnp.float32)
    coarse = coarse_at[:, None] * frequency
    small = fine_at[:, None] * frequency
    coarse_sin, coarse_cos = jnp.sin(coarse), jnp.cos(coarse)
    lead = jnp.where(odd, coarse_cos, coarse_sin)[:, None, :]
    quarter = jnp.where(odd, -coarse_sin, coarse_cos)[:, None, :]
    table = lead * jnp.cos(small)[None] - quarter * jnp.sin(small)[None]
    return table.reshape(rows, features).astype(jnp.bfloat16)


def mm(left, right):
    return jnp.dot(left, right, preferred_element_type=jnp.float32)


def mm_nt(left, right):
    return lax.dot_general(left, right, NT, preferred_element_type=jnp.float32)


def mm_tn(left, right):
    return lax.dot_general(left, right, TN, preferred_element_type=jnp.float32).astype(jnp.bfloat16)


def pair_swap(value):
    count = lax.axis_size("dp")
    return lax.ppermute(value, "dp", [(i, i + 1 - 2 * (i % 2)) for i in range(count)])


def redistribute(value):
    dp_count, seq_count = lax.axis_size("dp"), lax.axis_size("seq")
    z = lax.axis_index("seq")
    routes = ([], [])
    for dp in range(dp_count):
        for zz in range(seq_count):
            a, b, c = zz // 2, zz % 2, dp % 2
            for which in range(2):
                routes[which].append(
                    (dp * seq_count + zz, (dp - c + a) * seq_count + 2 * c + (b + which) % 2)
                )
    low = z % 2 == 0
    straight = lax.ppermute(jnp.where(low, value[0], value[1]), ("dp", "seq"), routes[0])
    crossed = lax.ppermute(jnp.where(low, value[1], value[0]), ("dp", "seq"), routes[1])
    return jnp.stack([jnp.where(low, straight, crossed), jnp.where(low, crossed, straight)])


def with_halo(rows, core):
    margin = (KERNEL - 1) // 2
    got = pair_swap(jnp.where(core == 0, rows[-margin:], rows[:margin]))
    none = jnp.zeros_like(got)
    return jnp.concatenate([jnp.where(core == 1, got, none), rows, jnp.where(core == 0, got, none)], axis=0)


def shards(
    frames, cotangent, lengths, assignment, norm_gains, norm_biases, expand_one, shrink_one, qkv_weight,
    pos_weight, pos_biases, attn_out, conv_in, conv_depth, conv_out, expand_two, shrink_two,
):
    seq_count = lax.axis_size("seq")
    dp, z = lax.axis_index("dp"), lax.axis_index("seq")
    core = dp % 2
    own_length = lengths[assignment[dp - core + z // 2], z % 2]
    small = jnp.concatenate(
        [norm_gains, norm_biases, conv_depth, pos_biases, jnp.zeros((13, norm_gains.shape[1]), jnp.bfloat16)], axis=0
    )
    weights, small_all, x_in, cot = gather(
        [expand_one, shrink_one, qkv_weight, pos_weight, attn_out, conv_in, conv_out, expand_two, shrink_two],
        small, frames[0], cotangent[0], seq_count,
    )
    w1, w2, wqkv, wpos, wo, wci, wco, w3, w4 = weights
    wpos = wpos.reshape(seq_count, D, D // seq_count).transpose(1, 0, 2).reshape(D, D)
    vectors = small_all.transpose(1, 0, 2).reshape(32, D).astype(jnp.float32)
    gains, biases, depth, pos_pair = vectors[0:6], vectors[6:12], vectors[12:17], vectors[16:24]
    pos_pair = jnp.concatenate([vectors[17:19], jnp.zeros((6, D), jnp.float32)], axis=0)
    rows = 2 * frames.shape[2]
    x0 = x_in.reshape(rows, D).astype(jnp.float32)
    cot = cot.reshape(rows, D).astype(jnp.float32)
    valid = (core * rows + jnp.arange(rows, dtype=jnp.int32) < own_length).astype(jnp.float32)[:, None]

    h1 = layer_norm(x0, gains[0], biases[0]).astype(jnp.bfloat16)
    a1 = mm(h1, w1)
    s1 = swish(a1).astype(jnp.bfloat16)
    x1 = x0 + 0.5 * mm(s1, w2)
    ha = layer_norm(x1, gains[1], biases[1]).astype(jnp.bfloat16)
    qkv = mm(ha, wqkv).astype(jnp.bfloat16)
    kv_other = pair_swap(qkv[:, D:])
    sinusoid = position_rows((1 - core) * rows, 3 * rows, 2 * rows, D)
    ptab = mm(sinusoid, wpos).astype(jnp.bfloat16)
    scalars = jnp.stack([core, own_length]).astype(jnp.int32)
    attn, prob = attn_fwd(scalars, qkv, kv_other, ptab, pos_pair)
    x2 = x1 + mm(attn, wo)
    hc = layer_norm(x2, gains[2], biases[2]).astype(jnp.bfloat16)
    dbl = mm(hc, wci)
    gate = jax.nn.sigmoid(dbl[:, D:])
    m = (dbl[:, :D] * gate * valid).astype(jnp.bfloat16)
    rim = with_halo(m, core)
    cv = depth[0] * rim[0:rows]
    for tap in range(1, KERNEL):
        cv = cv + depth[tap] * rim[tap : tap + rows]
    sc = swish(layer_norm(cv, gains[3], biases[3])).astype(jnp.bfloat16)
    x3 = x2 + mm(sc, wco)
    h2 = layer_norm(x3, gains[4], biases[4]).astype(jnp.bfloat16)
    a2 = mm(h2, w3)
    s2 = swish(a2).astype(jnp.bfloat16)
    x4 = x3 + 0.5 * mm(s2, w4)
    encoded = layer_norm(x4, gains[5], biases[5]).astype(jnp.bfloat16)
    encoded = redistribute(encoded.reshape(2, rows // 2, D))

    gx4, gg5, gb5 = layer_norm_back(x4, gains[5], cot)
    go2 = (0.5 * gx4).astype(jnp.bfloat16)
    g_w4 = mm_tn(s2, go2)
    ga2 = swish_back(a2, mm_nt(go2, w4)).astype(jnp.bfloat16)
    g_w3 = mm_tn(h2, ga2)
    back, gg4, gb4 = layer_norm_back(x3, gains[4], mm_nt(ga2, w3))
    gx3 = gx4 + back
    gco = gx3.astype(jnp.bfloat16)
    g_wco = mm_tn(sc, gco)
    inner = layer_norm(cv, gains[3], biases[3])
    gcv, gg3, gb3 = layer_norm_back(cv, gains[3], swish_back(inner, mm_nt(gco, wco)))
    gcv = gcv.astype(jnp.bfloat16)
    grim = with_halo(gcv, core)
    gm = depth[0] * grim[KERNEL - 1 : KERNEL - 1 + rows]
    for tap in range(1, KERNEL):
        gm = gm + depth[tap] * grim[KERNEL - 1 - tap : KERNEL - 1 - tap + rows]
    g_depth = jnp.stack([
        jnp.sum(gcv.astype(jnp.float32) * rim[tap : tap + rows].astype(jnp.float32), axis=0) for tap in range(KERNEL)
    ])
    gm = gm * valid
    gdbl = jnp.concatenate(
        [(gm * gate).astype(jnp.bfloat16), (gm * dbl[:, :D] * gate * (1.0 - gate)).astype(jnp.bfloat16)], axis=1
    )
    g_wci = mm_tn(hc, gdbl)
    back, gg2, gb2 = layer_norm_back(x2, gains[2], mm_nt(gdbl, wci))
    gx2 = gx3 + back
    gao = gx2.astype(jnp.bfloat16)
    g_wo = mm_tn(attn, gao)
    gattn = mm_nt(gao, wo).astype(jnp.bfloat16)
    gq, gk, gv, gk_other, gv_other, gptab, g_pair = attn_bwd(scalars, qkv, kv_other, ptab, pos_pair, gattn, prob)
    got = pair_swap(jnp.concatenate([gk_other, gv_other], axis=1))
    gk = (gk + got[:, :D]).astype(jnp.bfloat16)
    gv = (gv + got[:, D:]).astype(jnp.bfloat16)
    gqkv = jnp.concatenate([gq, gk, gv], axis=1)
    g_wpos = mm_tn(sinusoid, gptab)
    g_wpos = g_wpos.reshape(D, seq_count, D // seq_count).transpose(1, 0, 2).reshape(seq_count * D, D // seq_count)
    g_wqkv = mm_tn(ha, gqkv)
    back, gg1, gb1 = layer_norm_back(x1, gains[1], mm_nt(gqkv, wqkv))
    gx1 = gx2 + back
    go1 = (0.5 * gx1).astype(jnp.bfloat16)
    g_w2 = mm_tn(s1, go1)
    ga1 = swish_back(a1, mm_nt(go1, w2)).astype(jnp.bfloat16)
    g_w1 = mm_tn(h1, ga1)
    back, gg0, gb0 = layer_norm_back(x0, gains[0], mm_nt(ga1, w1))
    gx0 = gx1 + back
    grad_input = redistribute(gx0.astype(jnp.bfloat16).reshape(2, rows // 2, D)).astype(jnp.float32)

    g_small = jnp.concatenate(
        [jnp.stack([gg0, gg1, gg2, gg3, gg4, gg5, gb0, gb1, gb2, gb3, gb4, gb5]), g_depth, g_pair[:2]], axis=0
    )
    outs = reduce_all([g_w1, g_w2, g_wqkv, g_wpos, g_wo, g_wci, g_wco, g_w3, g_w4], g_small)
    s_w1, s_w2, s_wqkv, s_wpos, s_wo, s_wci, s_wco, s_w3, s_w4, s_small = outs
    return (
        encoded[None], grad_input[None], s_small[0:6], s_small[6:12], s_w1, s_w2, s_wqkv, s_wpos, s_small[17:19],
        s_wo, s_wci, s_small[12:17], s_wco, s_w3, s_w4,
    )


def solution(mesh):
    rows, columns = P("seq", None), P(None, "seq")
    act = P("dp", None, "seq", None)
    return jax.shard_map(
        shards,
        mesh=mesh,
        in_specs=(act, act, P(), P(), columns, columns, rows, rows, rows, columns, columns, rows, rows, columns, rows, rows, rows),
        out_specs=(act, act, columns, columns, rows, rows, rows, columns, columns, rows, rows, columns, rows, rows, rows),
        check_vma=False,
    )
```

```python
import functools
import math

import jax
import jax.numpy as jnp
from jax import lax
from jax.experimental import pallas as pl
from jax.experimental.pallas import tpu as pltpu
from jax.sharding import PartitionSpec as P

D = 1024
KERNEL = 5
EPSILON = 1e-05
MESH=pl.DeviceIdType.MESH

def place():
    dp=lax.axis_index("dp"); z=lax.axis_index("seq")
    c=dp%2; p=(dp//2)%4
    bx=p%2; by=p//2
    return dict(dp=dp,z=z,c=c,p=p,px=p+1-2*bx,py=p+2-4*by,
                core=dp+1-2*c, xn=dp+2-4*bx, yn=dp+4-8*by)

def gather_kernel(nw, nz, *refs):
    ins=refs[:nw]; small,fr,ct=refs[nw:nw+3]
    outs=refs[nw+3:2*nw+3]; small_o,fr_o,ct_o=refs[2*nw+3:2*nw+6]
    (zr,xr,yr,ar,br,cr,zsr,zsl,xs,ys,as_,bs,cs,loc,fs,frv)=refs[2*nw+6:]
    k=place(); dp,z,c,p=k["dp"],k["z"],k["c"],k["p"]
    here=lambda zz:(dp,zz)
    tcore=z//2; tdp=dp-c+tcore
    bar=pltpu.get_barrier_semaphore()
    def sig(dev): pl.semaphore_signal(bar,inc=1,device_id=dev,device_id_type=MESH)
    for n in ("core","xn","yn"): sig((k[n],z))
    for ok,zz in ((z>0,z-1),(z<nz-1,z+1)):
        @pl.when(ok)
        def _(): sig((dp,zz))
    for u in range(2):
        @pl.when(jnp.logical_or(tcore!=c, 2*c+u!=z))
        def _(): sig((tdp,2*c+u))
    one=lambda b: jnp.where(b,1,0)
    pl.semaphore_wait(bar,3+one(z>0)+one(z<nz-1)+2-one(tcore==c))
    def rc(src,dst,s,r,dev):
        return pltpu.make_async_remote_copy(src_ref=src,dst_ref=dst,send_sem=s,recv_sem=r,device_id=dev,device_id_type=MESH)
    allin=list(ins)+[small]; allout=list(outs)+[small_o]
    def piece(w,t,pp=None,half=None):
        if w==nw: return small_o.at[t]
        r=outs[w].at[t,p if pp is None else pp,c]
        if half is None: return r
        h=outs[w].shape[3]//2
        return r.at[pl.ds(half*h,h)]
    def own(w):
        return small if w==nw else ins[w].at[p,c]
    def zright(w,t,src=None): return rc(piece(w,t) if src is None else src,piece(w,t),zsr.at[w,t],zr.at[w,t],(dp,z+1))
    def zleft(w,t,src=None): return rc(piece(w,t) if src is None else src,piece(w,t),zsl.at[w,t],zr.at[w,t],(dp,z-1))
    def xsend(w,t): return rc(piece(w,t),piece(w,t),xs.at[w,t],xr.at[w,t],(k["xn"],z))
    def ysend(w,t): return rc(piece(w,t),piece(w,t),ys.at[w,t],yr.at[w,t],(k["yn"],z))
    def asend(w,t): return rc(piece(w,t,k["px"],0),piece(w,t,k["px"],0),as_.at[w,t],ar.at[w,t],(k["yn"],z))
    def bsend(w,t): return rc(piece(w,t,k["py"],1),piece(w,t,k["py"],1),bs.at[w,t],br.at[w,t],(k["xn"],z))
    def csend(w,t): return rc(outs[w].at[t,:,c],outs[w].at[t,:,c],cs.at[w,t],cr.at[w,t],(k["core"],z))
    def local(w): return pltpu.make_async_copy(allin[w],allout[w].at[z],loc.at[w])
    redo=[(fr,fr_o,0),(ct,ct_o,1)]
    def move(a,u):
        s,d,i=redo[a]
        return rc(s.at[u],d.at[z%2],fs.at[i,u],frv.at[i,z%2],(tdp,2*c+u))
    def keep(a):
        s,d,i=redo[a]
        return pltpu.make_async_copy(s.at[z%2],d.at[z%2],loc.at[nw+1+i])
    def moves(a,f_remote,f_local):
        for u in range(2):
            @pl.when(jnp.logical_or(tcore!=c,2*c+u!=z))
            def _(): f_remote(a,u)
        @pl.when(tcore==c)
        def _(): f_local(a)
    def away(f):
        for d in range(1,nz):
            @pl.when(z-d>=0)
            def _(): f(z-d,True)
            @pl.when(z+d<nz)
            def _(): f(z+d,False)
    moves(0,lambda a,u:move(a,u).start(),lambda a:keep(a).start())
    def go(w):
        @pl.when(z<nz-1)
        def _(): zright(w,z,own(w)).start()
        @pl.when(z>0)
        def _(): zleft(w,z,own(w)).start()
    def f1(w,t,fromleft):
        zright(w,t).wait_recv()
        if fromleft:
            @pl.when(z<nz-1)
            def _(): zright(w,t).start()
        else:
            @pl.when(z>0)
            def _(): zleft(w,t).start()
        if w<nw:
            xsend(w,t).start(); ysend(w,t).start()
    def f2(w,t,_):
        xsend(w,t).wait_recv(); asend(w,t).start()
        ysend(w,t).wait_recv(); bsend(w,t).start()
    def f3(w,t,_):
        asend(w,t).wait_recv(); bsend(w,t).wait_recv(); csend(w,t).start()
    def at(f,w,d):
        @pl.when(z-d>=0)
        def _(): f(w,z-d,True)
        @pl.when(z+d<nz)
        def _(): f(w,z+d,False)
    if True:
        for w in ([nw]+list(range(nw)))[:2]: go(w)
        for w in range(nw+1): local(w).start()
        for d in range(1,nz): at(f1,nw,d)
        for s in range(nw+2):
            for ww in (s+1,):
                if ww<nw: go(ww)
            if s==4: moves(1,lambda a,u:move(a,u).start(),lambda a:keep(a).start())
            for f,ww in ((f1,s),(f2,s-1),(f3,s-2)):
                if 0<=ww<nw:
                    for d in range(1,nz): at(f,ww,d)
    def away(f):
        for d in range(1,nz):
            @pl.when(z-d>=0)
            def _(): f(z-d,True)
            @pl.when(z+d<nz)
            def _(): f(z+d,False)
    for w in range(nw+1):
        local(w).wait()
        @pl.when(z<nz-1)
        def _(): zright(w,z,own(w)).wait_send()
        @pl.when(z>0)
        def _(): zleft(w,z,own(w)).wait_send()
        def f(t,fromleft):
            if fromleft:
                @pl.when(z<nz-1)
                def _(): zright(w,t).wait_send()
            else:
                @pl.when(z>0)
                def _(): zleft(w,t).wait_send()
            if w<nw:
                for g in (xsend,ysend,asend,bsend): g(w,t).wait_send()
                csend(w,t).wait()
        away(f)
    for a in range(2):
        moves(a,lambda a,u:move(a,u).wait_send(),lambda a:keep(a).wait())
        for pos in range(2):
            @pl.when(jnp.logical_or(tcore!=c,2*c+pos!=z))
            def _():
                s,d,i=redo[a]
                rc(s.at[pos],d.at[pos],fs.at[i,pos],frv.at[i,pos],(tdp,2*c+pos)).wait_recv()

def gather(ws,small,fr,ct,nz,cid=0):
    nw=len(ws)
    ins=[w.reshape(4,2,w.shape[0]//8,w.shape[1]) for w in ws]
    any_=pl.BlockSpec(memory_space=pl.ANY)
    shp=[jax.ShapeDtypeStruct((nz,)+w.shape,w.dtype) for w in ins]+[jax.ShapeDtypeStruct((nz,)+small.shape,small.dtype),jax.ShapeDtypeStruct(fr.shape,fr.dtype),jax.ShapeDtypeStruct(ct.shape,ct.dtype)]
    S=pltpu.SemaphoreType.DMA
    o=pl.pallas_call(functools.partial(gather_kernel,nw,nz),out_shape=shp,in_specs=[any_]*(nw+3),out_specs=[any_]*(nw+3),
        scratch_shapes=[S((nw+1,nz))]+[S((nw,nz))]*5+[S((nw+1,nz))]*2+[S((nw,nz))]*5+[S((nw+3,)),S((2,2)),S((2,2))],
        compiler_params=pltpu.CompilerParams(collective_id=cid,has_side_effects=True,vmem_limit_bytes=2**20),
        cost_estimate=pl.CostEstimate(flops=0,bytes_accessed=2*48*2**20,transcendentals=0),
    )(*ins,small,fr,ct)
    full=[x.reshape(nz*w.shape[0],w.shape[1]) for x,w in zip(o[:nw],ws)]
    return full,o[nw],o[nw+1],o[nw+2]

HD=128; SCALE=1.0/math.sqrt(128)
BLK=256
NT=(((1,),(1,)),((),()))
TN=(((0,),(0,)),((),()))
def dot(a,b,dims=(((1,),(0,)),((),()))):
    return lax.dot_general(a,b,dims,preferred_element_type=jnp.float32)

def order(first, own, oth):
    return jnp.concatenate([jnp.where(first, own, oth), jnp.where(first, oth, own)], axis=0)

def attn_fwd_kernel(sc_ref, q_ref, k_ref, v_ref, ko_ref, vo_ref, pt_ref, pb_ref, o_ref, p_ref):
    T=q_ref.shape[0]; L2=2*T
    first=sc_ref[0]==0; length=sc_ref[1]
    q=q_ref[...].astype(jnp.float32)
    pb=pb_ref[...].astype(jnp.float32)
    qu=(q+pb[0:1]).astype(jnp.bfloat16); qv=(q+pb[1:2]).astype(jnp.bfloat16)
    k=order(first,k_ref[...],ko_ref[...]); v=order(first,v_ref[...],vo_ref[...])
    W=BLK+L2
    keep=lax.broadcasted_iota(jnp.int32,(BLK,L2),1)<length
    for b in range(T//BLK):
        i0=b*BLK; w0=T-i0-BLK
        s=dot(qu[i0:i0+BLK],k,NT)
        pl_=dot(qv[i0:i0+BLK],pt_ref[w0:w0+W,:],NT)
        s=s+pltpu.roll(pl_,W-(BLK-1),1,stride=1,stride_axis=0)[:,:L2]
        s=jnp.where(keep,s*SCALE,-1e9)
        m=jnp.max(s,axis=-1,keepdims=True)
        e=jnp.exp(s-m)
        p=(e*(1.0/jnp.sum(e,axis=-1,keepdims=True))).astype(jnp.bfloat16)
        p_ref[0,i0:i0+BLK,:]=p
        o_ref[i0:i0+BLK,:]=dot(p,v).astype(jnp.bfloat16)

def attn_bwd_kernel(sc_ref, q_ref, k_ref, v_ref, ko_ref, vo_ref, pt_ref, pb_ref, g_ref, p_ref,
                    gq_ref, gk_ref, gv_ref, gko_ref, gvo_ref, gpt_ref, gb_ref, gpt_acc):
    T=q_ref.shape[0]; L2=2*T
    first=sc_ref[0]==0
    q=q_ref[...].astype(jnp.float32)
    pb=pb_ref[...].astype(jnp.float32)
    qu=(q+pb[0:1]).astype(jnp.bfloat16); qv=(q+pb[1:2]).astype(jnp.bfloat16)
    k=order(first,k_ref[...],ko_ref[...]); v=order(first,v_ref[...],vo_ref[...])
    W=BLK+L2
    flip=(lax.broadcasted_iota(jnp.int32,(BLK,BLK),0)+lax.broadcasted_iota(jnp.int32,(BLK,BLK),1)==BLK-1).astype(jnp.float32).astype(jnp.bfloat16)
    gpt_acc[...]=jnp.zeros_like(gpt_acc)
    gk=gv=None; su=sv=None
    for b in range(T//BLK):
        i0=b*BLK; w0=T-i0-BLK
        g=g_ref[i0:i0+BLK,:]
        pbf=p_ref[0,i0:i0+BLK,:]
        p=pbf.astype(jnp.float32)
        t=p*dot(g,v,NT)
        gl=t-p*jnp.sum(t,axis=-1,keepdims=True)
        gr=gl*SCALE
        grb=gr.astype(jnp.bfloat16)
        gvb=dot(pbf,g,TN); gkb=dot(grb,qu[i0:i0+BLK],TN)
        gv=gvb if gv is None else gv+gvb
        gk=gkb if gk is None else gk+gkb
        gqu=dot(grb,k)
        pad=jnp.concatenate([dot(flip,grb),jnp.zeros((BLK,BLK),jnp.float32)],axis=1)
        gp=pltpu.roll(pad,0,1,stride=1,stride_axis=0).astype(jnp.bfloat16)
        gpt_acc[w0:w0+W,:]+=dot(gp,dot(flip,qv[i0:i0+BLK]).astype(jnp.bfloat16),TN)
        gqv=lax.dot_general(flip.astype(jnp.float32),dot(gp,pt_ref[w0:w0+W,:]),(((1,),(0,)),((),())),precision=lax.Precision.HIGHEST,preferred_element_type=jnp.float32)
        gq_ref[i0:i0+BLK,:]=(gqu+gqv).astype(jnp.bfloat16)
        a=jnp.sum(gqu,axis=0,keepdims=True); c=jnp.sum(gqv,axis=0,keepdims=True)
        su=a if su is None else su+a; sv=c if sv is None else sv+c
    gpt_ref[...]=gpt_acc[...].astype(jnp.bfloat16)
    gk_ref[...]=jnp.where(first,gk[:T],gk[T:]); gv_ref[...]=jnp.where(first,gv[:T],gv[T:])
    gko_ref[...]=jnp.where(first,gk[T:],gk[:T]).astype(jnp.bfloat16); gvo_ref[...]=jnp.where(first,gv[T:],gv[:T]).astype(jnp.bfloat16)
    gb_ref[...]=jnp.concatenate([su,sv,jnp.zeros((6,su.shape[1]),jnp.float32)],axis=0)

def col(rows,off=0): return pl.BlockSpec((rows,HD),lambda h,off=off:(0,h+off))
def attn_fwd(sc,qkv,kvo,pt,pb):
    T=qkv.shape[0]; D=qkv.shape[1]//3; H=D//HD
    return pl.pallas_call(attn_fwd_kernel,grid=(H,),
        in_specs=[pl.BlockSpec(memory_space=pltpu.SMEM),col(T),col(T,H),col(T,2*H),col(T),col(T,H),col(3*T),col(pb.shape[0])],
        out_specs=[col(T),pl.BlockSpec((1,T,2*T),lambda h:(h,0,0))],
        out_shape=[jax.ShapeDtypeStruct((T,D),jnp.bfloat16),jax.ShapeDtypeStruct((H,T,2*T),jnp.bfloat16)],
        compiler_params=pltpu.CompilerParams(vmem_limit_bytes=48*2**20),
        cost_estimate=pl.CostEstimate(flops=H*T*2*T*HD*2*3,bytes_accessed=20*2**20,transcendentals=H*T*2*T),
    )(sc,qkv,qkv,qkv,kvo,kvo,pt,pb)
def attn_bwd(sc,qkv,kvo,pt,pb,g,p):
    T=qkv.shape[0]; D=qkv.shape[1]//3; H=D//HD
    f32=jnp.float32; bf=jnp.bfloat16
    return pl.pallas_call(attn_bwd_kernel,grid=(H,),
        in_specs=[pl.BlockSpec(memory_space=pltpu.SMEM),col(T),col(T,H),col(T,2*H),col(T),col(T,H),col(3*T),col(pb.shape[0]),col(T),pl.BlockSpec((1,T,2*T),lambda h:(h,0,0))],
        out_specs=[col(T)]*5+[col(3*T),col(8)],
        out_shape=[jax.ShapeDtypeStruct((T,D),bf),jax.ShapeDtypeStruct((T,D),f32),jax.ShapeDtypeStruct((T,D),f32),jax.ShapeDtypeStruct((T,D),bf),jax.ShapeDtypeStruct((T,D),bf),jax.ShapeDtypeStruct((3*T,D),bf),jax.ShapeDtypeStruct((8,D),f32)],
        scratch_shapes=[pltpu.VMEM((3*T,HD),f32)],
        compiler_params=pltpu.CompilerParams(vmem_limit_bytes=48*2**20),
        cost_estimate=pl.CostEstimate(flops=H*T*2*T*HD*2*6,bytes_accessed=30*2**20,transcendentals=0),
    )(sc,qkv,qkv,qkv,kvo,kvo,pt,pb,g,p)

def reduce_kernel(chunks, nz, ng, *refs):
    n=len(chunks)
    gs=refs[:ng]; gi=refs[ng]; outs=refs[ng+1:2*ng+1]; gi_o=refs[2*ng+1]; cbig=refs[2*ng+2:2*ng+2+n]
    rest=list(refs[2*ng+2+n:])
    t1=rest[:2]; cin=rest[2:4]; rest=rest[4:]
    x1=rest[:n]; y1=rest[n:2*n]; x2=rest[2*n:3*n]; y2=rest[3*n:4*n]; zb=rest[4*n:5*n]
    (cs,cr,x1s,x1r,y1s,y1r,x2s,x2r,y2s,y2r,axs,axr,ays,ayr,aas,aar,abs_,abr,acs,acr,zrs,zrr,zls,zlr,own,cld,loc,fs,frv,keeps)=rest[5*n:]
    k=place(); dp,z,c=k["dp"],k["z"],k["c"]
    bx=k["p"]%2; by=k["p"]//2
    tcore=z//2; tdp=dp-c+tcore
    bar=pltpu.get_barrier_semaphore()
    def sig(dev): pl.semaphore_signal(bar,inc=1,device_id=dev,device_id_type=MESH)
    for a in ("core","xn","yn"): sig((k[a],z))
    for ok,zz in ((z>0,z-1),(z<nz-1,z+1)):
        @pl.when(ok)
        def _(): sig((dp,zz))
    for u in range(2):
        @pl.when(jnp.logical_or(tcore!=c, 2*c+u!=z))
        def _(): sig((tdp,2*c+u))
    one=lambda b: jnp.where(b,1,0)
    pl.semaphore_wait(bar,3+one(z>0)+one(z<nz-1)+2-one(tcore==c))
    def rc(src,dst,s,r,dev):
        return pltpu.make_async_remote_copy(src_ref=src,dst_ref=dst,send_sem=s,recv_sem=r,device_id=dev,device_id_type=MESH)
    xn=(k["xn"],z); yn=(k["yn"],z); cn=(k["core"],z)
    ns=t1[0].shape[0]; nc=cin[0].shape[0]
    def tb(i): return t1[0].at[i%ns] if chunks[i][4]==1024 else t1[1].at[0]
    def cb(i): return cin[0].at[i%nc] if chunks[i][4]==1024 else cin[1].at[0]
    def sl(i): return pl.ds(chunks[i][1],chunks[i][2]),pl.ds(chunks[i][3],chunks[i][4])
    def g(i,cc): return gs[chunks[i][0]].at[(slice(None),slice(None),slice(None),cc)+sl(i)]
    def o(i,yy,xx,half=None):
        r0,q,c0,cc=chunks[i][1:]
        if half is not None: q=q//2; r0=r0+half*q
        return outs[chunks[i][0]].at[yy,xx,c,pl.ds(r0,q),pl.ds(c0,cc)]
    def oc(i): return outs[chunks[i][0]].at[(slice(None),slice(None),c)+sl(i)]
    H=lambda i: chunks[i][2]//2
    A=lambda i: pl.ds(0,H(i))
    B=lambda i: pl.ds(H(i),H(i))
    send_c=lambda i: rc(g(i,1-c),cbig[i],cs.at[i],cr.at[i],cn)
    load_own=lambda i: pltpu.make_async_copy(g(i,c),tb(i),own.at[i])
    load_c=lambda i: pltpu.make_async_copy(cbig[i],cb(i),cld.at[i])
    send_x1=lambda i: rc(tb(i).at[:,:,1-bx,A(i)],x1[i],x1s.at[i],x1r.at[i],xn)
    send_y1=lambda i: rc(tb(i).at[:,1-by,:,B(i)],y1[i],y1s.at[i],y1r.at[i],yn)
    send_x2=lambda i: rc(tb(i).at[:,1-by,bx,A(i)],x2[i],x2s.at[i],x2r.at[i],yn)
    send_y2=lambda i: rc(tb(i).at[:,by,1-bx,B(i)],y2[i],y2s.at[i],y2r.at[i],xn)
    send_r=lambda i,t: rc(tb(i).at[t,by,bx],zb[i].at[t],zrs.at[i,t],zrr.at[i,t],(dp,z+1))
    def send_l(i,t,last): return rc(tb(i).at[t,by,bx],zb[i].at[nz if last else t],zls.at[i,t],zlr.at[i,t],(dp,z-1))
    send_ax=lambda i: rc(tb(i).at[z,by,bx],o(i,by,bx),axs.at[i],axr.at[i],xn)
    send_ay=lambda i: rc(tb(i).at[z,by,bx],o(i,by,bx),ays.at[i],ayr.at[i],yn)
    keep_a=lambda i: pltpu.make_async_copy(tb(i).at[z,by,bx],o(i,by,bx),loc.at[i])
    send_aa=lambda i: rc(o(i,by,1-bx,0),o(i,by,1-bx,0),aas.at[i],aar.at[i],yn)
    send_ab=lambda i: rc(o(i,1-by,bx,1),o(i,1-by,bx,1),abs_.at[i],abr.at[i],xn)
    send_ac=lambda i: rc(oc(i),oc(i),acs.at[i],acr.at[i],cn)
    def add(dst,src):
        dst[...]=(dst[...].astype(jnp.float32)+src[...].astype(jnp.float32)).astype(jnp.bfloat16)
    def loop(m,f):
        lax.fori_loop(0,m,lambda j,_: (f(j),0)[1],0)
    def move(u): return rc(gi.at[u],gi_o.at[z%2],fs.at[u],frv.at[z%2],(tdp,2*c+u))
    keep=pltpu.make_async_copy(gi.at[z%2],gi_o.at[z%2],keeps.at[0])
    for u in range(2):
        @pl.when(jnp.logical_or(tcore!=c,2*c+u!=z))
        def _(): move(u).start()
    @pl.when(tcore==c)
    def _(): keep.start()
    def drain(i):
        for f in (send_x1,send_y1,send_x2,send_y2,send_ax,send_ay): f(i).wait_send()
        for t in range(nz):
            @pl.when(z<t)
            def _(): send_r(i,t).wait_send()
            @pl.when(z>t)
            def _(): send_l(i,t,False).wait_send()
    def s0(i):
        if chunks[i][4]==1024 and i>=ns: drain(i-ns)
        send_c(i).start(); load_own(i).start()
    def s1a(i):
        send_c(i).wait_recv(); load_c(i).start()
    def s1(i):
        load_own(i).wait(); load_c(i).wait()
        T=tb(i); C=cb(i)
        loop(nz*4,lambda j: add(T.at[j//4,(j//2)%2,j%2],C.at[j//4,(j//2)%2,j%2]))
        send_x1(i).start(); send_y1(i).start()
    def s2(i):
        T=tb(i)
        send_x1(i).wait_recv()
        loop(nz*2,lambda j: add(T.at[j//2,j%2,bx,A(i)],x1[i].at[j//2,j%2]))
        send_x2(i).start()
        send_y1(i).wait_recv()
        loop(nz*2,lambda j: add(T.at[j//2,by,j%2,B(i)],y1[i].at[j//2,j%2]))
        send_y2(i).start()
    def s3(i):
        T=tb(i)
        send_x2(i).wait_recv()
        loop(nz,lambda j: add(T.at[j,by,bx,A(i)],x2[i].at[j]))
        send_y2(i).wait_recv()
        loop(nz,lambda j: add(T.at[j,by,bx,B(i)],y2[i].at[j]))
        for t in range(1,nz):
            @pl.when(z==0)
            def _(): send_r(i,t).start()
        for t in range(nz-1):
            @pl.when(z==nz-1)
            def _(): send_l(i,t,t==nz-2).start()
    def hop(i,h):
        T=tb(i)
        @pl.when(z==h)
        def _():
            for t in range(h+1,nz):
                send_r(i,t).wait_recv()
                add(T.at[t,by,bx],zb[i].at[t])
                send_r(i,t).start()
        @pl.when(z==nz-1-h)
        def _():
            for t in range(nz-1-h):
                send_l(i,t,False).wait_recv()
                add(T.at[t,by,bx],zb[i].at[t])
                send_l(i,t,t==nz-2-h).start()
    def s6(i):
        T=tb(i)
        @pl.when(z>0)
        def _():
            send_r(i,z).wait_recv()
            add(T.at[z,by,bx],zb[i].at[z])
        @pl.when(z<nz-1)
        def _():
            send_l(i,z,False).wait_recv()
            add(T.at[z,by,bx],zb[i].at[nz])
        send_ax(i).start(); send_ay(i).start(); keep_a(i).start()
    def s7(i):
        send_ax(i).wait_recv(); send_aa(i).start()
        send_ay(i).wait_recv(); send_ab(i).start()
    def s8(i):
        keep_a(i).wait()
        send_aa(i).wait_recv(); send_ab(i).wait_recv(); send_ac(i).start()
    stages=[(s0,0),(s1a,LAGS[0]),(s1,LAGS[1]),(s2,LAGS[2]),(s3,LAGS[3])]
    lag=LAGS[3]
    for h in range(1,nz-1):
        lag+=1; stages.append((functools.partial(lambda h,i: hop(i,h),h),lag))
    for f in (s6,s7,s8):
        lag+=1; stages.append((f,lag))
    for s in range(n+lag):
        for f,l in reversed(stages):
            if 0<=s-l<n: f(s-l)
    for i in range(n):
        if chunks[i][4]!=1024 or i+ns>=n or not any(j==i+ns and chunks[j][4]==1024 for j in range(n)): drain(i)
        send_c(i).wait_send()
        for f in (send_aa,send_ab): f(i).wait_send()
        send_ac(i).wait()
    for u in range(2):
        @pl.when(jnp.logical_or(tcore!=c,2*c+u!=z))
        def _():
            move(u).wait_send()
            rc(gi.at[u],gi_o.at[u],fs.at[u],frv.at[u],(tdp,2*c+u)).wait_recv()
    @pl.when(tcore==c)
    def _(): keep.wait()
LAGS=(2,3,4,5)
SLOTS=12

def reduce_call(grads,gi,nz,cid):
    views=[x.reshape(nz,2,2,2,x.shape[0]//(8*nz),x.shape[1]) for x in grads]
    chunks=[]
    for w,v in enumerate(views):
        r,cc=v.shape[4:]
        wide=min(cc,1024)
        for r0 in range(0,r,32):
            for c0 in range(0,cc,wide): chunks.append((w,r0,32,c0,wide))
    n=len(chunks); bf=jnp.bfloat16
    any_=pl.BlockSpec(memory_space=pl.ANY)
    outs=[jax.ShapeDtypeStruct((2,2,2)+v.shape[4:],bf) for v in views]+[jax.ShapeDtypeStruct(gi.shape,gi.dtype)]+[jax.ShapeDtypeStruct((nz,2,2,q,cc),bf) for _,_,q,_,cc in chunks]
    V=pltpu.VMEM; S=pltpu.SemaphoreType.DMA
    scratch=[V((SLOTS,nz,2,2,32,1024),bf),V((1,nz,2,2,32,128),bf),V((2,nz,2,2,32,1024),bf),V((1,nz,2,2,32,128),bf)]
    scratch+=[V((nz,2,q//2,cc),bf) for _,_,q,_,cc in chunks]*1+[V((nz,2,q//2,cc),bf) for _,_,q,_,cc in chunks]
    scratch+=[V((nz,q//2,cc),bf) for _,_,q,_,cc in chunks]+[V((nz,q//2,cc),bf) for _,_,q,_,cc in chunks]
    scratch+=[V((nz+1,q,cc),bf) for _,_,q,_,cc in chunks]
    scratch+=[S((n,))]*20+[S((n,nz))]*4+[S((n,))]*3+[S((2,)),S((2,)),S((1,))]
    ng=len(grads)
    o=pl.pallas_call(functools.partial(reduce_kernel,chunks,nz,ng),out_shape=outs,in_specs=[any_]*(ng+1),out_specs=[any_]*len(outs),
        scratch_shapes=scratch,
        compiler_params=pltpu.CompilerParams(collective_id=cid,has_side_effects=True,vmem_limit_bytes=58*2**20),
        cost_estimate=pl.CostEstimate(flops=0,bytes_accessed=3*48*2**20,transcendentals=0),
    )(*views,gi)
    return [x.reshape(-1,x.shape[-1]) for x in o[:ng]],o[ng]

def reduce_all(grads, g_small, grad_input, seq_count):
    width = D // seq_count
    small = g_small.reshape(32, seq_count, width // 128, 128).transpose(1, 2, 0, 3).reshape(seq_count, width // 4, 128)
    small = jnp.pad(small, ((0, 0), (0, 256 - width // 4), (0, 0))).reshape(seq_count * 256, 128)
    sums, grad_input = reduce_call(grads + [small], grad_input, seq_count, 1)
    count = lax.axis_size("dp")
    if count > 8:
        groups = [[i + 8 * quad for quad in range(count // 8)] for i in range(8)]
        sums = [lax.psum(x, "dp", axis_index_groups=groups) for x in sums]
    sums = [x.astype(jnp.float32) for x in sums]
    small = sums[-1][: width // 4].reshape(width // 128, 32, 128).transpose(1, 0, 2).reshape(32, width)
    pos = sums[3].reshape(D, width)
    return (*sums[:3], pos, *sums[4:-1], small), grad_input

def layer_norm(stream, gain, offset):
    average = jnp.mean(stream, axis=-1, keepdims=True)
    centred = stream - average
    spread = jnp.mean(centred * centred, axis=-1, keepdims=True)
    return centred * lax.rsqrt(spread + EPSILON) * gain + offset


def layer_norm_back(stream, gain, grad):
    average = jnp.mean(stream, axis=-1, keepdims=True)
    centred = stream - average
    spread = jnp.mean(centred * centred, axis=-1, keepdims=True)
    inverse = lax.rsqrt(spread + EPSILON)
    unit = centred * inverse
    scaled = grad * gain
    grad_stream = inverse * (
        scaled
        - jnp.mean(scaled, axis=-1, keepdims=True)
        - unit * jnp.mean(scaled * unit, axis=-1, keepdims=True)
    )
    return grad_stream, jnp.sum(grad * unit, axis=0), jnp.sum(grad, axis=0)


def swish(value):
    return value * jax.nn.sigmoid(value)


def swish_back(value, grad):
    gate = jax.nn.sigmoid(value)
    return grad * gate * (1.0 + value * (1.0 - gate))


def position_rows(first_row, rows, length, features):
    fine = 32
    column = lax.broadcasted_iota(jnp.int32, (1, features), 1)
    odd = column % 2 == 1
    frequency = jnp.exp((column // 2).astype(jnp.float32) * (-2.0 * math.log(10000.0) / features))
    coarse_at = (length - 1 - first_row - fine * jnp.arange(rows // fine, dtype=jnp.int32)).astype(jnp.float32)
    fine_at = jnp.arange(fine, dtype=jnp.int32).astype(jnp.float32)
    coarse = coarse_at[:, None] * frequency
    small = fine_at[:, None] * frequency
    coarse_sin, coarse_cos = jnp.sin(coarse), jnp.cos(coarse)
    lead = jnp.where(odd, coarse_cos, coarse_sin)[:, None, :]
    quarter = jnp.where(odd, -coarse_sin, coarse_cos)[:, None, :]
    table = lead * jnp.cos(small)[None] - quarter * jnp.sin(small)[None]
    return table.reshape(rows, features).astype(jnp.bfloat16)


def mm(left, right):
    return jnp.dot(left, right, preferred_element_type=jnp.float32)


def mm_nt(left, right):
    return lax.dot_general(left, right, NT, preferred_element_type=jnp.float32)


def mm_tn(left, right):
    return lax.dot_general(left, right, TN, preferred_element_type=jnp.float32).astype(jnp.bfloat16)


def pair_swap(value):
    count = lax.axis_size("dp")
    return lax.ppermute(value, "dp", [(i, i + 1 - 2 * (i % 2)) for i in range(count)])


def redistribute(value):
    dp_count, seq_count = lax.axis_size("dp"), lax.axis_size("seq")
    z = lax.axis_index("seq")
    routes = ([], [])
    for dp in range(dp_count):
        for zz in range(seq_count):
            a, b, c = zz // 2, zz % 2, dp % 2
            for which in range(2):
                routes[which].append(
                    (dp * seq_count + zz, (dp - c + a) * seq_count + 2 * c + (b + which) % 2)
                )
    low = z % 2 == 0
    straight = lax.ppermute(jnp.where(low, value[0], value[1]), ("dp", "seq"), routes[0])
    crossed = lax.ppermute(jnp.where(low, value[1], value[0]), ("dp", "seq"), routes[1])
    return jnp.stack([jnp.where(low, straight, crossed), jnp.where(low, crossed, straight)])


def with_halo(rows, core):
    margin = (KERNEL - 1) // 2
    got = pair_swap(jnp.where(core == 0, rows[-margin:], rows[:margin]))
    none = jnp.zeros_like(got)
    return jnp.concatenate([jnp.where(core == 1, got, none), rows, jnp.where(core == 0, got, none)], axis=0)


def shards(
    frames, cotangent, lengths, assignment, norm_gains, norm_biases, expand_one, shrink_one, qkv_weight,
    pos_weight, pos_biases, attn_out, conv_in, conv_depth, conv_out, expand_two, shrink_two,
):
    seq_count = lax.axis_size("seq")
    dp, z = lax.axis_index("dp"), lax.axis_index("seq")
    core = dp % 2
    own_length = lengths[assignment[dp - core + z // 2], z % 2]
    small = jnp.concatenate(
        [norm_gains, norm_biases, conv_depth, pos_biases, jnp.zeros((13, norm_gains.shape[1]), jnp.bfloat16)], axis=0
    )
    weights, small_all, x_in, cot = gather(
        [expand_one, shrink_one, qkv_weight, pos_weight, attn_out, conv_in, conv_out, expand_two, shrink_two],
        small, frames[0], cotangent[0], seq_count,
    )
    w1, w2, wqkv, wpos, wo, wci, wco, w3, w4 = weights
    wpos = wpos.reshape(seq_count, D, D // seq_count).transpose(1, 0, 2).reshape(D, D)
    vectors = small_all.transpose(1, 0, 2).reshape(32, D).astype(jnp.float32)
    gains, biases, depth, pos_pair = vectors[0:6], vectors[6:12], vectors[12:17], vectors[16:24]
    pos_pair = jnp.concatenate([vectors[17:19], jnp.zeros((6, D), jnp.float32)], axis=0)
    rows = 2 * frames.shape[2]
    x0 = x_in.reshape(rows, D).astype(jnp.float32)
    cot = cot.reshape(rows, D).astype(jnp.float32)
    valid = (core * rows + jnp.arange(rows, dtype=jnp.int32) < own_length).astype(jnp.float32)[:, None]

    h1 = layer_norm(x0, gains[0], biases[0]).astype(jnp.bfloat16)
    a1 = mm(h1, w1)
    s1 = swish(a1).astype(jnp.bfloat16)
    x1 = x0 + 0.5 * mm(s1, w2)
    ha = layer_norm(x1, gains[1], biases[1]).astype(jnp.bfloat16)
    qkv = mm(ha, wqkv).astype(jnp.bfloat16)
    kv_other = pair_swap(qkv[:, D:])
    sinusoid = position_rows((1 - core) * rows, 3 * rows, 2 * rows, D)
    ptab = mm(sinusoid, wpos).astype(jnp.bfloat16)
    scalars = jnp.stack([core, own_length]).astype(jnp.int32)
    attn, prob = attn_fwd(scalars, qkv, kv_other, ptab, pos_pair)
    x2 = x1 + mm(attn, wo)
    hc = layer_norm(x2, gains[2], biases[2]).astype(jnp.bfloat16)
    dbl = mm(hc, wci)
    gate = jax.nn.sigmoid(dbl[:, D:])
    m = (dbl[:, :D] * gate * valid).astype(jnp.bfloat16)
    rim = with_halo(m, core)
    cv = depth[0] * rim[0:rows]
    for tap in range(1, KERNEL):
        cv = cv + depth[tap] * rim[tap : tap + rows]
    sc = swish(layer_norm(cv, gains[3], biases[3])).astype(jnp.bfloat16)
    x3 = x2 + mm(sc, wco)
    h2 = layer_norm(x3, gains[4], biases[4]).astype(jnp.bfloat16)
    a2 = mm(h2, w3)
    s2 = swish(a2).astype(jnp.bfloat16)
    x4 = x3 + 0.5 * mm(s2, w4)
    encoded = layer_norm(x4, gains[5], biases[5]).astype(jnp.bfloat16)
    encoded = redistribute(encoded.reshape(2, rows // 2, D))

    gx4, gg5, gb5 = layer_norm_back(x4, gains[5], cot)
    go2 = (0.5 * gx4).astype(jnp.bfloat16)
    g_w4 = mm_tn(s2, go2)
    ga2 = swish_back(a2, mm_nt(go2, w4)).astype(jnp.bfloat16)
    g_w3 = mm_tn(h2, ga2)
    back, gg4, gb4 = layer_norm_back(x3, gains[4], mm_nt(ga2, w3))
    gx3 = gx4 + back
    gco = gx3.astype(jnp.bfloat16)
    g_wco = mm_tn(sc, gco)
    inner = layer_norm(cv, gains[3], biases[3])
    gcv, gg3, gb3 = layer_norm_back(cv, gains[3], swish_back(inner, mm_nt(gco, wco)))
    gcv = gcv.astype(jnp.bfloat16)
    grim = with_halo(gcv, core)
    gm = depth[0] * grim[KERNEL - 1 : KERNEL - 1 + rows]
    for tap in range(1, KERNEL):
        gm = gm + depth[tap] * grim[KERNEL - 1 - tap : KERNEL - 1 - tap + rows]
    g_depth = jnp.stack([
        jnp.sum(gcv.astype(jnp.float32) * rim[tap : tap + rows].astype(jnp.float32), axis=0) for tap in range(KERNEL)
    ])
    gm = gm * valid
    gdbl = jnp.concatenate(
        [(gm * gate).astype(jnp.bfloat16), (gm * dbl[:, :D] * gate * (1.0 - gate)).astype(jnp.bfloat16)], axis=1
    )
    g_wci = mm_tn(hc, gdbl)
    back, gg2, gb2 = layer_norm_back(x2, gains[2], mm_nt(gdbl, wci))
    gx2 = gx3 + back
    gao = gx2.astype(jnp.bfloat16)
    g_wo = mm_tn(attn, gao)
    gattn = mm_nt(gao, wo).astype(jnp.bfloat16)
    gq, gk, gv, gk_other, gv_other, gptab, g_pair = attn_bwd(scalars, qkv, kv_other, ptab, pos_pair, gattn, prob)
    got = pair_swap(jnp.concatenate([gk_other, gv_other], axis=1))
    gk = (gk + got[:, :D]).astype(jnp.bfloat16)
    gv = (gv + got[:, D:]).astype(jnp.bfloat16)
    gqkv = jnp.concatenate([gq, gk, gv], axis=1)
    g_wpos = mm_tn(sinusoid, gptab)
    g_wpos = g_wpos.reshape(D, seq_count, D // seq_count).transpose(1, 0, 2).reshape(D, D)
    g_wqkv = mm_tn(ha, gqkv)
    back, gg1, gb1 = layer_norm_back(x1, gains[1], mm_nt(gqkv, wqkv))
    gx1 = gx2 + back
    go1 = (0.5 * gx1).astype(jnp.bfloat16)
    g_w2 = mm_tn(s1, go1)
    ga1 = swish_back(a1, mm_nt(go1, w2)).astype(jnp.bfloat16)
    g_w1 = mm_tn(h1, ga1)
    back, gg0, gb0 = layer_norm_back(x0, gains[0], mm_nt(ga1, w1))
    gx0 = gx1 + back
    g_small = jnp.concatenate(
        [jnp.stack([gg0, gg1, gg2, gg3, gg4, gg5, gb0, gb1, gb2, gb3, gb4, gb5]), g_depth, g_pair[:2], jnp.zeros((13, D), jnp.float32)],
        axis=0,
    ).astype(jnp.bfloat16)
    sums, grad_input = reduce_all(
        [g_w1, g_w2, g_wqkv, g_wpos, g_wo, g_wci, g_wco, g_w3, g_w4],
        g_small, gx0.astype(jnp.bfloat16).reshape(2, rows // 2, D), seq_count,
    )
    s_w1, s_w2, s_wqkv, s_wpos, s_wo, s_wci, s_wco, s_w3, s_w4, s_small = sums
    grad_input = grad_input.astype(jnp.float32)
    return (
        encoded[None], grad_input[None], s_small[0:6], s_small[6:12], s_w1, s_w2, s_wqkv, s_wpos, s_small[17:19],
        s_wo, s_wci, s_small[12:17], s_wco, s_w3, s_w4,
    )


def solution(mesh):
    rows, columns = P("seq", None), P(None, "seq")
    act = P("dp", None, "seq", None)
    return jax.shard_map(
        shards,
        mesh=mesh,
        in_specs=(act, act, P(), P(), columns, columns, rows, rows, rows, columns, columns, rows, rows, columns, rows, rows, rows),
        out_specs=(act, act, columns, columns, rows, rows, rows, columns, columns, rows, rows, columns, rows, rows, rows),
        check_vma=False,
    )
```

```python
import functools
import math

import jax
import jax.numpy as jnp
from jax import lax
from jax.experimental import pallas as pl
from jax.experimental.pallas import tpu as pltpu
from jax.sharding import PartitionSpec as P

D = 1024
KERNEL = 5
EPSILON = 1e-05
MESH=pl.DeviceIdType.MESH

def place():
    dp=lax.axis_index("dp"); z=lax.axis_index("seq")
    c=dp%2; p=(dp//2)%4
    bx=p%2; by=p//2
    return dict(dp=dp,z=z,c=c,p=p,px=p+1-2*bx,py=p+2-4*by,
                core=dp+1-2*c, xn=dp+2-4*bx, yn=dp+4-8*by)

def rows_norm(value, gain, offset):
    centred=value-jnp.mean(value,axis=-1,keepdims=True)
    return centred*lax.rsqrt(jnp.mean(centred*centred,axis=-1,keepdims=True)+EPSILON)*gain+offset

def gather_kernel(items, order, nw, nz, *refs):
    ni=len(items)
    refs=list(refs)
    take=lambda m: [refs.pop(0) for _ in range(m)]
    ins=take(nw); vecs=take(4); fr,ct,length,lead,quarter,fine_c,fine_s=take(7)
    outs=take(nw); small_o,fr_o,ct_o,h1_o,a1_o,s1_o,x1_o,ha_o,qkv_o,kvo_o,pe_o,pt_o,p_o,at_o=take(14)
    stage=take(nw)
    x0,sv,h1,acc,ha,qkv,kvo,pe,pt,at,w1b,w2b,ab,sb,wqb,wpb,pb,x1b,small,small_f=take(20)
    (zr,xr,yr,ar,br,cr,zsr,zsl,xs,ys,as_,bs,cs,loc,lod,fs,frv,one_sem,in_sem,out_sem,kv_s,kv_r)=refs
    k=place(); dp,z,c,p=k["dp"],k["z"],k["c"],k["p"]
    here=lambda zz:(dp,zz)
    tcore=z//2; tdp=dp-c+tcore
    small_f[...]=jnp.zeros_like(small_f)
    row=0
    for part in vecs:
        small_f[row:row+part.shape[0],:]=part[...].astype(jnp.float32); row+=part.shape[0]
    small[...]=small_f[...].astype(jnp.bfloat16)
    bar=pltpu.get_barrier_semaphore()
    def sig(dev): pl.semaphore_signal(bar,inc=1,device_id=dev,device_id_type=MESH)
    for n in ("core","xn","yn"): sig((k[n],z))
    for ok,zz in ((z>0,z-1),(z<nz-1,z+1)):
        @pl.when(ok)
        def _(): sig((dp,zz))
    for u in range(2):
        @pl.when(jnp.logical_or(tcore!=c, 2*c+u!=z))
        def _(): sig((tdp,2*c+u))
    one=lambda b: jnp.where(b,1,0)
    pl.semaphore_wait(bar,3+one(z>0)+one(z<nz-1)+2-one(tcore==c))
    def rc(src,dst,s,r,dev):
        return pltpu.make_async_remote_copy(src_ref=src,dst_ref=dst,send_sem=s,recv_sem=r,device_id=dev,device_id_type=MESH)
    allin=list(ins)+[small]; allout=list(outs)+[small_o]
    def piece(i,t,pp=None,half=None):
        if i==ni: return small_o.at[t]
        w,r0,q,c0,cc=items[i]
        if half is not None: q=q//2; r0=r0+half*q
        return outs[w].at[t,p if pp is None else pp,c,pl.ds(r0,q),pl.ds(c0,cc)]
    def own(i):
        if i==ni: return small
        w,r0,q,c0,cc=items[i]
        return ins[w].at[p,c,pl.ds(r0,q),pl.ds(c0,cc)]
    def zright(w,t,src=None): return rc(piece(w,t) if src is None else src,piece(w,t),zsr.at[w,t],zr.at[w,t],(dp,z+1))
    def zleft(w,t,src=None): return rc(piece(w,t) if src is None else src,piece(w,t),zsl.at[w,t],zr.at[w,t],(dp,z-1))
    def xsend(w,t): return rc(piece(w,t),piece(w,t),xs.at[w,t],xr.at[w,t],(k["xn"],z))
    def ysend(w,t): return rc(piece(w,t),piece(w,t),ys.at[w,t],yr.at[w,t],(k["yn"],z))
    def asend(w,t): return rc(piece(w,t,k["px"],0),piece(w,t,k["px"],0),as_.at[w,t],ar.at[w,t],(k["yn"],z))
    def bsend(w,t): return rc(piece(w,t,k["py"],1),piece(w,t,k["py"],1),bs.at[w,t],br.at[w,t],(k["xn"],z))
    def csend(i,t):
        w,r0,q,c0,cc=items[i]
        four=outs[w].at[t,:,c,pl.ds(r0,q),pl.ds(c0,cc)]
        return rc(four,four,cs.at[i,t],cr.at[i,t],(k["core"],z))
    def load(w): return pltpu.make_async_copy(allin[w],stage[w],lod.at[w])
    from_vmem=lambda w: small if w==nw else stage[w]
    def local(w): return pltpu.make_async_copy(from_vmem(w),allout[w].at[z],loc.at[w])
    redo=[(fr,fr_o,0),(ct,ct_o,1)]
    def move(a,u):
        s,d,i=redo[a]
        return rc(s.at[u],d.at[z%2],fs.at[i,u],frv.at[i,z%2],(tdp,2*c+u))
    def keep(a):
        s,d,i=redo[a]
        return pltpu.make_async_copy(s.at[z%2],d.at[z%2],loc.at[nw+1+i])
    def moves(a,f_remote,f_local):
        for u in range(2):
            @pl.when(jnp.logical_or(tcore!=c,2*c+u!=z))
            def _(): f_remote(a,u)
        @pl.when(tcore==c)
        def _(): f_local(a)
    def away(f):
        for d in range(1,nz):
            @pl.when(z-d>=0)
            def _(): f(z-d,True)
            @pl.when(z+d<nz)
            def _(): f(z+d,False)
    moves(0,lambda a,u:move(a,u).start(),lambda a:keep(a).start())
    def go(w):
        @pl.when(z<nz-1)
        def _(): zright(w,z,own(w)).start()
        @pl.when(z>0)
        def _(): zleft(w,z,own(w)).start()
    def f1(w,t,fromleft):
        zright(w,t).wait_recv()
        if fromleft:
            @pl.when(z<nz-1)
            def _(): zright(w,t).start()
        else:
            @pl.when(z>0)
            def _(): zleft(w,t).start()
        if w<ni:
            xsend(w,t).start(); ysend(w,t).start()
    def f2(w,t,_):
        xsend(w,t).wait_recv(); asend(w,t).start()
        ysend(w,t).wait_recv(); bsend(w,t).start()
    def f3(w,t,_):
        asend(w,t).wait_recv(); bsend(w,t).wait_recv(); csend(w,t).start()
    def at_(f,w,d):
        @pl.when(z-d>=0)
        def _(): f(w,z-d,True)
        @pl.when(z+d<nz)
        def _(): f(w,z+d,False)
    def arrived(i):
        for d in range(1,nz): at_(lambda i,t,_: csend(i,t).wait_recv(),i,d)
    got=set(); laid=set()
    def ensure(w):
        for i in range(ni):
            if items[i][0]==w: arrived(i); got.add(i)
        local(w).wait(); laid.add(w)
    rows=x0.shape[0]; quarter_rows=rows//4
    def landed(a):
        for pos in range(2):
            @pl.when(jnp.logical_or(tcore!=c,2*c+pos!=z))
            def _():
                s,d,i=redo[a]
                rc(s.at[pos],d.at[pos],fs.at[i,pos],frv.at[i,pos],(tdp,2*c+pos)).wait_recv()
        @pl.when(tcore==c)
        def _(): keep(a).wait()
    vec=lambda r: jnp.concatenate([sv[t,r:r+1,:] for t in range(nz)],axis=1).astype(jnp.float32)
    def copy_now(src,dst,sem):
        cp=pltpu.make_async_copy(src,dst,sem); cp.start(); return cp
    pending=[]
    def store(src,dst,key):
        pending.append(copy_now(src,dst,out_sem.at[key]))
    def u_norm0():
        landed(0); local(nw).wait(); laid.add(nw)
        cps=[copy_now(fr_o.at[j],x0.at[pl.ds(j*rows//2,rows//2)],one_sem.at[j]) for j in range(2)]+[copy_now(small_o,sv,one_sem.at[2])]
        for cp in cps: cp.wait()
        gain,off=vec(0),vec(6)
        def f(j):
            at_rows=pl.ds(pl.multiple_of(j*quarter_rows,quarter_rows),quarter_rows)
            h1[at_rows,:]=rows_norm(x0[at_rows,:].astype(jnp.float32),gain,off).astype(jnp.bfloat16)
        loop(4,f)
        acc[...]=jnp.zeros_like(acc)
        store(h1,h1_o,0)
    def u_table():
        n_fine=fine_c.shape[0]
        def f(j):
            row=pl.ds(j,1)
            block=lead[row,:]*fine_c[...]-quarter[row,:]*fine_s[...]
            pe[pl.ds(pl.multiple_of(j*n_fine,n_fine),n_fine),:]=block.astype(jnp.bfloat16)
        loop(lead.shape[0],f)
        store(pe,pe_o,1)
    def u_ptab(t):
        if t==0: ensure(3)
        copy_now(outs[3].at[t],wpb,one_sem.at[0]).wait()
        width=wpb.shape[3]
        pt[:,width*t:width*t+width]=mmv(pe[...],wpb[...].reshape(-1,width)).astype(jnp.bfloat16)
        if t==nz-1: store(pt,pt_o,2)
    mmv=lambda l,r: jnp.dot(l,r,preferred_element_type=jnp.float32)
    fcols=w1b.shape[-1]; nf=outs[0].shape[-1]//fcols
    per_z=outs[1].shape[3]*8; zb_rows=per_z//fcols
    lows=4//zb_rows
    a_load=lambda j: copy_now(outs[0].at[:,:,:,:,pl.ds(j*fcols,fcols)],w1b.at[j%2],in_sem.at[0,j%2])
    b_load=lambda j: copy_now(outs[1].at[j//zb_rows,pl.ds(j%zb_rows*lows,lows)],w2b.at[j%2],in_sem.at[1,j%2])
    flight={}
    def u_expand(j):
        if j==0:
            ensure(0); flight["a",0]=a_load(0)
        if j+1<nf: flight["a",j+1]=a_load(j+1)
        flight.pop(("a",j)).wait()
        if j>=2: flight.pop(("o",j-2)).wait()
        hidden=mmv(h1[...],w1b[j%2].reshape(-1,fcols))
        ab[j%2]=hidden
        cols=pl.ds(j*fcols,fcols)
        sb[:,cols]=(hidden*jax.nn.sigmoid(hidden)).astype(jnp.bfloat16)
        flight["o",j]=copy_now(ab.at[j%2],a1_o.at[:,cols],out_sem.at[3+j%2])
        if j==nf-1:
            pending.extend((flight.pop(("o",j-1)),flight.pop(("o",j))))
            store(sb,s1_o,5)
    def u_shrink(j):
        if j==0:
            ensure(1); flight["b",0]=b_load(0)
        if j+1<nf: flight["b",j+1]=b_load(j+1)
        flight.pop(("b",j)).wait()
        acc[...]+=mmv(sb[:,j*fcols:j*fcols+fcols],w2b[j%2].reshape(fcols,-1))
    def u_norm1():
        gain,off=vec(1),vec(7)
        def f(j):
            at_rows=pl.ds(pl.multiple_of(j*quarter_rows,quarter_rows),quarter_rows)
            mid=x0[at_rows,:].astype(jnp.float32)+0.5*acc[at_rows,:]
            acc[at_rows,:]=mid
            ha[at_rows,:]=rows_norm(mid,gain,off).astype(jnp.bfloat16)
        loop(4,f)
        store(acc,x1_o,7); store(ha,ha_o,8)
    qcols=wqb.shape[-1]; nq=outs[2].shape[-1]//qcols
    q_load=lambda j: copy_now(outs[2].at[:,:,:,:,pl.ds(j*qcols,qcols)],wqb.at[j%2],in_sem.at[2,j%2])
    def u_qkv(j):
        if j==0:
            ensure(2); flight["q",0]=q_load(0)
        if j+1<nq: flight["q",j+1]=q_load(j+1)
        flight.pop(("q",j)).wait()
        qkv[:,j*qcols:j*qcols+qcols]=mmv(ha[...],wqb[j%2].reshape(-1,qcols)).astype(jnp.bfloat16)
        if j==nq-1:
            store(qkv,qkv_o,9)
            swap_kv().start()
    dim=x0.shape[1]
    swap_kv=lambda: rc(qkv.at[:,pl.ds(dim,2*dim)],kvo,kv_s.at[0],kv_r.at[0],(k["core"],z))
    def u_head(h):
        if h==0:
            swap_kv().wait()
            store(kvo,kvo_o,10)
        if h>=2: flight.pop(("p",h-2)).wait()
        col=lambda off: pl.ds(off+h*HD,HD)
        attn_head(c==0,length[0],qkv[:,col(0)],qkv[:,col(dim)],qkv[:,col(2*dim)],kvo[:,col(0)],kvo[:,col(dim)],
            pt.at[:,col(0)],pairv[0:2,col(0)],at.at[:,col(0)],pb.at[h%2])
        flight["p",h]=copy_now(pb.at[h%2],p_o.at[h],out_sem.at[11+h%2])
        if h==heads-1:
            store(at,at_o,13)
            pending.extend((flight.pop(("p",h-1)),flight.pop(("p",h))))
    pairv=x1b
    def u_pair():
        pairv[0:1,:]=vec(17); pairv[1:2,:]=vec(18)
    def loop(m,f):
        lax.fori_loop(0,m,lambda j,_: (f(j),0)[1],0)
    last_item=lambda w: max(i for i in range(ni) if items[i][0]==w)
    heads=at.shape[1]//HD
    ready=lambda w: last_item(w)+nz+SLACK
    units=[(nz-1,2,u_norm0),(0,0,u_pair),(0,4,u_table)]
    units+=[(ready(3),1.5,functools.partial(u_ptab,t)) for t in range(nz)]
    units+=[(ready(0),1,functools.partial(u_expand,j)) for j in range(nf)]
    units+=[(ready(1),1,functools.partial(u_shrink,j)) for j in range(nf)]+[(0,2,u_norm1)]
    units+=[(ready(2),1,functools.partial(u_qkv,j)) for j in range(nq)]
    units+=[(ready(2)+2,2.5,functools.partial(u_head,h)) for h in range(heads)]
    def run(s,budget):
        while budget>0 and units and units[0][0]<=s:
            _,cost,unit=units.pop(0)
            unit(); budget-=cost
    go(ni)
    for w in range(AHEAD): go(w)
    for w in order: load(w).start()
    local(nw).start()
    for s in range(ni+nz):
        if s<nw:
            load(order[s]).wait(); local(order[s]).start()
        if s+AHEAD<ni: go(s+AHEAD)
        if s<nz-1: at_(f1,ni,s+1)
        if s==ni//2: moves(1,lambda a,u:move(a,u).start(),lambda a:keep(a).start())
        for f,late in ((f3,1),(f2,0),(f1,-1)):
            for d in range(1,nz):
                if 0<=s-d-late<ni: at_(f,s-d-late,d)
            run(s,BUDGET)
    run(10**6,10**6)
    for cp in pending: cp.wait()
    def away(f):
        for d in range(1,nz):
            @pl.when(z-d>=0)
            def _(): f(z-d,True)
            @pl.when(z+d<nz)
            def _(): f(z+d,False)
    for w in range(nw+1):
        if w not in laid: local(w).wait()
    for w in range(ni+1):
        @pl.when(z<nz-1)
        def _(): zright(w,z,own(w)).wait_send()
        @pl.when(z>0)
        def _(): zleft(w,z,own(w)).wait_send()
        def f(t,fromleft):
            if fromleft:
                @pl.when(z<nz-1)
                def _(): zright(w,t).wait_send()
            else:
                @pl.when(z>0)
                def _(): zleft(w,t).wait_send()
            if w<ni:
                for g in (xsend,ysend,asend,bsend,csend): g(w,t).wait_send()
                if w not in got: csend(w,t).wait_recv()
        away(f)
    for a in range(2):
        moves(a,lambda a,u:move(a,u).wait_send(),lambda a:None)
    landed(1)

ITEM=2**21
BUDGET=2.0
SLACK=1
AHEAD=1
def gather(ws,vecs,fr,ct,length,tables,nz,cid=0):
    nw=len(ws); bf=jnp.bfloat16; f32=jnp.float32
    small=jax.ShapeDtypeStruct((32,vecs[0].shape[1]),bf)
    ins=[w.reshape(4,2,w.shape[0]//8,w.shape[1]) for w in ws]
    order=[3,0,1,2]+list(range(4,nw))
    items=[]
    for w in order:
        q,cc=ins[w].shape[2:]
        parts=max(1,nz*8*q*cc//ITEM)
        for j in range(parts): items.append((w,0,q,j*cc//parts,cc//parts) if q<64 else (w,j*q//parts,q//parts,0,cc))
    ni=len(items)
    rows=2*fr.shape[1]; dim=fr.shape[2]; ff=ws[0].shape[1]; heads=dim//HD; wide=ws[3].shape[1]
    any_=pl.BlockSpec(memory_space=pl.ANY); vm=pl.BlockSpec(memory_space=pltpu.VMEM); sm=pl.BlockSpec(memory_space=pltpu.SMEM)
    sd=jax.ShapeDtypeStruct; V=pltpu.VMEM
    shp=[sd((nz,)+w.shape,w.dtype) for w in ins]+[sd((nz,)+small.shape,small.dtype),sd(fr.shape,fr.dtype),sd(ct.shape,ct.dtype)]
    shp+=[sd((rows,dim),bf),sd((rows,ff),f32),sd((rows,ff),bf),sd((rows,dim),f32),sd((rows,dim),bf),sd((rows,3*dim),bf),sd((rows,2*dim),bf),
        sd((3*rows,dim),bf),sd((3*rows,dim),bf),sd((heads,rows,2*rows),bf),sd((rows,dim),bf)]
    S=pltpu.SemaphoreType.DMA
    cut=512
    q0=ins[0].shape[2]; q2=ins[1].shape[2]
    scratch=[V(w.shape,w.dtype) for w in ins]
    scratch+=[V((rows,dim),bf),V((nz,)+small.shape,bf),V((rows,dim),bf),V((rows,dim),f32),V((rows,dim),bf),V((rows,3*dim),bf),V((rows,2*dim),bf),
        V((3*rows,dim),bf),V((3*rows,dim),bf),V((rows,dim),bf),
        V((2,nz,4,2,q0,cut),bf),V((2,cut//(2*q2),2,q2,dim),bf),V((2,rows,cut),f32),V((rows,ff),bf),V((2,nz,4,2,q0,cut),bf),V((4,2,ins[3].shape[2],wide),bf),
        V((2,rows,2*rows),bf),V((8,dim),f32),V(small.shape,bf),V(small.shape,f32)]
    scratch+=[S((ni+1,nz))]+[S((ni,nz))]*5+[S((ni+1,nz))]*2+[S((ni,nz))]*5+[S((nw+3,)),S((nw,)),S((2,2)),S((2,2)),S((3,)),S((3,2)),S((14,)),S((1,)),S((1,))]
    o=pl.pallas_call(functools.partial(gather_kernel,items,order,nw,nz),out_shape=shp,
        in_specs=[any_]*nw+[vm]*4+[any_]*2+[sm]+[vm]*4,out_specs=[any_]*len(shp),
        scratch_shapes=scratch,
        compiler_params=pltpu.CompilerParams(collective_id=cid,has_side_effects=True,vmem_limit_bytes=60*2**20),
        cost_estimate=pl.CostEstimate(flops=25*10**9,bytes_accessed=2*48*2**20,transcendentals=0),
    )(*ins,*vecs,fr,ct,length,*tables)
    full=[x.reshape(nz*w.shape[0],w.shape[1]) for x,w in zip(o[:nw],ws)]
    return full,o[nw],o[nw+1],o[nw+2],o[nw+3:]

HD=128; SCALE=1.0/math.sqrt(128)
BLK=256
NT=(((1,),(1,)),((),()))
TN=(((0,),(0,)),((),()))
def dot(a,b,dims=(((1,),(0,)),((),()))):
    return lax.dot_general(a,b,dims,preferred_element_type=jnp.float32)

def order(first, own, oth):
    return jnp.concatenate([jnp.where(first, own, oth), jnp.where(first, oth, own)], axis=0)

def attn_head(first,length,q,k,v,ko,vo,pt_ref,pb,o_ref,p_ref):
    T=q.shape[0]; L2=2*T
    q=q.astype(jnp.float32)
    qu=(q+pb[0:1]).astype(jnp.bfloat16); qv=(q+pb[1:2]).astype(jnp.bfloat16)
    k=order(first,k,ko); v=order(first,v,vo)
    W=BLK+L2
    keep=lax.broadcasted_iota(jnp.int32,(BLK,L2),1)<length
    for b in range(T//BLK):
        i0=b*BLK; w0=T-i0-BLK
        s=dot(qu[i0:i0+BLK],k,NT)
        placed=dot(qv[i0:i0+BLK],pt_ref[w0:w0+W,:],NT)
        s=s+pltpu.roll(placed,W-(BLK-1),1,stride=1,stride_axis=0)[:,:L2]
        s=jnp.where(keep,s*SCALE,-1e9)
        m=jnp.max(s,axis=-1,keepdims=True)
        e=jnp.exp(s-m)
        p=(e*(1.0/jnp.sum(e,axis=-1,keepdims=True))).astype(jnp.bfloat16)
        p_ref[i0:i0+BLK,:]=p
        o_ref[i0:i0+BLK,:]=dot(p,v).astype(jnp.bfloat16)

def attn_bwd_kernel(sc_ref, q_ref, k_ref, v_ref, ko_ref, vo_ref, pt_ref, pb_ref, g_ref, at_ref, p_ref,
                    gq_ref, gk_ref, gv_ref, gko_ref, gvo_ref, gpt_ref, gb_ref, gpt_acc):
    T=q_ref.shape[0]; L2=2*T
    first=sc_ref[0]==0
    q=q_ref[...].astype(jnp.float32)
    pb=pb_ref[...].astype(jnp.float32)
    qu=(q+pb[0:1]).astype(jnp.bfloat16); qv=(q+pb[1:2]).astype(jnp.bfloat16)
    k=order(first,k_ref[...],ko_ref[...]); v=order(first,v_ref[...],vo_ref[...])
    W=BLK+L2
    flip=(lax.broadcasted_iota(jnp.int32,(BLK,BLK),0)+lax.broadcasted_iota(jnp.int32,(BLK,BLK),1)==BLK-1).astype(jnp.float32).astype(jnp.bfloat16)
    gpt_acc[...]=jnp.zeros_like(gpt_acc)
    gk=gv=None; su=sv=None
    low=lambda v: v.astype(jnp.bfloat16)
    for b in range(T//BLK):
        i0=b*BLK; w0=T-i0-BLK
        g0=g_ref[i0:i0+BLK,:]
        rows=jnp.concatenate([g0,qu[i0:i0+BLK],qv[i0:i0+BLK],p_ref[0,i0:i0+BLK,:]],axis=1)
        back=dot(flip,rows)
        g=low(back[:,:HD]); qur=low(back[:,HD:2*HD]); qvr=low(back[:,2*HD:3*HD]); p=back[:,3*HD:]
        pbf=low(p)
        delta=jnp.sum(g0.astype(jnp.float32)*at_ref[i0:i0+BLK,:].astype(jnp.float32),axis=-1,keepdims=True)
        delta=lax.dot_general(flip.astype(jnp.float32),jnp.broadcast_to(delta,(BLK,HD)),(((1,),(0,)),((),())),precision=lax.Precision.HIGHEST,preferred_element_type=jnp.float32)[:,:1]
        gr=p*((dot(g,v,NT)-delta)*SCALE)
        grb=low(gr)
        gvb=dot(pbf,g,TN); gkb=dot(grb,qur,TN)
        gv=gvb if gv is None else gv+gvb
        gk=gkb if gk is None else gk+gkb
        gqu=dot(grb,k)
        pad=jnp.concatenate([gr,jnp.zeros((BLK,BLK),jnp.float32)],axis=1)
        gp=low(pltpu.roll(pad,0,1,stride=1,stride_axis=0))
        gpt_acc[w0:w0+W,:]+=dot(gp,qvr,TN)
        gqv=dot(gp,pt_ref[w0:w0+W,:])
        gq_ref[i0:i0+BLK,:]=low(dot(flip,low(gqu+gqv)))
        a=jnp.sum(gqu,axis=0,keepdims=True); c=jnp.sum(gqv,axis=0,keepdims=True)
        su=a if su is None else su+a; sv=c if sv is None else sv+c
    gpt_ref[...]=gpt_acc[...].astype(jnp.bfloat16)
    gk_ref[...]=jnp.where(first,gk[:T],gk[T:]); gv_ref[...]=jnp.where(first,gv[:T],gv[T:])
    gko_ref[...]=jnp.where(first,gk[T:],gk[:T]).astype(jnp.bfloat16); gvo_ref[...]=jnp.where(first,gv[T:],gv[:T]).astype(jnp.bfloat16)
    gb_ref[...]=jnp.concatenate([su,sv,jnp.zeros((6,su.shape[1]),jnp.float32)],axis=0)

def col(rows,off=0): return pl.BlockSpec((rows,HD),lambda h,off=off:(0,h+off))
def attn_bwd(sc,qkv,kvo,pt,pb,g,at,p):
    T=qkv.shape[0]; D=qkv.shape[1]//3; H=D//HD
    f32=jnp.float32; bf=jnp.bfloat16
    return pl.pallas_call(attn_bwd_kernel,grid=(H,),
        in_specs=[pl.BlockSpec(memory_space=pltpu.SMEM),col(T),col(T,H),col(T,2*H),col(T),col(T,H),col(3*T),col(pb.shape[0]),col(T),col(T),pl.BlockSpec((1,T,2*T),lambda h:(h,0,0))],
        out_specs=[col(T)]*5+[col(3*T),col(8)],
        out_shape=[jax.ShapeDtypeStruct((T,D),bf),jax.ShapeDtypeStruct((T,D),f32),jax.ShapeDtypeStruct((T,D),f32),jax.ShapeDtypeStruct((T,D),bf),jax.ShapeDtypeStruct((T,D),bf),jax.ShapeDtypeStruct((3*T,D),bf),jax.ShapeDtypeStruct((8,D),f32)],
        scratch_shapes=[pltpu.VMEM((3*T,HD),f32)],
        compiler_params=pltpu.CompilerParams(vmem_limit_bytes=48*2**20),
        cost_estimate=pl.CostEstimate(flops=H*T*2*T*HD*2*6,bytes_accessed=30*2**20,transcendentals=0),
    )(sc,qkv,qkv,qkv,kvo,kvo,pt,pb,g,at,p)

def reduce_kernel(plan, zfirst, nz, nops, *refs):
    n=len(plan)
    refs=list(refs)
    take=lambda m: [refs.pop(0) for _ in range(m)]
    ops=take(nops); ready,small,gi=take(3)
    out,out_s,gi_o,far,far_s=take(5)
    tw,tsm,sw,ssm,cw,csm,ab,bb=take(8)
    x1=take(n); y1=take(n); x2=take(n); y2=take(n); zb=take(n)
    (cs,cr,x1s,x1r,y1s,y1r,x2s,x2r,y2s,y2r,axs,axr,ays,ayr,aas,aar,abs_,abr,acs,acr,zrs,zrr,zls,zlr,own,cld,loc,opsem,fs,frv,keeps)=refs
    k=place(); dp,z,c=k["dp"],k["z"],k["c"]
    bx=k["p"]%2; by=k["p"]//2
    tcore=z//2; tdp=dp-c+tcore
    bar=pltpu.get_barrier_semaphore()
    def sig(dev): pl.semaphore_signal(bar,inc=1,device_id=dev,device_id_type=MESH)
    for a in ("core","xn","yn"): sig((k[a],z))
    for ok,zz in ((z>0,z-1),(z<nz-1,z+1)):
        @pl.when(ok)
        def _(): sig((dp,zz))
    for u in range(2):
        @pl.when(jnp.logical_or(tcore!=c, 2*c+u!=z))
        def _(): sig((tdp,2*c+u))
    one=lambda b: jnp.where(b,1,0)
    pl.semaphore_wait(bar,3+one(z>0)+one(z<nz-1)+2-one(tcore==c))
    def rc(src,dst,s,r,dev):
        return pltpu.make_async_remote_copy(src_ref=src,dst_ref=dst,send_sem=s,recv_sem=r,device_id=dev,device_id_type=MESH)
    xn=(k["xn"],z); yn=(k["yn"],z); cn=(k["core"],z)
    nt=tw.shape[0]; nsnd=sw.shape[0]; nc=cw.shape[0]
    big=lambda i: len(plan[i])>0
    tb=lambda i: tw.at[i%nt] if big(i) else tsm
    sb=lambda i: sw.at[i%nsnd] if big(i) else ssm
    cb=lambda i: cw.at[i%nc] if big(i) else csm
    fb=lambda i: far.at[i] if big(i) else far_s
    ob=lambda i: out.at[i] if big(i) else out_s
    half=lambda i: 128 if big(i) else 16
    A=lambda i: pl.ds(0,half(i))
    B=lambda i: pl.ds(half(i),half(i))
    send_c=lambda i: rc(sb(i),fb(i),cs.at[i],cr.at[i],cn)
    load_c=lambda i: pltpu.make_async_copy(fb(i),cb(i),cld.at[i])
    zf=lambda i: i in zfirst
    def shard(i,r,*rest):
        return r.at[(z,)+rest] if zf(i) else r.at[(slice(None),)+rest]
    send_x1=lambda i: rc(shard(i,tb(i),slice(None),1-bx,A(i)),x1[i],x1s.at[i],x1r.at[i],xn)
    send_y1=lambda i: rc(shard(i,tb(i),1-by,slice(None),B(i)),y1[i],y1s.at[i],y1r.at[i],yn)
    send_x2=lambda i: rc(shard(i,tb(i),1-by,bx,A(i)),x2[i],x2s.at[i],x2r.at[i],yn)
    send_y2=lambda i: rc(shard(i,tb(i),by,1-bx,B(i)),y2[i],y2s.at[i],y2r.at[i],xn)
    line=lambda i,t: tb(i).at[t] if zf(i) else tb(i).at[t,by,bx]
    send_r=lambda i,t: rc(line(i,t),zb[i].at[t],zrs.at[i,t],zrr.at[i,t],(dp,z+1))
    send_l=lambda i,t,last: rc(line(i,t),zb[i].at[nz if last else t],zls.at[i,t],zlr.at[i,t],(dp,z-1))
    mine=lambda i: tb(i).at[z,by,bx]
    send_ax=lambda i: rc(mine(i),ob(i).at[by,bx,c],axs.at[i],axr.at[i],xn)
    send_ay=lambda i: rc(mine(i),ob(i).at[by,bx,c],ays.at[i],ayr.at[i],yn)
    keep_a=lambda i: pltpu.make_async_copy(mine(i),ob(i).at[by,bx,c],loc.at[i])
    send_aa=lambda i: rc(ob(i).at[by,1-bx,c,A(i)],ob(i).at[by,1-bx,c,A(i)],aas.at[i],aar.at[i],yn)
    send_ab=lambda i: rc(ob(i).at[1-by,bx,c,B(i)],ob(i).at[1-by,bx,c,B(i)],abs_.at[i],abr.at[i],xn)
    send_ac=lambda i: rc(ob(i).at[:,:,c],ob(i).at[:,:,c],acs.at[i],acr.at[i],cn)
    def add(dst,src):
        dst[...]=(dst[...].astype(jnp.float32)+src[...].astype(jnp.float32)).astype(jnp.bfloat16)
    def loop(m,f):
        lax.fori_loop(0,m,lambda j,_: (f(j),0)[1],0)
    def move(u): return rc(gi.at[u],gi_o.at[z%2],fs.at[u],frv.at[z%2],(tdp,2*c+u))
    keep=pltpu.make_async_copy(gi.at[z%2],gi_o.at[z%2],keeps.at[0])
    def operand(i):
        if len(plan[i])==5:
            l,r,zs,lo,ro=plan[i]; s=i%2
            cps=[pltpu.make_async_copy(ops[l].at[:,pl.ds(t*zs+lo,256)],ab.at[s,t],opsem.at[s,t]) for t in range(nz)]
            return cps+[pltpu.make_async_copy(ops[r].at[:,pl.ds(ro,1024)],bb.at[s],opsem.at[s,nz])]
        if big(i):
            q=[(yy,xx) for yy in range(2) for xx in range(2)]
            cols=lambda yy,xx,cc: pl.ds(pl.multiple_of((yy*4+xx*2+cc)*128,128),128)
            return ([pltpu.make_async_copy(ready.at[:,:,cols(yy,xx,c)],tb(i).at[:,yy,xx],opsem.at[i%2,yy*2+xx]) for yy,xx in q]
                +[pltpu.make_async_copy(ready.at[:,:,cols(yy,xx,1-c)],sb(i).at[:,yy,xx],opsem.at[i%2,4+yy*2+xx]) for yy,xx in q])
        return [pltpu.make_async_copy(small.at[:,:,:,c],tb(i),opsem.at[i%2,0]),pltpu.make_async_copy(small.at[:,:,:,1-c],sb(i),opsem.at[i%2,1])]
    def drain(i):
        for f in (send_x1,send_y1,send_x2,send_y2,send_ax,send_ay): f(i).wait_send()
        for t in range(nz):
            @pl.when(z<t)
            def _(): send_r(i,t).wait_send()
            @pl.when(z>t)
            def _(): send_l(i,t,False).wait_send()
    bigs=[i for i in range(n) if big(i)]
    def sl(i):
        if big(i) and i-nt in bigs: drain(i-nt)
        if big(i) and i-nsnd in bigs: send_c(i-nsnd).wait_send()
        for cp in operand(i): cp.start()
    def s0(i):
        for cp in operand(i): cp.wait()
        if len(plan[i])==5:
            s=i%2; T=tb(i); Sb=sb(i)
            cut=lambda cc: jnp.concatenate([bb[s,:,pl.ds(pl.multiple_of((2*q+cc)*128,128),128)] for q in range(4)],axis=1)
            def make(cc,dst):
                right=cut(cc)
                def f(t):
                    tile=lax.dot_general(ab[s,t],right,TN,preferred_element_type=jnp.float32).astype(jnp.bfloat16)
                    for q in range(4): dst[t,q//2,q%2]=tile[:,128*q:128*q+128]
                loop(nz,f)
            make(1-c,Sb)
            send_c(i).start()
            make(c,T)
        else:
            send_c(i).start()
    def s1a(i):
        send_c(i).wait_recv(); load_c(i).start()
    def s1(i):
        load_c(i).wait()
        T=tb(i); C=cb(i)
        loop(nz*4,lambda j: add(T.at[j//4,(j//2)%2,j%2],C.at[j//4,(j//2)%2,j%2]))
        if zf(i): line_start(i)
        else: xy_start(i)
    def xy_start(i):
        send_x1(i).start(); send_y1(i).start()
    def line_start(i):
        @pl.when(z==0)
        def _():
            for t in reversed(range(1,nz)): send_r(i,t).start()
        @pl.when(z==nz-1)
        def _():
            for t in range(nz-1): send_l(i,t,t==nz-2).start()
    def s2(i):
        T=tb(i)
        send_x1(i).wait_recv()
        if zf(i): loop(2,lambda j: add(T.at[z,j,bx,A(i)],x1[i].at[j]))
        else: loop(nz*2,lambda j: add(T.at[j//2,j%2,bx,A(i)],x1[i].at[j//2,j%2]))
        send_x2(i).start()
        send_y1(i).wait_recv()
        if zf(i): loop(2,lambda j: add(T.at[z,by,j,B(i)],y1[i].at[j]))
        else: loop(nz*2,lambda j: add(T.at[j//2,by,j%2,B(i)],y1[i].at[j//2,j%2]))
        send_y2(i).start()
    def s3(i):
        T=tb(i)
        send_x2(i).wait_recv()
        if zf(i): add(T.at[z,by,bx,A(i)],x2[i])
        else: loop(nz,lambda j: add(T.at[j,by,bx,A(i)],x2[i].at[j]))
        send_y2(i).wait_recv()
        if zf(i): add(T.at[z,by,bx,B(i)],y2[i])
        else: loop(nz,lambda j: add(T.at[j,by,bx,B(i)],y2[i].at[j]))
        if zf(i): spread_start(i)
        else: line_start(i)
    def add_line(i,t,slot):
        if zf(i): loop(4,lambda j: add(tb(i).at[t,j//2,j%2],zb[i].at[slot,j//2,j%2]))
        else: add(line(i,t),zb[i].at[slot])
    def hop(h,i):
        @pl.when(z==h)
        def _():
            for t in reversed(range(h+1,nz)):
                send_r(i,t).wait_recv()
                add_line(i,t,t)
                send_r(i,t).start()
        @pl.when(z==nz-1-h)
        def _():
            for t in range(nz-1-h):
                send_l(i,t,False).wait_recv()
                add_line(i,t,t)
                send_l(i,t,t==nz-2-h).start()
    def s6(i):
        @pl.when(z>0)
        def _():
            send_r(i,z).wait_recv()
            add_line(i,z,z)
        @pl.when(z<nz-1)
        def _():
            send_l(i,z,False).wait_recv()
            add_line(i,z,nz)
        if zf(i): xy_start(i)
        else: spread_start(i)
    def spread_start(i):
        send_ax(i).start(); send_ay(i).start(); keep_a(i).start()
    def s7(i):
        send_ax(i).wait_recv(); send_aa(i).start()
        send_ay(i).wait_recv(); send_ab(i).start()
    def s8(i):
        keep_a(i).wait()
        send_aa(i).wait_recv(); send_ab(i).wait_recv(); send_ac(i).start()
    def start_moves():
        for u in range(2):
            @pl.when(jnp.logical_or(tcore!=c,2*c+u!=z))
            def _(): move(u).start()
        @pl.when(tcore==c)
        def _(): keep.start()
    hops=[functools.partial(hop,h) for h in range(1,nz-1)]
    xy_stages=list(zip([sl,s0,s1a,s1,s2,s3]+hops+[s6,s7,s8],XY_LAGS))
    z_stages=list(zip([sl,s0,s1a,s1]+hops+[s6,s2,s3,s7,s8],Z_LAGS))
    for s in range(n+max(XY_LAGS+Z_LAGS)):
        if s==MOVE_AT: start_moves()
        todo=[(d,f,i) for i in range(n) for f,d in (z_stages if zf(i) else xy_stages) if i+d==s]
        for d,f,i in sorted(todo,key=lambda x:-x[0]): f(i)
    for i in range(n):
        if not (big(i) and i+nt in bigs): drain(i)
        if not (big(i) and i+nsnd in bigs): send_c(i).wait_send()
        send_aa(i).wait_send(); send_ab(i).wait_send()
        send_ac(i).wait()
    for u in range(2):
        @pl.when(jnp.logical_or(tcore!=c,2*c+u!=z))
        def _():
            move(u).wait_send()
            rc(gi.at[u],gi_o.at[u],fs.at[u],frv.at[u],(tdp,2*c+u)).wait_recv()
    @pl.when(tcore==c)
    def _(): keep.wait()

XY_LAGS=(0,1,2,3,5,6,7,8,9,10,11)
Z_LAGS=(0,1,2,3,5,6,8,9,10,11,12)
SLOTS=14
MOVE_AT=0
def reduce_call(ops,ready,small,gi,plan,zfirst,nz,cid):
    n=len(plan); nb=sum(len(x)>0 for x in plan); bf=jnp.bfloat16
    rows=ops[0].shape[0]
    any_=pl.BlockSpec(memory_space=pl.ANY)
    sd=jax.ShapeDtypeStruct
    outs=[sd((nb,2,2,2,256,128),bf),sd((2,2,2,32,128),bf),sd(gi.shape,gi.dtype),sd((nb,nz,2,2,256,128),bf),sd((nz,2,2,32,128),bf)]
    V=pltpu.VMEM; S=pltpu.SemaphoreType.DMA
    h=[128 if len(x) else 16 for x in plan]
    lead=lambda i: () if i in zfirst else (nz,)
    scratch=[V((SLOTS,nz,2,2,256,128),bf),V((nz,2,2,32,128),bf),V((2,nz,2,2,256,128),bf),V((nz,2,2,32,128),bf),V((2,nz,2,2,256,128),bf),V((nz,2,2,32,128),bf),
        V((2,nz,rows,256),bf),V((2,rows,1024),bf)]
    scratch+=[V(lead(i)+(2,h[i],128),bf) for i in range(n)]*2+[V(lead(i)+(h[i],128),bf) for i in range(n)]*2
    scratch+=[V((nz+1,)+((2,2) if i in zfirst else ())+(2*h[i],128),bf) for i in range(n)]
    scratch+=[S((n,))]*20+[S((n,nz))]*4+[S((1,)),S((n,)),S((n,)),S((2,8)),S((2,)),S((2,)),S((1,))]
    return pl.pallas_call(functools.partial(reduce_kernel,plan,zfirst,nz,len(ops)),out_shape=outs,in_specs=[any_]*(len(ops)+3),out_specs=[any_]*len(outs),
        scratch_shapes=scratch,
        compiler_params=pltpu.CompilerParams(collective_id=cid,has_side_effects=True,vmem_limit_bytes=58*2**20),
        cost_estimate=pl.CostEstimate(flops=2*n*rows*2**20,bytes_accessed=100*2**20,transcendentals=0),
    )(*ops,ready,small,gi)[:3]

def grad_plan(seq_count):
    plan, names = [], {}
    def weight(name, left, right, blocks, shrink):
        names[name] = len(plan), blocks
        for j in range(blocks):
            plan.append((left, right, 256 * blocks, 256 * j, 0) if shrink else (left, right, 256, 0, 1024 * j))
    weight("w4", 0, 1, 4, True)
    weight("w3", 2, 3, 4, False)
    weight("wco", 4, 5, 1, False)
    weight("wci", 6, 7, 2, False)
    weight("wo", 8, 9, 1, False)
    weight("wqkv", 10, 11, 3, False)
    names["wpos"] = len(plan), 1
    plan.append((0,))
    weight("w2", 12, 13, 4, True)
    weight("w1", 14, 15, 4, False)
    plan.append(())
    return plan, names

WIDEN_SLOTS = 4


def widen_kernel(spots, blocks_ref, *refs):
    outs, (narrow, wide, in_sem, out_sem) = refs[:-4], refs[-4:]
    count = len(spots)

    def fetch(i):
        return pltpu.make_async_copy(blocks_ref.at[i], narrow.at[i % WIDEN_SLOTS], in_sem.at[i % WIDEN_SLOTS])

    def put(i):
        which, row, column = spots[i]
        target = outs[which].at[pl.ds(row, 256), pl.ds(column, 1024)]
        return pltpu.make_async_copy(wide.at[i % WIDEN_SLOTS], target, out_sem.at[i % WIDEN_SLOTS])

    for i in range(WIDEN_SLOTS - 1):
        fetch(i).start()
    for i in range(count):
        if i + WIDEN_SLOTS - 1 < count:
            fetch(i + WIDEN_SLOTS - 1).start()
        fetch(i).wait()
        if i >= WIDEN_SLOTS:
            put(i - WIDEN_SLOTS).wait()
        slot = i % WIDEN_SLOTS

        def cast(piece, _):
            wide[slot, :, pl.ds(pl.multiple_of(128 * piece, 128), 128)] = narrow[slot, piece].astype(jnp.float32)
            return 0

        lax.fori_loop(0, 8, cast, 0, unroll=True)
        put(i).start()
    for i in range(count - WIDEN_SLOTS, count):
        put(i).wait()


def widen(blocks, names):
    spots, shapes = [], []
    for which, (name, (first, length)) in enumerate(names.items()):
        tall = name in ("w2", "w4")
        spots += [(which, 256 * j if tall else 0, 0 if tall else 1024 * j) for j in range(length)]
        shapes.append(jax.ShapeDtypeStruct((256 * length, 1024) if tall else (256, 1024 * length), jnp.float32))
    anywhere = pl.BlockSpec(memory_space=pl.ANY)
    wide = pl.pallas_call(
        functools.partial(widen_kernel, spots),
        in_specs=[anywhere],
        out_specs=[anywhere] * len(shapes),
        out_shape=shapes,
        scratch_shapes=[
            pltpu.VMEM((WIDEN_SLOTS, 8, 256, 128), jnp.bfloat16),
            pltpu.VMEM((WIDEN_SLOTS, 256, 1024), jnp.float32),
            pltpu.SemaphoreType.DMA((WIDEN_SLOTS,)),
            pltpu.SemaphoreType.DMA((WIDEN_SLOTS,)),
        ],
        compiler_params=pltpu.CompilerParams(vmem_limit_bytes=56 * 2**20),
        cost_estimate=pl.CostEstimate(flops=0, bytes_accessed=36 * 2**20, transcendentals=0),
    )(blocks)
    return dict(zip(names, wide))


def reduce_all(ops, ready, g_small, grad_input, seq_count):
    width = D // seq_count
    pieces = width // 128
    small = g_small.reshape(32, seq_count, pieces, 128).transpose(1, 2, 0, 3)
    small = jnp.pad(small, ((0, 0), (0, 8 - pieces), (0, 0), (0, 0))).reshape(seq_count, 2, 2, 2, 32, 128)
    plan, names = grad_plan(seq_count)
    by_line = {i for i in range(2, len(plan) - 1, 3)}
    blocks, small, grad_input = reduce_call(ops, ready, small, grad_input, plan, by_line, seq_count, 1)
    count = lax.axis_size("dp")
    if count > 8:
        groups = [[i + 8 * quad for quad in range(count // 8)] for i in range(8)]
        blocks, small = (lax.psum(x, "dp", axis_index_groups=groups) for x in (blocks, small))
    sums = widen(blocks.reshape(-1, 8, 256, 128), names)
    sums["wpos"] = sums["wpos"].T
    small = small.reshape(8, 32, 128)[:pieces].transpose(1, 0, 2).reshape(32, width).astype(jnp.float32)
    return sums, small, grad_input


def layer_norm(stream, gain, offset):
    average = jnp.mean(stream, axis=-1, keepdims=True)
    centred = stream - average
    spread = jnp.mean(centred * centred, axis=-1, keepdims=True)
    return centred * lax.rsqrt(spread + EPSILON) * gain + offset


def layer_norm_back(stream, gain, grad):
    average = jnp.mean(stream, axis=-1, keepdims=True)
    centred = stream - average
    spread = jnp.mean(centred * centred, axis=-1, keepdims=True)
    inverse = lax.rsqrt(spread + EPSILON)
    unit = centred * inverse
    scaled = grad * gain
    grad_stream = inverse * (
        scaled
        - jnp.mean(scaled, axis=-1, keepdims=True)
        - unit * jnp.mean(scaled * unit, axis=-1, keepdims=True)
    )
    return grad_stream, jnp.sum(grad * unit, axis=0), jnp.sum(grad, axis=0)


def swish(value):
    return value * jax.nn.sigmoid(value)


def swish_back(value, grad):
    gate = jax.nn.sigmoid(value)
    return grad * gate * (1.0 + value * (1.0 - gate))


def position_tables(first_row, rows, length, features):
    fine = 32
    column = lax.broadcasted_iota(jnp.int32, (1, features), 1)
    odd = column % 2 == 1
    frequency = jnp.exp((column // 2).astype(jnp.float32) * (-2.0 * math.log(10000.0) / features))
    coarse_at = (length - 1 - first_row - fine * jnp.arange(rows // fine, dtype=jnp.int32)).astype(jnp.float32)
    fine_at = jnp.arange(fine, dtype=jnp.int32).astype(jnp.float32)
    coarse = coarse_at[:, None] * frequency
    small = fine_at[:, None] * frequency
    coarse_sin, coarse_cos = jnp.sin(coarse), jnp.cos(coarse)
    return jnp.where(odd, coarse_cos, coarse_sin), jnp.where(odd, -coarse_sin, coarse_cos), jnp.cos(small), jnp.sin(small)


def mm(left, right):
    return jnp.dot(left, right, preferred_element_type=jnp.float32)


def mm_nt(left, right):
    return lax.dot_general(left, right, NT, preferred_element_type=jnp.float32)


def mm_tn(left, right):
    return lax.dot_general(left, right, TN, preferred_element_type=jnp.float32).astype(jnp.bfloat16)


def pair_swap(value):
    count = lax.axis_size("dp")
    return lax.ppermute(value, "dp", [(i, i + 1 - 2 * (i % 2)) for i in range(count)])


def redistribute(value):
    dp_count, seq_count = lax.axis_size("dp"), lax.axis_size("seq")
    z = lax.axis_index("seq")
    routes = ([], [])
    for dp in range(dp_count):
        for zz in range(seq_count):
            a, b, c = zz // 2, zz % 2, dp % 2
            for which in range(2):
                routes[which].append(
                    (dp * seq_count + zz, (dp - c + a) * seq_count + 2 * c + (b + which) % 2)
                )
    low = z % 2 == 0
    straight = lax.ppermute(jnp.where(low, value[0], value[1]), ("dp", "seq"), routes[0])
    crossed = lax.ppermute(jnp.where(low, value[1], value[0]), ("dp", "seq"), routes[1])
    return jnp.stack([jnp.where(low, straight, crossed), jnp.where(low, crossed, straight)])


def with_halo(rows, core):
    margin = (KERNEL - 1) // 2
    got = pair_swap(jnp.where(core == 0, rows[-margin:], rows[:margin]))
    none = jnp.zeros_like(got)
    return jnp.concatenate([jnp.where(core == 1, got, none), rows, jnp.where(core == 0, got, none)], axis=0)


def shards(
    frames, cotangent, lengths, assignment, norm_gains, norm_biases, expand_one, shrink_one, qkv_weight,
    pos_weight, pos_biases, attn_out, conv_in, conv_depth, conv_out, expand_two, shrink_two,
):
    seq_count = lax.axis_size("seq")
    dp, z = lax.axis_index("dp"), lax.axis_index("seq")
    core = dp % 2
    own_length = lengths[assignment[dp - core + z // 2], z % 2]
    rows = 2 * frames.shape[2]
    tables = position_tables((1 - core) * rows, 3 * rows, 2 * rows, D)
    weights, small_all, x_in, cot, first_part = gather(
        [expand_one, shrink_one, qkv_weight, pos_weight, attn_out, conv_in, conv_out, expand_two, shrink_two],
        [norm_gains, norm_biases, conv_depth, pos_biases], frames[0], cotangent[0], own_length.reshape(1), tables, seq_count,
    )
    w1, w2, wqkv, _, wo, wci, wco, w3, w4 = weights
    h1, a1, s1, x1, ha, qkv, kv_other, sinusoid, ptab, prob, attn = first_part
    vectors = small_all.transpose(1, 0, 2).reshape(32, D).astype(jnp.float32)
    gains, biases, depth, pos_pair = vectors[0:6], vectors[6:12], vectors[12:17], vectors[16:24]
    pos_pair = jnp.concatenate([vectors[17:19], jnp.zeros((6, D), jnp.float32)], axis=0)
    x0 = x_in.reshape(rows, D).astype(jnp.float32)
    cot = cot.reshape(rows, D).astype(jnp.float32)
    valid = (core * rows + jnp.arange(rows, dtype=jnp.int32) < own_length).astype(jnp.float32)[:, None]

    scalars = jnp.stack([core, own_length]).astype(jnp.int32)
    x2 = x1 + mm(attn, wo)
    hc = layer_norm(x2, gains[2], biases[2]).astype(jnp.bfloat16)
    dbl = mm(hc, wci)
    gate = jax.nn.sigmoid(dbl[:, D:])
    m = (dbl[:, :D] * gate * valid).astype(jnp.bfloat16)
    rim = with_halo(m, core)
    cv = depth[0] * rim[0:rows]
    for tap in range(1, KERNEL):
        cv = cv + depth[tap] * rim[tap : tap + rows]
    sc = swish(layer_norm(cv, gains[3], biases[3])).astype(jnp.bfloat16)
    x3 = x2 + mm(sc, wco)
    h2 = layer_norm(x3, gains[4], biases[4]).astype(jnp.bfloat16)
    a2 = mm(h2, w3)
    s2 = swish(a2).astype(jnp.bfloat16)
    x4 = x3 + 0.5 * mm(s2, w4)
    encoded = layer_norm(x4, gains[5], biases[5]).astype(jnp.bfloat16)
    encoded = redistribute(encoded.reshape(2, rows // 2, D))

    gx4, gg5, gb5 = layer_norm_back(x4, gains[5], cot)
    go2 = (0.5 * gx4).astype(jnp.bfloat16)
    ga2 = swish_back(a2, mm_nt(go2, w4)).astype(jnp.bfloat16)
    back, gg4, gb4 = layer_norm_back(x3, gains[4], mm_nt(ga2, w3))
    gx3 = gx4 + back
    gco = gx3.astype(jnp.bfloat16)
    inner = layer_norm(cv, gains[3], biases[3])
    gcv, gg3, gb3 = layer_norm_back(cv, gains[3], swish_back(inner, mm_nt(gco, wco)))
    gcv = gcv.astype(jnp.bfloat16)
    grim = with_halo(gcv, core)
    gm = depth[0] * grim[KERNEL - 1 : KERNEL - 1 + rows]
    for tap in range(1, KERNEL):
        gm = gm + depth[tap] * grim[KERNEL - 1 - tap : KERNEL - 1 - tap + rows]
    g_depth = jnp.stack([
        jnp.sum(gcv.astype(jnp.float32) * rim[tap : tap + rows].astype(jnp.float32), axis=0) for tap in range(KERNEL)
    ])
    gm = gm * valid
    gdbl = jnp.concatenate(
        [(gm * gate).astype(jnp.bfloat16), (gm * dbl[:, :D] * gate * (1.0 - gate)).astype(jnp.bfloat16)], axis=1
    )
    back, gg2, gb2 = layer_norm_back(x2, gains[2], mm_nt(gdbl, wci))
    gx2 = gx3 + back
    gao = gx2.astype(jnp.bfloat16)
    gattn = mm_nt(gao, wo).astype(jnp.bfloat16)
    gq, gk, gv, gk_other, gv_other, gptab, g_pair = attn_bwd(scalars, qkv, kv_other, ptab, pos_pair, gattn, attn, prob)
    got = pair_swap(jnp.concatenate([gk_other, gv_other], axis=1))
    gk = (gk + got[:, :D]).astype(jnp.bfloat16)
    gv = (gv + got[:, D:]).astype(jnp.bfloat16)
    gqkv = jnp.concatenate([gq, gk, gv], axis=1)
    g_wpos = mm_tn(gptab, sinusoid).reshape(seq_count, D // seq_count, D)
    back, gg1, gb1 = layer_norm_back(x1, gains[1], mm_nt(gqkv, wqkv))
    gx1 = gx2 + back
    go1 = (0.5 * gx1).astype(jnp.bfloat16)
    ga1 = swish_back(a1, mm_nt(go1, w2)).astype(jnp.bfloat16)
    back, gg0, gb0 = layer_norm_back(x0, gains[0], mm_nt(ga1, w1))
    gx0 = gx1 + back
    g_small = jnp.concatenate(
        [jnp.stack([gg0, gg1, gg2, gg3, gg4, gg5, gb0, gb1, gb2, gb3, gb4, gb5]), g_depth, g_pair[:2], jnp.zeros((13, D), jnp.float32)],
        axis=0,
    ).astype(jnp.bfloat16)
    sums, s_small, grad_input = reduce_all(
        [s2, go2, h2, ga2, sc, gco, hc, gdbl, attn, gao, ha, gqkv, s1, go1, h1, ga1],
        g_wpos, g_small, gx0.astype(jnp.bfloat16).reshape(2, rows // 2, D), seq_count,
    )
    grad_input = grad_input.astype(jnp.float32)
    return (
        encoded[None], grad_input[None], s_small[0:6], s_small[6:12], sums["w1"], sums["w2"], sums["wqkv"],
        sums["wpos"], s_small[17:19], sums["wo"], sums["wci"], s_small[12:17], sums["wco"], sums["w3"], sums["w4"],
    )


def solution(mesh):
    rows, columns = P("seq", None), P(None, "seq")
    act = P("dp", None, "seq", None)
    return jax.shard_map(
        shards,
        mesh=mesh,
        in_specs=(act, act, P(), P(), columns, columns, rows, rows, rows, columns, columns, rows, rows, columns, rows, rows, rows),
        out_specs=(act, act, columns, columns, rows, rows, rows, columns, columns, rows, rows, columns, rows, rows, rows),
        check_vma=False,
    )
```

```python
import functools
import math

import jax
import jax.numpy as jnp
from jax import lax
from jax.experimental import pallas as pl
from jax.experimental.pallas import tpu as pltpu
from jax.sharding import PartitionSpec as P

D = 1024
KERNEL = 5
EPSILON = 1e-05
MESH=pl.DeviceIdType.MESH

def place():
    dp=lax.axis_index("dp"); z=lax.axis_index("seq")
    c=dp%2; p=(dp//2)%4
    bx=p%2; by=p//2
    return dict(dp=dp,z=z,c=c,p=p,px=p+1-2*bx,py=p+2-4*by,
                core=dp+1-2*c, xn=dp+2-4*bx, yn=dp+4-8*by)

def rows_norm(value, gain, offset):
    centred=value-jnp.mean(value,axis=-1,keepdims=True)
    return centred*lax.rsqrt(jnp.mean(centred*centred,axis=-1,keepdims=True)+EPSILON)*gain+offset

def gather_kernel(items, order, nw, nz, *refs):
    ni=len(items)
    refs=list(refs)
    take=lambda m: [refs.pop(0) for _ in range(m)]
    ins=take(nw); vecs=take(4); fr,ct,length,lead,quarter,fine_c,fine_s=take(7)
    outs=take(nw); small_o,fr_o,ct_o,h1_o,a1_o,s1_o,x1_o,ha_o,qkv_o,kvo_o,pe_o,pt_o,p_o,at_o=take(14)
    stage=take(nw)
    x0,sv,h1,acc,ha,qkv,kvo,pe,pt,at,w1b,w2b,ab,sb,wqb,wpb,pb,x1b,small,small_f=take(20)
    (zr,xr,yr,ar,br,cr,zsr,zsl,xs,ys,as_,bs,cs,loc,lod,fs,frv,one_sem,in_sem,out_sem,kv_s,kv_r)=refs
    k=place(); dp,z,c,p=k["dp"],k["z"],k["c"],k["p"]
    here=lambda zz:(dp,zz)
    tcore=z//2; tdp=dp-c+tcore
    small_f[...]=jnp.zeros_like(small_f)
    row=0
    for part in vecs:
        small_f[row:row+part.shape[0],:]=part[...].astype(jnp.float32); row+=part.shape[0]
    small[...]=small_f[...].astype(jnp.bfloat16)
    bar=pltpu.get_barrier_semaphore()
    def sig(dev): pl.semaphore_signal(bar,inc=1,device_id=dev,device_id_type=MESH)
    for n in ("core","xn","yn"): sig((k[n],z))
    for ok,zz in ((z>0,z-1),(z<nz-1,z+1)):
        @pl.when(ok)
        def _(): sig((dp,zz))
    for u in range(2):
        @pl.when(jnp.logical_or(tcore!=c, 2*c+u!=z))
        def _(): sig((tdp,2*c+u))
    one=lambda b: jnp.where(b,1,0)
    pl.semaphore_wait(bar,3+one(z>0)+one(z<nz-1)+2-one(tcore==c))
    def rc(src,dst,s,r,dev):
        return pltpu.make_async_remote_copy(src_ref=src,dst_ref=dst,send_sem=s,recv_sem=r,device_id=dev,device_id_type=MESH)
    allin=list(ins)+[small]; allout=list(outs)+[small_o]
    def piece(i,t,pp=None,half=None):
        if i==ni: return small_o.at[t]
        w,r0,q,c0,cc=items[i]
        if half is not None: q=q//2; r0=r0+half*q
        return outs[w].at[t,p if pp is None else pp,c,pl.ds(r0,q),pl.ds(c0,cc)]
    def own(i):
        if i==ni: return small
        w,r0,q,c0,cc=items[i]
        return ins[w].at[p,c,pl.ds(r0,q),pl.ds(c0,cc)]
    def zright(w,t,src=None): return rc(piece(w,t) if src is None else src,piece(w,t),zsr.at[w,t],zr.at[w,t],(dp,z+1))
    def zleft(w,t,src=None): return rc(piece(w,t) if src is None else src,piece(w,t),zsl.at[w,t],zr.at[w,t],(dp,z-1))
    def xsend(w,t): return rc(piece(w,t),piece(w,t),xs.at[w,t],xr.at[w,t],(k["xn"],z))
    def ysend(w,t): return rc(piece(w,t),piece(w,t),ys.at[w,t],yr.at[w,t],(k["yn"],z))
    def asend(w,t): return rc(piece(w,t,k["px"],0),piece(w,t,k["px"],0),as_.at[w,t],ar.at[w,t],(k["yn"],z))
    def bsend(w,t): return rc(piece(w,t,k["py"],1),piece(w,t,k["py"],1),bs.at[w,t],br.at[w,t],(k["xn"],z))
    def csend(i,t):
        w,r0,q,c0,cc=items[i]
        four=outs[w].at[t,:,c,pl.ds(r0,q),pl.ds(c0,cc)]
        return rc(four,four,cs.at[i,t],cr.at[i,t],(k["core"],z))
    def load(w): return pltpu.make_async_copy(allin[w],stage[w],lod.at[w])
    from_vmem=lambda w: small if w==nw else stage[w]
    def local(w): return pltpu.make_async_copy(from_vmem(w),allout[w].at[z],loc.at[w])
    redo=[(fr,fr_o,0),(ct,ct_o,1)]
    def move(a,u):
        s,d,i=redo[a]
        return rc(s.at[u],d.at[z%2],fs.at[i,u],frv.at[i,z%2],(tdp,2*c+u))
    def keep(a):
        s,d,i=redo[a]
        return pltpu.make_async_copy(s.at[z%2],d.at[z%2],loc.at[nw+1+i])
    def moves(a,f_remote,f_local):
        for u in range(2):
            @pl.when(jnp.logical_or(tcore!=c,2*c+u!=z))
            def _(): f_remote(a,u)
        @pl.when(tcore==c)
        def _(): f_local(a)
    def away(f):
        for d in range(1,nz):
            @pl.when(z-d>=0)
            def _(): f(z-d,True)
            @pl.when(z+d<nz)
            def _(): f(z+d,False)
    moves(0,lambda a,u:move(a,u).start(),lambda a:keep(a).start())
    def go(w):
        @pl.when(z<nz-1)
        def _(): zright(w,z,own(w)).start()
        @pl.when(z>0)
        def _(): zleft(w,z,own(w)).start()
    def f1(w,t,fromleft):
        zright(w,t).wait_recv()
        if fromleft:
            @pl.when(z<nz-1)
            def _(): zright(w,t).start()
        else:
            @pl.when(z>0)
            def _(): zleft(w,t).start()
        if w<ni:
            xsend(w,t).start(); ysend(w,t).start()
    def f2(w,t,_):
        xsend(w,t).wait_recv(); asend(w,t).start()
        ysend(w,t).wait_recv(); bsend(w,t).start()
    def f3(w,t,_):
        asend(w,t).wait_recv(); bsend(w,t).wait_recv(); csend(w,t).start()
    def at_(f,w,d):
        @pl.when(z-d>=0)
        def _(): f(w,z-d,True)
        @pl.when(z+d<nz)
        def _(): f(w,z+d,False)
    def arrived(i):
        for d in range(1,nz): at_(lambda i,t,_: csend(i,t).wait_recv(),i,d)
    got=set(); laid=set()
    def ensure(w):
        for i in range(ni):
            if items[i][0]==w: arrived(i); got.add(i)
        local(w).wait(); laid.add(w)
    rows=x0.shape[0]; quarter_rows=rows//4
    def landed(a):
        for pos in range(2):
            @pl.when(jnp.logical_or(tcore!=c,2*c+pos!=z))
            def _():
                s,d,i=redo[a]
                rc(s.at[pos],d.at[pos],fs.at[i,pos],frv.at[i,pos],(tdp,2*c+pos)).wait_recv()
        @pl.when(tcore==c)
        def _(): keep(a).wait()
    vec=lambda r: jnp.concatenate([sv[t,r:r+1,:] for t in range(nz)],axis=1).astype(jnp.float32)
    def copy_now(src,dst,sem):
        cp=pltpu.make_async_copy(src,dst,sem); cp.start(); return cp
    pending=[]
    def store(src,dst,key):
        pending.append(copy_now(src,dst,out_sem.at[key]))
    def u_norm0():
        landed(0); local(nw).wait(); laid.add(nw)
        cps=[copy_now(fr_o.at[j],x0.at[pl.ds(j*rows//2,rows//2)],one_sem.at[j]) for j in range(2)]+[copy_now(small_o,sv,one_sem.at[2])]
        for cp in cps: cp.wait()
        gain,off=vec(0),vec(6)
        def f(j):
            at_rows=pl.ds(pl.multiple_of(j*quarter_rows,quarter_rows),quarter_rows)
            h1[at_rows,:]=rows_norm(x0[at_rows,:].astype(jnp.float32),gain,off).astype(jnp.bfloat16)
        loop(4,f)
        acc[...]=jnp.zeros_like(acc)
        store(h1,h1_o,0)
    def u_table():
        n_fine=fine_c.shape[0]
        def f(j):
            row=pl.ds(j,1)
            block=lead[row,:]*fine_c[...]-quarter[row,:]*fine_s[...]
            pe[pl.ds(pl.multiple_of(j*n_fine,n_fine),n_fine),:]=block.astype(jnp.bfloat16)
        loop(lead.shape[0],f)
        store(pe,pe_o,1)
    def u_ptab(t):
        if t==0: ensure(3)
        copy_now(outs[3].at[t],wpb,one_sem.at[0]).wait()
        width=wpb.shape[3]
        pt[:,width*t:width*t+width]=mmv(pe[...],wpb[...].reshape(-1,width)).astype(jnp.bfloat16)
        if t==nz-1: store(pt,pt_o,2)
    mmv=lambda l,r: jnp.dot(l,r,preferred_element_type=jnp.float32)
    fcols=w1b.shape[-1]; nf=outs[0].shape[-1]//fcols
    per_z=outs[1].shape[3]*8; zb_rows=per_z//fcols
    lows=4//zb_rows
    a_load=lambda j: copy_now(outs[0].at[:,:,:,:,pl.ds(j*fcols,fcols)],w1b.at[j%2],in_sem.at[0,j%2])
    b_load=lambda j: copy_now(outs[1].at[j//zb_rows,pl.ds(j%zb_rows*lows,lows)],w2b.at[j%2],in_sem.at[1,j%2])
    flight={}
    def u_expand(j):
        if j==0:
            ensure(0); flight["a",0]=a_load(0)
        if j+1<nf: flight["a",j+1]=a_load(j+1)
        flight.pop(("a",j)).wait()
        if j>=2: flight.pop(("o",j-2)).wait()
        hidden=mmv(h1[...],w1b[j%2].reshape(-1,fcols))
        ab[j%2]=hidden
        cols=pl.ds(j*fcols,fcols)
        sb[:,cols]=(hidden*jax.nn.sigmoid(hidden)).astype(jnp.bfloat16)
        flight["o",j]=copy_now(ab.at[j%2],a1_o.at[:,cols],out_sem.at[3+j%2])
        if j==nf-1:
            pending.extend((flight.pop(("o",j-1)),flight.pop(("o",j))))
            store(sb,s1_o,5)
    def u_shrink(j):
        if j==0:
            ensure(1); flight["b",0]=b_load(0)
        if j+1<nf: flight["b",j+1]=b_load(j+1)
        flight.pop(("b",j)).wait()
        acc[...]+=mmv(sb[:,j*fcols:j*fcols+fcols],w2b[j%2].reshape(fcols,-1))
    def u_norm1():
        gain,off=vec(1),vec(7)
        def f(j):
            at_rows=pl.ds(pl.multiple_of(j*quarter_rows,quarter_rows),quarter_rows)
            mid=x0[at_rows,:].astype(jnp.float32)+0.5*acc[at_rows,:]
            acc[at_rows,:]=mid
            ha[at_rows,:]=rows_norm(mid,gain,off).astype(jnp.bfloat16)
        loop(4,f)
        store(acc,x1_o,7); store(ha,ha_o,8)
    qcols=wqb.shape[-1]; nq=outs[2].shape[-1]//qcols
    q_load=lambda j: copy_now(outs[2].at[:,:,:,:,pl.ds(j*qcols,qcols)],wqb.at[j%2],in_sem.at[2,j%2])
    def u_qkv(j):
        if j==0:
            ensure(2); flight["q",0]=q_load(0)
        if j+1<nq: flight["q",j+1]=q_load(j+1)
        flight.pop(("q",j)).wait()
        qkv[:,j*qcols:j*qcols+qcols]=mmv(ha[...],wqb[j%2].reshape(-1,qcols)).astype(jnp.bfloat16)
        if j==nq-1:
            store(qkv,qkv_o,9)
            swap_kv().start()
    dim=x0.shape[1]
    swap_kv=lambda: rc(qkv.at[:,pl.ds(dim,2*dim)],kvo,kv_s.at[0],kv_r.at[0],(k["core"],z))
    def u_head(h):
        if h==0:
            swap_kv().wait()
            store(kvo,kvo_o,10)
        if h>=2: flight.pop(("p",h-2)).wait()
        col=lambda off: pl.ds(off+h*HD,HD)
        attn_head(c==0,length[0],qkv[:,col(0)],qkv[:,col(dim)],qkv[:,col(2*dim)],kvo[:,col(0)],kvo[:,col(dim)],
            pt.at[:,col(0)],pairv[0:2,col(0)],at.at[:,col(0)],pb.at[h%2])
        flight["p",h]=copy_now(pb.at[h%2],p_o.at[h],out_sem.at[11+h%2])
        if h==heads-1:
            store(at,at_o,13)
            pending.extend((flight.pop(("p",h-1)),flight.pop(("p",h))))
    pairv=x1b
    def u_pair():
        pairv[0:1,:]=vec(17); pairv[1:2,:]=vec(18)
    def loop(m,f):
        lax.fori_loop(0,m,lambda j,_: (f(j),0)[1],0)
    last_item=lambda w: max(i for i in range(ni) if items[i][0]==w)
    heads=at.shape[1]//HD
    ready=lambda w: last_item(w)+nz+SLACK
    units=[(nz-1,2,u_norm0),(0,0,u_pair),(0,4,u_table)]
    units+=[(ready(3),1.5,functools.partial(u_ptab,t)) for t in range(nz)]
    units+=[(ready(0),1,functools.partial(u_expand,j)) for j in range(nf)]
    units+=[(ready(1),1,functools.partial(u_shrink,j)) for j in range(nf)]+[(0,2,u_norm1)]
    units+=[(ready(2),1,functools.partial(u_qkv,j)) for j in range(nq)]
    units+=[(ready(2)+2,2.5,functools.partial(u_head,h)) for h in range(heads)]
    def run(s,budget):
        while budget>0 and units and units[0][0]<=s:
            _,cost,unit=units.pop(0)
            unit(); budget-=cost
    go(ni)
    for w in range(AHEAD): go(w)
    for w in order: load(w).start()
    local(nw).start()
    for s in range(ni+nz):
        if s<nw:
            load(order[s]).wait(); local(order[s]).start()
        if s+AHEAD<ni: go(s+AHEAD)
        if s<nz-1: at_(f1,ni,s+1)
        if s==ni-1: moves(1,lambda a,u:move(a,u).start(),lambda a:keep(a).start())
        for f,late in ((f3,1),(f2,0),(f1,-1)):
            for d in range(1,nz):
                if 0<=s-d-late<ni: at_(f,s-d-late,d)
            run(s,BUDGET)
    run(10**6,10**6)
    for cp in pending: cp.wait()
    def away(f):
        for d in range(1,nz):
            @pl.when(z-d>=0)
            def _(): f(z-d,True)
            @pl.when(z+d<nz)
            def _(): f(z+d,False)
    for w in range(nw+1):
        if w not in laid: local(w).wait()
    for w in range(ni+1):
        @pl.when(z<nz-1)
        def _(): zright(w,z,own(w)).wait_send()
        @pl.when(z>0)
        def _(): zleft(w,z,own(w)).wait_send()
        def f(t,fromleft):
            if fromleft:
                @pl.when(z<nz-1)
                def _(): zright(w,t).wait_send()
            else:
                @pl.when(z>0)
                def _(): zleft(w,t).wait_send()
            if w<ni:
                for g in (xsend,ysend,asend,bsend,csend): g(w,t).wait_send()
                if w not in got: csend(w,t).wait_recv()
        away(f)
    for a in range(2):
        moves(a,lambda a,u:move(a,u).wait_send(),lambda a:None)
    landed(1)

ITEM=2**21
BUDGET=1.5
SLACK=1
AHEAD=2
def gather(ws,vecs,fr,ct,length,tables,nz,cid=0):
    nw=len(ws); bf=jnp.bfloat16; f32=jnp.float32
    small=jax.ShapeDtypeStruct((32,vecs[0].shape[1]),bf)
    ins=[w.reshape(4,2,w.shape[0]//8,w.shape[1]) for w in ws]
    order=[3,0,1,2]+list(range(4,nw))
    items=[]
    for w in order:
        q,cc=ins[w].shape[2:]
        parts=max(1,nz*8*q*cc//ITEM)
        for j in range(parts): items.append((w,0,q,j*cc//parts,cc//parts) if q<64 else (w,j*q//parts,q//parts,0,cc))
    ni=len(items)
    rows=2*fr.shape[1]; dim=fr.shape[2]; ff=ws[0].shape[1]; heads=dim//HD; wide=ws[3].shape[1]
    any_=pl.BlockSpec(memory_space=pl.ANY); vm=pl.BlockSpec(memory_space=pltpu.VMEM); sm=pl.BlockSpec(memory_space=pltpu.SMEM)
    sd=jax.ShapeDtypeStruct; V=pltpu.VMEM
    shp=[sd((nz,)+w.shape,w.dtype) for w in ins]+[sd((nz,)+small.shape,small.dtype),sd(fr.shape,fr.dtype),sd(ct.shape,ct.dtype)]
    shp+=[sd((rows,dim),bf),sd((rows,ff),f32),sd((rows,ff),bf),sd((rows,dim),f32),sd((rows,dim),bf),sd((rows,3*dim),bf),sd((rows,2*dim),bf),
        sd((3*rows,dim),bf),sd((3*rows,dim),bf),sd((heads,rows,2*rows),bf),sd((rows,dim),bf)]
    S=pltpu.SemaphoreType.DMA
    cut=512
    q0=ins[0].shape[2]; q2=ins[1].shape[2]
    scratch=[V(w.shape,w.dtype) for w in ins]
    scratch+=[V((rows,dim),bf),V((nz,)+small.shape,bf),V((rows,dim),bf),V((rows,dim),f32),V((rows,dim),bf),V((rows,3*dim),bf),V((rows,2*dim),bf),
        V((3*rows,dim),bf),V((3*rows,dim),bf),V((rows,dim),bf),
        V((2,nz,4,2,q0,cut),bf),V((2,cut//(2*q2),2,q2,dim),bf),V((2,rows,cut),f32),V((rows,ff),bf),V((2,nz,4,2,q0,cut),bf),V((4,2,ins[3].shape[2],wide),bf),
        V((2,rows,2*rows),bf),V((8,dim),f32),V(small.shape,bf),V(small.shape,f32)]
    scratch+=[S((ni+1,nz))]+[S((ni,nz))]*5+[S((ni+1,nz))]*2+[S((ni,nz))]*5+[S((nw+3,)),S((nw,)),S((2,2)),S((2,2)),S((3,)),S((3,2)),S((14,)),S((1,)),S((1,))]
    o=pl.pallas_call(functools.partial(gather_kernel,items,order,nw,nz),out_shape=shp,
        in_specs=[any_]*nw+[vm]*4+[any_]*2+[sm]+[vm]*4,out_specs=[any_]*len(shp),
        scratch_shapes=scratch,
        compiler_params=pltpu.CompilerParams(collective_id=cid,has_side_effects=True,vmem_limit_bytes=60*2**20),
        cost_estimate=pl.CostEstimate(flops=25*10**9,bytes_accessed=2*48*2**20,transcendentals=0),
    )(*ins,*vecs,fr,ct,length,*tables)
    full=[x.reshape(nz*w.shape[0],w.shape[1]) for x,w in zip(o[:nw],ws)]
    return full,o[nw],o[nw+1],o[nw+2],o[nw+3:]

HD=128; SCALE=1.0/math.sqrt(128)
BLK=256
NT=(((1,),(1,)),((),()))
TN=(((0,),(0,)),((),()))
def dot(a,b,dims=(((1,),(0,)),((),()))):
    return lax.dot_general(a,b,dims,preferred_element_type=jnp.float32)

def order(first, own, oth):
    return jnp.concatenate([jnp.where(first, own, oth), jnp.where(first, oth, own)], axis=0)

def attn_head(first,length,q,k,v,ko,vo,pt_ref,pb,o_ref,p_ref):
    T=q.shape[0]; L2=2*T
    q=q.astype(jnp.float32)
    qu=(q+pb[0:1]).astype(jnp.bfloat16); qv=(q+pb[1:2]).astype(jnp.bfloat16)
    k=order(first,k,ko); v=order(first,v,vo)
    W=BLK+L2
    keep=lax.broadcasted_iota(jnp.int32,(BLK,L2),1)<length
    for b in range(T//BLK):
        i0=b*BLK; w0=T-i0-BLK
        s=dot(qu[i0:i0+BLK],k,NT)
        placed=dot(qv[i0:i0+BLK],pt_ref[w0:w0+W,:],NT)
        s=s+pltpu.roll(placed,W-(BLK-1),1,stride=1,stride_axis=0)[:,:L2]
        s=jnp.where(keep,s*SCALE,-1e9)
        m=jnp.max(s,axis=-1,keepdims=True)
        e=jnp.exp(s-m)
        p=(e*(1.0/jnp.sum(e,axis=-1,keepdims=True))).astype(jnp.bfloat16)
        p_ref[i0:i0+BLK,:]=p
        o_ref[i0:i0+BLK,:]=dot(p,v).astype(jnp.bfloat16)

def attn_bwd_kernel(sc_ref, q_ref, k_ref, v_ref, ko_ref, vo_ref, pt_ref, pb_ref, g_ref, at_ref, p_ref,
                    gq_ref, gk_ref, gv_ref, gko_ref, gvo_ref, gpt_ref, gb_ref, gpt_acc):
    T=q_ref.shape[0]; L2=2*T
    first=sc_ref[0]==0
    q=q_ref[...].astype(jnp.float32)
    pb=pb_ref[...].astype(jnp.float32)
    qu=(q+pb[0:1]).astype(jnp.bfloat16); qv=(q+pb[1:2]).astype(jnp.bfloat16)
    k=order(first,k_ref[...],ko_ref[...]); v=order(first,v_ref[...],vo_ref[...])
    W=BLK+L2
    flip=(lax.broadcasted_iota(jnp.int32,(BLK,BLK),0)+lax.broadcasted_iota(jnp.int32,(BLK,BLK),1)==BLK-1).astype(jnp.float32).astype(jnp.bfloat16)
    gpt_acc[...]=jnp.zeros_like(gpt_acc)
    gk=gv=None; su=sv=None
    low=lambda v: v.astype(jnp.bfloat16)
    for b in range(T//BLK):
        i0=b*BLK; w0=T-i0-BLK
        g0=g_ref[i0:i0+BLK,:]
        rows=jnp.concatenate([g0,qu[i0:i0+BLK],qv[i0:i0+BLK],p_ref[0,i0:i0+BLK,:]],axis=1)
        back=dot(flip,rows)
        g=low(back[:,:HD]); qur=low(back[:,HD:2*HD]); qvr=low(back[:,2*HD:3*HD]); p=back[:,3*HD:]
        pbf=low(p)
        delta=jnp.sum(g0.astype(jnp.float32)*at_ref[i0:i0+BLK,:].astype(jnp.float32),axis=-1,keepdims=True)
        delta=lax.dot_general(flip.astype(jnp.float32),jnp.broadcast_to(delta,(BLK,HD)),(((1,),(0,)),((),())),precision=lax.Precision.HIGHEST,preferred_element_type=jnp.float32)[:,:1]
        gr=p*((dot(g,v,NT)-delta)*SCALE)
        grb=low(gr)
        gvb=dot(pbf,g,TN); gkb=dot(grb,qur,TN)
        gv=gvb if gv is None else gv+gvb
        gk=gkb if gk is None else gk+gkb
        gqu=dot(grb,k)
        pad=jnp.concatenate([gr,jnp.zeros((BLK,BLK),jnp.float32)],axis=1)
        gp=low(pltpu.roll(pad,0,1,stride=1,stride_axis=0))
        gpt_acc[w0:w0+W,:]+=dot(gp,qvr,TN)
        gqv=dot(gp,pt_ref[w0:w0+W,:])
        gq_ref[i0:i0+BLK,:]=low(dot(flip,low(gqu+gqv)))
        a=jnp.sum(gqu,axis=0,keepdims=True); c=jnp.sum(gqv,axis=0,keepdims=True)
        su=a if su is None else su+a; sv=c if sv is None else sv+c
    gpt_ref[...]=gpt_acc[...].astype(jnp.bfloat16)
    gk_ref[...]=jnp.where(first,gk[:T],gk[T:]); gv_ref[...]=jnp.where(first,gv[:T],gv[T:])
    gko_ref[...]=jnp.where(first,gk[T:],gk[:T]).astype(jnp.bfloat16); gvo_ref[...]=jnp.where(first,gv[T:],gv[:T]).astype(jnp.bfloat16)
    gb_ref[...]=jnp.concatenate([su,sv,jnp.zeros((6,su.shape[1]),jnp.float32)],axis=0)

def col(rows,off=0): return pl.BlockSpec((rows,HD),lambda h,off=off:(0,h+off))
def attn_bwd(sc,qkv,kvo,pt,pb,g,at,p):
    T=qkv.shape[0]; D=qkv.shape[1]//3; H=D//HD
    f32=jnp.float32; bf=jnp.bfloat16
    return pl.pallas_call(attn_bwd_kernel,grid=(H,),
        in_specs=[pl.BlockSpec(memory_space=pltpu.SMEM),col(T),col(T,H),col(T,2*H),col(T),col(T,H),col(3*T),col(pb.shape[0]),col(T),col(T),pl.BlockSpec((1,T,2*T),lambda h:(h,0,0))],
        out_specs=[col(T)]*5+[col(3*T),col(8)],
        out_shape=[jax.ShapeDtypeStruct((T,D),bf),jax.ShapeDtypeStruct((T,D),f32),jax.ShapeDtypeStruct((T,D),f32),jax.ShapeDtypeStruct((T,D),bf),jax.ShapeDtypeStruct((T,D),bf),jax.ShapeDtypeStruct((3*T,D),bf),jax.ShapeDtypeStruct((8,D),f32)],
        scratch_shapes=[pltpu.VMEM((3*T,HD),f32)],
        compiler_params=pltpu.CompilerParams(vmem_limit_bytes=48*2**20),
        cost_estimate=pl.CostEstimate(flops=H*T*2*T*HD*2*6,bytes_accessed=30*2**20,transcendentals=0),
    )(sc,qkv,qkv,qkv,kvo,kvo,pt,pb,g,at,p)

def reduce_kernel(plan, zfirst, nz, nops, *refs):
    n=len(plan)
    refs=list(refs)
    take=lambda m: [refs.pop(0) for _ in range(m)]
    ops=take(nops); ready,small,gi=take(3)
    out,out_s,gi_o,far,far_s=take(5)
    tw,tsm,sw,ssm,cw,csm,ab,bb=take(8)
    x1=take(n); y1=take(n); x2=take(n); y2=take(n); zb=take(n)
    (cs,cr,x1s,x1r,y1s,y1r,x2s,x2r,y2s,y2r,axs,axr,ays,ayr,aas,aar,abs_,abr,acs,acr,zrs,zrr,zls,zlr,own,cld,loc,opsem,fs,frv,keeps)=refs
    k=place(); dp,z,c=k["dp"],k["z"],k["c"]
    bx=k["p"]%2; by=k["p"]//2
    tcore=z//2; tdp=dp-c+tcore
    bar=pltpu.get_barrier_semaphore()
    def sig(dev): pl.semaphore_signal(bar,inc=1,device_id=dev,device_id_type=MESH)
    for a in ("core","xn","yn"): sig((k[a],z))
    for ok,zz in ((z>0,z-1),(z<nz-1,z+1)):
        @pl.when(ok)
        def _(): sig((dp,zz))
    for u in range(2):
        @pl.when(jnp.logical_or(tcore!=c, 2*c+u!=z))
        def _(): sig((tdp,2*c+u))
    one=lambda b: jnp.where(b,1,0)
    pl.semaphore_wait(bar,3+one(z>0)+one(z<nz-1)+2-one(tcore==c))
    def rc(src,dst,s,r,dev):
        return pltpu.make_async_remote_copy(src_ref=src,dst_ref=dst,send_sem=s,recv_sem=r,device_id=dev,device_id_type=MESH)
    xn=(k["xn"],z); yn=(k["yn"],z); cn=(k["core"],z)
    nt=tw.shape[0]; nsnd=sw.shape[0]; nc=cw.shape[0]
    big=lambda i: len(plan[i])>0
    tb=lambda i: tw.at[i%nt] if big(i) else tsm
    sb=lambda i: sw.at[i%nsnd] if big(i) else ssm
    cb=lambda i: cw.at[i%nc] if big(i) else csm
    fb=lambda i: far.at[i] if big(i) else far_s
    ob=lambda i: out.at[i] if big(i) else out_s
    half=lambda i: 128 if big(i) else 16
    A=lambda i: pl.ds(0,half(i))
    B=lambda i: pl.ds(half(i),half(i))
    send_c=lambda i: rc(sb(i),fb(i),cs.at[i],cr.at[i],cn)
    load_c=lambda i: pltpu.make_async_copy(fb(i),cb(i),cld.at[i])
    zf=lambda i: i in zfirst
    def shard(i,r,*rest):
        return r.at[(z,)+rest] if zf(i) else r.at[(slice(None),)+rest]
    send_x1=lambda i: rc(shard(i,tb(i),slice(None),1-bx,A(i)),x1[i],x1s.at[i],x1r.at[i],xn)
    send_y1=lambda i: rc(shard(i,tb(i),1-by,slice(None),B(i)),y1[i],y1s.at[i],y1r.at[i],yn)
    send_x2=lambda i: rc(shard(i,tb(i),1-by,bx,A(i)),x2[i],x2s.at[i],x2r.at[i],yn)
    send_y2=lambda i: rc(shard(i,tb(i),by,1-bx,B(i)),y2[i],y2s.at[i],y2r.at[i],xn)
    line=lambda i,t: tb(i).at[t] if zf(i) else tb(i).at[t,by,bx]
    send_r=lambda i,t: rc(line(i,t),zb[i].at[t],zrs.at[i,t],zrr.at[i,t],(dp,z+1))
    send_l=lambda i,t,last: rc(line(i,t),zb[i].at[nz if last else t],zls.at[i,t],zlr.at[i,t],(dp,z-1))
    mine=lambda i: tb(i).at[z,by,bx]
    send_ax=lambda i: rc(mine(i),ob(i).at[by,bx,c],axs.at[i],axr.at[i],xn)
    send_ay=lambda i: rc(mine(i),ob(i).at[by,bx,c],ays.at[i],ayr.at[i],yn)
    keep_a=lambda i: pltpu.make_async_copy(mine(i),ob(i).at[by,bx,c],loc.at[i])
    send_aa=lambda i: rc(ob(i).at[by,1-bx,c,A(i)],ob(i).at[by,1-bx,c,A(i)],aas.at[i],aar.at[i],yn)
    send_ab=lambda i: rc(ob(i).at[1-by,bx,c,B(i)],ob(i).at[1-by,bx,c,B(i)],abs_.at[i],abr.at[i],xn)
    send_ac=lambda i: rc(ob(i).at[:,:,c],ob(i).at[:,:,c],acs.at[i],acr.at[i],cn)
    def add(dst,src):
        dst[...]=(dst[...].astype(jnp.float32)+src[...].astype(jnp.float32)).astype(jnp.bfloat16)
    def loop(m,f):
        lax.fori_loop(0,m,lambda j,_: (f(j),0)[1],0)
    def move(u): return rc(gi.at[u],gi_o.at[z%2],fs.at[u],frv.at[z%2],(tdp,2*c+u))
    keep=pltpu.make_async_copy(gi.at[z%2],gi_o.at[z%2],keeps.at[0])
    def operand(i):
        if len(plan[i])==5:
            l,r,zs,lo,ro=plan[i]; s=i%2
            cps=[pltpu.make_async_copy(ops[l].at[:,pl.ds(t*zs+lo,256)],ab.at[s,t],opsem.at[s,t]) for t in range(nz)]
            return cps+[pltpu.make_async_copy(ops[r].at[:,pl.ds(ro,1024)],bb.at[s],opsem.at[s,nz])]
        if big(i):
            q=[(yy,xx) for yy in range(2) for xx in range(2)]
            cols=lambda yy,xx,cc: pl.ds(pl.multiple_of((yy*4+xx*2+cc)*128,128),128)
            return ([pltpu.make_async_copy(ready.at[:,:,cols(yy,xx,c)],tb(i).at[:,yy,xx],opsem.at[i%2,yy*2+xx]) for yy,xx in q]
                +[pltpu.make_async_copy(ready.at[:,:,cols(yy,xx,1-c)],sb(i).at[:,yy,xx],opsem.at[i%2,4+yy*2+xx]) for yy,xx in q])
        return [pltpu.make_async_copy(small.at[:,:,:,c],tb(i),opsem.at[i%2,0]),pltpu.make_async_copy(small.at[:,:,:,1-c],sb(i),opsem.at[i%2,1])]
    def drain(i):
        for f in (send_x1,send_y1,send_x2,send_y2,send_ax,send_ay): f(i).wait_send()
        for t in range(nz):
            @pl.when(z<t)
            def _(): send_r(i,t).wait_send()
            @pl.when(z>t)
            def _(): send_l(i,t,False).wait_send()
    bigs=[i for i in range(n) if big(i)]
    def sl(i):
        if big(i) and i-nt in bigs: drain(i-nt)
        if big(i) and i-nsnd in bigs: send_c(i-nsnd).wait_send()
        for cp in operand(i): cp.start()
    def s0(i):
        for cp in operand(i): cp.wait()
        if len(plan[i])==5:
            s=i%2; T=tb(i); Sb=sb(i)
            cut=lambda cc: jnp.concatenate([bb[s,:,pl.ds(pl.multiple_of((2*q+cc)*128,128),128)] for q in range(4)],axis=1)
            def make(cc,dst):
                right=cut(cc)
                def f(t):
                    tile=lax.dot_general(ab[s,t],right,TN,preferred_element_type=jnp.float32).astype(jnp.bfloat16)
                    for q in range(4): dst[t,q//2,q%2]=tile[:,128*q:128*q+128]
                loop(nz,f)
            make(1-c,Sb)
            send_c(i).start()
            make(c,T)
        else:
            send_c(i).start()
    def s1a(i):
        send_c(i).wait_recv(); load_c(i).start()
    def s1(i):
        load_c(i).wait()
        T=tb(i); C=cb(i)
        loop(nz*4,lambda j: add(T.at[j//4,(j//2)%2,j%2],C.at[j//4,(j//2)%2,j%2]))
        if zf(i): line_start(i)
        else: xy_start(i)
    def xy_start(i):
        send_x1(i).start(); send_y1(i).start()
    def line_start(i):
        @pl.when(z==0)
        def _():
            for t in reversed(range(1,nz)): send_r(i,t).start()
        @pl.when(z==nz-1)
        def _():
            for t in range(nz-1): send_l(i,t,t==nz-2).start()
    def s2(i):
        T=tb(i)
        send_x1(i).wait_recv()
        if zf(i): loop(2,lambda j: add(T.at[z,j,bx,A(i)],x1[i].at[j]))
        else: loop(nz*2,lambda j: add(T.at[j//2,j%2,bx,A(i)],x1[i].at[j//2,j%2]))
        send_x2(i).start()
        send_y1(i).wait_recv()
        if zf(i): loop(2,lambda j: add(T.at[z,by,j,B(i)],y1[i].at[j]))
        else: loop(nz*2,lambda j: add(T.at[j//2,by,j%2,B(i)],y1[i].at[j//2,j%2]))
        send_y2(i).start()
    def s3(i):
        T=tb(i)
        send_x2(i).wait_recv()
        if zf(i): add(T.at[z,by,bx,A(i)],x2[i])
        else: loop(nz,lambda j: add(T.at[j,by,bx,A(i)],x2[i].at[j]))
        send_y2(i).wait_recv()
        if zf(i): add(T.at[z,by,bx,B(i)],y2[i])
        else: loop(nz,lambda j: add(T.at[j,by,bx,B(i)],y2[i].at[j]))
        if zf(i): spread_start(i)
        else: line_start(i)
    def add_line(i,t,slot):
        if zf(i): loop(4,lambda j: add(tb(i).at[t,j//2,j%2],zb[i].at[slot,j//2,j%2]))
        else: add(line(i,t),zb[i].at[slot])
    def hop(h,i):
        @pl.when(z==h)
        def _():
            for t in reversed(range(h+1,nz)):
                send_r(i,t).wait_recv()
                add_line(i,t,t)
                send_r(i,t).start()
        @pl.when(z==nz-1-h)
        def _():
            for t in range(nz-1-h):
                send_l(i,t,False).wait_recv()
                add_line(i,t,t)
                send_l(i,t,t==nz-2-h).start()
    def s6(i):
        @pl.when(z>0)
        def _():
            send_r(i,z).wait_recv()
            add_line(i,z,z)
        @pl.when(z<nz-1)
        def _():
            send_l(i,z,False).wait_recv()
            add_line(i,z,nz)
        if zf(i): xy_start(i)
        else: spread_start(i)
    def spread_start(i):
        send_ax(i).start(); send_ay(i).start(); keep_a(i).start()
    def s7(i):
        send_ax(i).wait_recv(); send_aa(i).start()
        send_ay(i).wait_recv(); send_ab(i).start()
    def s8(i):
        keep_a(i).wait()
        send_aa(i).wait_recv(); send_ab(i).wait_recv(); send_ac(i).start()
    def start_moves():
        for u in range(2):
            @pl.when(jnp.logical_or(tcore!=c,2*c+u!=z))
            def _(): move(u).start()
        @pl.when(tcore==c)
        def _(): keep.start()
    hops=[functools.partial(hop,h) for h in range(1,nz-1)]
    xy_stages=list(zip([sl,s0,s1a,s1,s2,s3]+hops+[s6,s7,s8],XY_LAGS))
    z_stages=list(zip([sl,s0,s1a,s1]+hops+[s6,s2,s3,s7,s8],Z_LAGS))
    for s in range(n+max(XY_LAGS+Z_LAGS)):
        if s==MOVE_AT: start_moves()
        todo=[(d,f,i) for i in range(n) for f,d in (z_stages if zf(i) else xy_stages) if i+d==s]
        for d,f,i in sorted(todo,key=lambda x:-x[0]): f(i)
    for i in range(n):
        if not (big(i) and i+nt in bigs): drain(i)
        if not (big(i) and i+nsnd in bigs): send_c(i).wait_send()
        send_aa(i).wait_send(); send_ab(i).wait_send()
        send_ac(i).wait()
    for u in range(2):
        @pl.when(jnp.logical_or(tcore!=c,2*c+u!=z))
        def _():
            move(u).wait_send()
            rc(gi.at[u],gi_o.at[u],fs.at[u],frv.at[u],(tdp,2*c+u)).wait_recv()
    @pl.when(tcore==c)
    def _(): keep.wait()

XY_LAGS=(0,1,2,3,5,6,7,8,9,10,11)
Z_LAGS=(0,1,2,3,5,6,8,9,10,11,12)
SLOTS=14
MOVE_AT=0
def reduce_call(ops,ready,small,gi,plan,zfirst,nz,cid):
    n=len(plan); nb=sum(len(x)>0 for x in plan); bf=jnp.bfloat16
    rows=ops[0].shape[0]
    any_=pl.BlockSpec(memory_space=pl.ANY)
    sd=jax.ShapeDtypeStruct
    outs=[sd((nb,2,2,2,256,128),bf),sd((2,2,2,32,128),bf),sd(gi.shape,gi.dtype),sd((nb,nz,2,2,256,128),bf),sd((nz,2,2,32,128),bf)]
    V=pltpu.VMEM; S=pltpu.SemaphoreType.DMA
    h=[128 if len(x) else 16 for x in plan]
    lead=lambda i: () if i in zfirst else (nz,)
    scratch=[V((SLOTS,nz,2,2,256,128),bf),V((nz,2,2,32,128),bf),V((2,nz,2,2,256,128),bf),V((nz,2,2,32,128),bf),V((2,nz,2,2,256,128),bf),V((nz,2,2,32,128),bf),
        V((2,nz,rows,256),bf),V((2,rows,1024),bf)]
    scratch+=[V(lead(i)+(2,h[i],128),bf) for i in range(n)]*2+[V(lead(i)+(h[i],128),bf) for i in range(n)]*2
    scratch+=[V((nz+1,)+((2,2) if i in zfirst else ())+(2*h[i],128),bf) for i in range(n)]
    scratch+=[S((n,))]*20+[S((n,nz))]*4+[S((1,)),S((n,)),S((n,)),S((2,8)),S((2,)),S((2,)),S((1,))]
    return pl.pallas_call(functools.partial(reduce_kernel,plan,zfirst,nz,len(ops)),out_shape=outs,in_specs=[any_]*(len(ops)+3),out_specs=[any_]*len(outs),
        scratch_shapes=scratch,
        compiler_params=pltpu.CompilerParams(collective_id=cid,has_side_effects=True,vmem_limit_bytes=58*2**20),
        cost_estimate=pl.CostEstimate(flops=2*n*rows*2**20,bytes_accessed=100*2**20,transcendentals=0),
    )(*ops,ready,small,gi)[:3]

def grad_plan(seq_count):
    plan, names = [], {}
    def weight(name, left, right, blocks, shrink):
        names[name] = len(plan), blocks
        for j in range(blocks):
            plan.append((left, right, 256 * blocks, 256 * j, 0) if shrink else (left, right, 256, 0, 1024 * j))
    weight("w4", 0, 1, 4, True)
    weight("w3", 2, 3, 4, False)
    weight("wco", 4, 5, 1, False)
    weight("wci", 6, 7, 2, False)
    weight("wo", 8, 9, 1, False)
    weight("wqkv", 10, 11, 3, False)
    names["wpos"] = len(plan), 1
    plan.append((0,))
    weight("w2", 12, 13, 4, True)
    weight("w1", 14, 15, 4, False)
    plan.append(())
    return plan, names

WIDEN_SLOTS = 4


def widen_kernel(spots, blocks_ref, *refs):
    outs, (narrow, wide, in_sem, out_sem) = refs[:-4], refs[-4:]
    count = len(spots)

    def fetch(i):
        return pltpu.make_async_copy(blocks_ref.at[i], narrow.at[i % WIDEN_SLOTS], in_sem.at[i % WIDEN_SLOTS])

    def put(i):
        which, row, column = spots[i]
        target = outs[which].at[pl.ds(row, 256), pl.ds(column, 1024)]
        return pltpu.make_async_copy(wide.at[i % WIDEN_SLOTS], target, out_sem.at[i % WIDEN_SLOTS])

    for i in range(WIDEN_SLOTS - 1):
        fetch(i).start()
    for i in range(count):
        if i + WIDEN_SLOTS - 1 < count:
            fetch(i + WIDEN_SLOTS - 1).start()
        fetch(i).wait()
        if i >= WIDEN_SLOTS:
            put(i - WIDEN_SLOTS).wait()
        slot = i % WIDEN_SLOTS

        def cast(piece, _):
            wide[slot, :, pl.ds(pl.multiple_of(128 * piece, 128), 128)] = narrow[slot, piece].astype(jnp.float32)
            return 0

        lax.fori_loop(0, 8, cast, 0, unroll=True)
        put(i).start()
    for i in range(count - WIDEN_SLOTS, count):
        put(i).wait()


def widen(blocks, names):
    spots, shapes = [], []
    for which, (name, (first, length)) in enumerate(names.items()):
        tall = name in ("w2", "w4")
        spots += [(which, 256 * j if tall else 0, 0 if tall else 1024 * j) for j in range(length)]
        shapes.append(jax.ShapeDtypeStruct((256 * length, 1024) if tall else (256, 1024 * length), jnp.float32))
    anywhere = pl.BlockSpec(memory_space=pl.ANY)
    wide = pl.pallas_call(
        functools.partial(widen_kernel, spots),
        in_specs=[anywhere],
        out_specs=[anywhere] * len(shapes),
        out_shape=shapes,
        scratch_shapes=[
            pltpu.VMEM((WIDEN_SLOTS, 8, 256, 128), jnp.bfloat16),
            pltpu.VMEM((WIDEN_SLOTS, 256, 1024), jnp.float32),
            pltpu.SemaphoreType.DMA((WIDEN_SLOTS,)),
            pltpu.SemaphoreType.DMA((WIDEN_SLOTS,)),
        ],
        compiler_params=pltpu.CompilerParams(vmem_limit_bytes=56 * 2**20),
        cost_estimate=pl.CostEstimate(flops=0, bytes_accessed=36 * 2**20, transcendentals=0),
    )(blocks)
    return dict(zip(names, wide))


def reduce_all(ops, ready, g_small, grad_input, seq_count):
    width = D // seq_count
    pieces = width // 128
    small = g_small.reshape(32, seq_count, pieces, 128).transpose(1, 2, 0, 3)
    small = jnp.pad(small, ((0, 0), (0, 8 - pieces), (0, 0), (0, 0))).reshape(seq_count, 2, 2, 2, 32, 128)
    plan, names = grad_plan(seq_count)
    by_line = {i for i in range(1, len(plan) - 1, 3)}
    blocks, small, grad_input = reduce_call(ops, ready, small, grad_input, plan, by_line, seq_count, 1)
    count = lax.axis_size("dp")
    if count > 8:
        groups = [[i + 8 * quad for quad in range(count // 8)] for i in range(8)]
        blocks, small = (lax.psum(x, "dp", axis_index_groups=groups) for x in (blocks, small))
    sums = widen(blocks.reshape(-1, 8, 256, 128), names)
    sums["wpos"] = sums["wpos"].T
    small = small.reshape(8, 32, 128)[:pieces].transpose(1, 0, 2).reshape(32, width).astype(jnp.float32)
    return sums, small, grad_input


def layer_norm(stream, gain, offset):
    average = jnp.mean(stream, axis=-1, keepdims=True)
    centred = stream - average
    spread = jnp.mean(centred * centred, axis=-1, keepdims=True)
    return centred * lax.rsqrt(spread + EPSILON) * gain + offset


def layer_norm_back(stream, gain, grad):
    average = jnp.mean(stream, axis=-1, keepdims=True)
    centred = stream - average
    spread = jnp.mean(centred * centred, axis=-1, keepdims=True)
    inverse = lax.rsqrt(spread + EPSILON)
    unit = centred * inverse
    scaled = grad * gain
    grad_stream = inverse * (
        scaled
        - jnp.mean(scaled, axis=-1, keepdims=True)
        - unit * jnp.mean(scaled * unit, axis=-1, keepdims=True)
    )
    return grad_stream, jnp.sum(grad * unit, axis=0), jnp.sum(grad, axis=0)


def swish(value):
    return value * jax.nn.sigmoid(value)


def swish_back(value, grad):
    gate = jax.nn.sigmoid(value)
    return grad * gate * (1.0 + value * (1.0 - gate))


def position_tables(first_row, rows, length, features):
    fine = 32
    column = lax.broadcasted_iota(jnp.int32, (1, features), 1)
    odd = column % 2 == 1
    frequency = jnp.exp((column // 2).astype(jnp.float32) * (-2.0 * math.log(10000.0) / features))
    coarse_at = (length - 1 - first_row - fine * jnp.arange(rows // fine, dtype=jnp.int32)).astype(jnp.float32)
    fine_at = jnp.arange(fine, dtype=jnp.int32).astype(jnp.float32)
    coarse = coarse_at[:, None] * frequency
    small = fine_at[:, None] * frequency
    coarse_sin, coarse_cos = jnp.sin(coarse), jnp.cos(coarse)
    return jnp.where(odd, coarse_cos, coarse_sin), jnp.where(odd, -coarse_sin, coarse_cos), jnp.cos(small), jnp.sin(small)


def mm(left, right):
    return jnp.dot(left, right, preferred_element_type=jnp.float32)


def mm_nt(left, right):
    return lax.dot_general(left, right, NT, preferred_element_type=jnp.float32)


def mm_tn(left, right):
    return lax.dot_general(left, right, TN, preferred_element_type=jnp.float32).astype(jnp.bfloat16)


def pair_swap(value):
    count = lax.axis_size("dp")
    return lax.ppermute(value, "dp", [(i, i + 1 - 2 * (i % 2)) for i in range(count)])


def redistribute(value):
    dp_count, seq_count = lax.axis_size("dp"), lax.axis_size("seq")
    z = lax.axis_index("seq")
    routes = ([], [])
    for dp in range(dp_count):
        for zz in range(seq_count):
            a, b, c = zz // 2, zz % 2, dp % 2
            for which in range(2):
                routes[which].append(
                    (dp * seq_count + zz, (dp - c + a) * seq_count + 2 * c + (b + which) % 2)
                )
    low = z % 2 == 0
    straight = lax.ppermute(jnp.where(low, value[0], value[1]), ("dp", "seq"), routes[0])
    crossed = lax.ppermute(jnp.where(low, value[1], value[0]), ("dp", "seq"), routes[1])
    return jnp.stack([jnp.where(low, straight, crossed), jnp.where(low, crossed, straight)])


def with_halo(rows, core):
    margin = (KERNEL - 1) // 2
    got = pair_swap(jnp.where(core == 0, rows[-margin:], rows[:margin]))
    none = jnp.zeros_like(got)
    return jnp.concatenate([jnp.where(core == 1, got, none), rows, jnp.where(core == 0, got, none)], axis=0)


def shards(
    frames, cotangent, lengths, assignment, norm_gains, norm_biases, expand_one, shrink_one, qkv_weight,
    pos_weight, pos_biases, attn_out, conv_in, conv_depth, conv_out, expand_two, shrink_two,
):
    seq_count = lax.axis_size("seq")
    dp, z = lax.axis_index("dp"), lax.axis_index("seq")
    core = dp % 2
    own_length = lengths[assignment[dp - core + z // 2], z % 2]
    rows = 2 * frames.shape[2]
    tables = position_tables((1 - core) * rows, 3 * rows, 2 * rows, D)
    weights, small_all, x_in, cot, first_part = gather(
        [expand_one, shrink_one, qkv_weight, pos_weight, attn_out, conv_in, conv_out, expand_two, shrink_two],
        [norm_gains, norm_biases, conv_depth, pos_biases], frames[0], cotangent[0], own_length.reshape(1), tables, seq_count,
    )
    w1, w2, wqkv, _, wo, wci, wco, w3, w4 = weights
    h1, a1, s1, x1, ha, qkv, kv_other, sinusoid, ptab, prob, attn = first_part
    vectors = small_all.transpose(1, 0, 2).reshape(32, D).astype(jnp.float32)
    gains, biases, depth, pos_pair = vectors[0:6], vectors[6:12], vectors[12:17], vectors[16:24]
    pos_pair = jnp.concatenate([vectors[17:19], jnp.zeros((6, D), jnp.float32)], axis=0)
    x0 = x_in.reshape(rows, D).astype(jnp.float32)
    cot = cot.reshape(rows, D).astype(jnp.float32)
    valid = (core * rows + jnp.arange(rows, dtype=jnp.int32) < own_length).astype(jnp.float32)[:, None]

    scalars = jnp.stack([core, own_length]).astype(jnp.int32)
    x2 = x1 + mm(attn, wo)
    hc = layer_norm(x2, gains[2], biases[2]).astype(jnp.bfloat16)
    dbl = mm(hc, wci)
    gate = jax.nn.sigmoid(dbl[:, D:])
    m = (dbl[:, :D] * gate * valid).astype(jnp.bfloat16)
    rim = with_halo(m, core)
    cv = depth[0] * rim[0:rows]
    for tap in range(1, KERNEL):
        cv = cv + depth[tap] * rim[tap : tap + rows]
    sc = swish(layer_norm(cv, gains[3], biases[3])).astype(jnp.bfloat16)
    x3 = x2 + mm(sc, wco)
    h2 = layer_norm(x3, gains[4], biases[4]).astype(jnp.bfloat16)
    a2 = mm(h2, w3)
    s2 = swish(a2).astype(jnp.bfloat16)
    x4 = x3 + 0.5 * mm(s2, w4)
    encoded = layer_norm(x4, gains[5], biases[5]).astype(jnp.bfloat16)
    encoded = redistribute(encoded.reshape(2, rows // 2, D))

    gx4, gg5, gb5 = layer_norm_back(x4, gains[5], cot)
    go2 = (0.5 * gx4).astype(jnp.bfloat16)
    ga2 = swish_back(a2, mm_nt(go2, w4)).astype(jnp.bfloat16)
    back, gg4, gb4 = layer_norm_back(x3, gains[4], mm_nt(ga2, w3))
    gx3 = gx4 + back
    gco = gx3.astype(jnp.bfloat16)
    inner = layer_norm(cv, gains[3], biases[3])
    gcv, gg3, gb3 = layer_norm_back(cv, gains[3], swish_back(inner, mm_nt(gco, wco)))
    gcv = gcv.astype(jnp.bfloat16)
    grim = with_halo(gcv, core)
    gm = depth[0] * grim[KERNEL - 1 : KERNEL - 1 + rows]
    for tap in range(1, KERNEL):
        gm = gm + depth[tap] * grim[KERNEL - 1 - tap : KERNEL - 1 - tap + rows]
    g_depth = jnp.stack([
        jnp.sum(gcv.astype(jnp.float32) * rim[tap : tap + rows].astype(jnp.float32), axis=0) for tap in range(KERNEL)
    ])
    gm = gm * valid
    gdbl = jnp.concatenate(
        [(gm * gate).astype(jnp.bfloat16), (gm * dbl[:, :D] * gate * (1.0 - gate)).astype(jnp.bfloat16)], axis=1
    )
    back, gg2, gb2 = layer_norm_back(x2, gains[2], mm_nt(gdbl, wci))
    gx2 = gx3 + back
    gao = gx2.astype(jnp.bfloat16)
    gattn = mm_nt(gao, wo).astype(jnp.bfloat16)
    gq, gk, gv, gk_other, gv_other, gptab, g_pair = attn_bwd(scalars, qkv, kv_other, ptab, pos_pair, gattn, attn, prob)
    got = pair_swap(jnp.concatenate([gk_other, gv_other], axis=1))
    gk = (gk + got[:, :D]).astype(jnp.bfloat16)
    gv = (gv + got[:, D:]).astype(jnp.bfloat16)
    gqkv = jnp.concatenate([gq, gk, gv], axis=1)
    g_wpos = mm_tn(gptab, sinusoid).reshape(seq_count, D // seq_count, D)
    back, gg1, gb1 = layer_norm_back(x1, gains[1], mm_nt(gqkv, wqkv))
    gx1 = gx2 + back
    go1 = (0.5 * gx1).astype(jnp.bfloat16)
    ga1 = swish_back(a1, mm_nt(go1, w2)).astype(jnp.bfloat16)
    back, gg0, gb0 = layer_norm_back(x0, gains[0], mm_nt(ga1, w1))
    gx0 = gx1 + back
    g_small = jnp.concatenate(
        [jnp.stack([gg0, gg1, gg2, gg3, gg4, gg5, gb0, gb1, gb2, gb3, gb4, gb5]), g_depth, g_pair[:2], jnp.zeros((13, D), jnp.float32)],
        axis=0,
    ).astype(jnp.bfloat16)
    sums, s_small, grad_input = reduce_all(
        [s2, go2, h2, ga2, sc, gco, hc, gdbl, attn, gao, ha, gqkv, s1, go1, h1, ga1],
        g_wpos, g_small, gx0.astype(jnp.bfloat16).reshape(2, rows // 2, D), seq_count,
    )
    grad_input = grad_input.astype(jnp.float32)
    return (
        encoded[None], grad_input[None], s_small[0:6], s_small[6:12], sums["w1"], sums["w2"], sums["wqkv"],
        sums["wpos"], s_small[17:19], sums["wo"], sums["wci"], s_small[12:17], sums["wco"], sums["w3"], sums["w4"],
    )


def solution(mesh):
    rows, columns = P("seq", None), P(None, "seq")
    act = P("dp", None, "seq", None)
    return jax.shard_map(
        shards,
        mesh=mesh,
        in_specs=(act, act, P(), P(), columns, columns, rows, rows, rows, columns, columns, rows, rows, columns, rows, rows, rows),
        out_specs=(act, act, columns, columns, rows, rows, rows, columns, columns, rows, rows, columns, rows, rows, rows),
        check_vma=False,
    )
```

```python
import functools
import math

import jax
import jax.numpy as jnp
from jax import lax
from jax.experimental import pallas as pl
from jax.experimental.pallas import tpu as pltpu
from jax.sharding import PartitionSpec as P

D = 1024
KERNEL = 5
EPSILON = 1e-05
MESH=pl.DeviceIdType.MESH

def place():
    dp=lax.axis_index("dp"); z=lax.axis_index("seq")
    c=dp%2; p=(dp//2)%4
    bx=p%2; by=p//2
    return dict(dp=dp,z=z,c=c,p=p,px=p+1-2*bx,py=p+2-4*by,
                core=dp+1-2*c, xn=dp+2-4*bx, yn=dp+4-8*by)

def rows_norm(value, gain, offset):
    centred=value-jnp.mean(value,axis=-1,keepdims=True)
    return centred*lax.rsqrt(jnp.mean(centred*centred,axis=-1,keepdims=True)+EPSILON)*gain+offset

def gather_kernel(items, order, nw, nz, *refs):
    ni=len(items)
    refs=list(refs)
    take=lambda m: [refs.pop(0) for _ in range(m)]
    ins=take(nw); vecs=take(4); fr,ct,length,lead,quarter,fine_c,fine_s=take(7)
    outs=take(nw); small_o,fr_o,ct_o,h1_o,a1_o,s1_o,x1_o,ha_o,qkv_o,kvo_o,pe_o,pt_o,p_o,at_o=take(14)
    stage=take(nw)
    x0,sv,h1,acc,ha,qkv,kvo,pe,pt,at,w1b,w2b,ab,sb,wqb,wpb,pb,x1b,small,small_f=take(20)
    (zr,xr,yr,ar,br,cr,zsr,zsl,xs,ys,as_,bs,cs,loc,lod,fs,frv,one_sem,in_sem,out_sem,kv_s,kv_r)=refs
    k=place(); dp,z,c,p=k["dp"],k["z"],k["c"],k["p"]
    here=lambda zz:(dp,zz)
    tcore=z//2; tdp=dp-c+tcore
    small_f[...]=jnp.zeros_like(small_f)
    row=0
    for part in vecs:
        small_f[row:row+part.shape[0],:]=part[...].astype(jnp.float32); row+=part.shape[0]
    small[...]=small_f[...].astype(jnp.bfloat16)
    bar=pltpu.get_barrier_semaphore()
    def sig(dev): pl.semaphore_signal(bar,inc=1,device_id=dev,device_id_type=MESH)
    for n in ("core","xn","yn"): sig((k[n],z))
    for ok,zz in ((z>0,z-1),(z<nz-1,z+1)):
        @pl.when(ok)
        def _(): sig((dp,zz))
    for u in range(2):
        @pl.when(jnp.logical_or(tcore!=c, 2*c+u!=z))
        def _(): sig((tdp,2*c+u))
    one=lambda b: jnp.where(b,1,0)
    pl.semaphore_wait(bar,3+one(z>0)+one(z<nz-1)+2-one(tcore==c))
    def rc(src,dst,s,r,dev):
        return pltpu.make_async_remote_copy(src_ref=src,dst_ref=dst,send_sem=s,recv_sem=r,device_id=dev,device_id_type=MESH)
    allin=list(ins)+[small]; allout=list(outs)+[small_o]
    def piece(i,t,pp=None,half=None):
        if i==ni: return small_o.at[t]
        w,r0,q,c0,cc=items[i]
        if half is not None: q=q//2; r0=r0+half*q
        return outs[w].at[t,p if pp is None else pp,c,pl.ds(r0,q),pl.ds(c0,cc)]
    def own(i):
        if i==ni: return small
        w,r0,q,c0,cc=items[i]
        return ins[w].at[p,c,pl.ds(r0,q),pl.ds(c0,cc)]
    def zright(w,t,src=None): return rc(piece(w,t) if src is None else src,piece(w,t),zsr.at[w,t],zr.at[w,t],(dp,z+1))
    def zleft(w,t,src=None): return rc(piece(w,t) if src is None else src,piece(w,t),zsl.at[w,t],zr.at[w,t],(dp,z-1))
    def xsend(w,t): return rc(piece(w,t),piece(w,t),xs.at[w,t],xr.at[w,t],(k["xn"],z))
    def ysend(w,t): return rc(piece(w,t),piece(w,t),ys.at[w,t],yr.at[w,t],(k["yn"],z))
    def asend(w,t): return rc(piece(w,t,k["px"],0),piece(w,t,k["px"],0),as_.at[w,t],ar.at[w,t],(k["yn"],z))
    def bsend(w,t): return rc(piece(w,t,k["py"],1),piece(w,t,k["py"],1),bs.at[w,t],br.at[w,t],(k["xn"],z))
    def csend(i,t):
        w,r0,q,c0,cc=items[i]
        four=outs[w].at[t,:,c,pl.ds(r0,q),pl.ds(c0,cc)]
        return rc(four,four,cs.at[i,t],cr.at[i,t],(k["core"],z))
    def load(w): return pltpu.make_async_copy(allin[w],stage[w],lod.at[w])
    from_vmem=lambda w: small if w==nw else stage[w]
    def local(w): return pltpu.make_async_copy(from_vmem(w),allout[w].at[z],loc.at[w])
    redo=[(fr,fr_o,0),(ct,ct_o,1)]
    def move(a,u):
        s,d,i=redo[a]
        return rc(s.at[u],d.at[z%2],fs.at[i,u],frv.at[i,z%2],(tdp,2*c+u))
    def keep(a):
        s,d,i=redo[a]
        return pltpu.make_async_copy(s.at[z%2],d.at[z%2],loc.at[nw+1+i])
    def moves(a,f_remote,f_local):
        for u in range(2):
            @pl.when(jnp.logical_or(tcore!=c,2*c+u!=z))
            def _(): f_remote(a,u)
        @pl.when(tcore==c)
        def _(): f_local(a)
    def away(f):
        for d in range(1,nz):
            @pl.when(z-d>=0)
            def _(): f(z-d,True)
            @pl.when(z+d<nz)
            def _(): f(z+d,False)
    moves(0,lambda a,u:move(a,u).start(),lambda a:keep(a).start())
    def go(w):
        @pl.when(z<nz-1)
        def _(): zright(w,z,own(w)).start()
        @pl.when(z>0)
        def _(): zleft(w,z,own(w)).start()
    def f1(w,t,fromleft):
        zright(w,t).wait_recv()
        if fromleft:
            @pl.when(z<nz-1)
            def _(): zright(w,t).start()
        else:
            @pl.when(z>0)
            def _(): zleft(w,t).start()
        if w<ni:
            xsend(w,t).start(); ysend(w,t).start()
    def f2(w,t,_):
        xsend(w,t).wait_recv(); asend(w,t).start()
        ysend(w,t).wait_recv(); bsend(w,t).start()
    def f3(w,t,_):
        asend(w,t).wait_recv(); bsend(w,t).wait_recv(); csend(w,t).start()
    def at_(f,w,d):
        @pl.when(z-d>=0)
        def _(): f(w,z-d,True)
        @pl.when(z+d<nz)
        def _(): f(w,z+d,False)
    def arrived(i):
        for d in range(1,nz): at_(lambda i,t,_: csend(i,t).wait_recv(),i,d)
    got=set(); laid=set()
    def ensure(w):
        for i in range(ni):
            if items[i][0]==w: arrived(i); got.add(i)
        local(w).wait(); laid.add(w)
    rows=x0.shape[0]; quarter_rows=rows//4
    def landed(a):
        for pos in range(2):
            @pl.when(jnp.logical_or(tcore!=c,2*c+pos!=z))
            def _():
                s,d,i=redo[a]
                rc(s.at[pos],d.at[pos],fs.at[i,pos],frv.at[i,pos],(tdp,2*c+pos)).wait_recv()
        @pl.when(tcore==c)
        def _(): keep(a).wait()
    vec=lambda r: jnp.concatenate([sv[t,r:r+1,:] for t in range(nz)],axis=1).astype(jnp.float32)
    def copy_now(src,dst,sem):
        cp=pltpu.make_async_copy(src,dst,sem); cp.start(); return cp
    pending=[]
    def store(src,dst,key):
        pending.append(copy_now(src,dst,out_sem.at[key]))
    def u_norm0():
        landed(0); local(nw).wait(); laid.add(nw)
        cps=[copy_now(fr_o.at[j],x0.at[pl.ds(j*rows//2,rows//2)],one_sem.at[j]) for j in range(2)]+[copy_now(small_o,sv,one_sem.at[2])]
        for cp in cps: cp.wait()
        gain,off=vec(0),vec(6)
        def f(j):
            at_rows=pl.ds(pl.multiple_of(j*quarter_rows,quarter_rows),quarter_rows)
            h1[at_rows,:]=rows_norm(x0[at_rows,:].astype(jnp.float32),gain,off).astype(jnp.bfloat16)
        loop(4,f)
        acc[...]=jnp.zeros_like(acc)
        store(h1,h1_o,0)
    def u_table():
        n_fine=fine_c.shape[0]
        def f(j):
            row=pl.ds(j,1)
            block=lead[row,:]*fine_c[...]-quarter[row,:]*fine_s[...]
            pe[pl.ds(pl.multiple_of(j*n_fine,n_fine),n_fine),:]=block.astype(jnp.bfloat16)
        loop(lead.shape[0],f)
        store(pe,pe_o,1)
    def u_ptab(t):
        if t==0: ensure(3)
        copy_now(outs[3].at[t],wpb,one_sem.at[0]).wait()
        width=wpb.shape[3]
        pt[:,width*t:width*t+width]=mmv(pe[...],wpb[...].reshape(-1,width)).astype(jnp.bfloat16)
        if t==nz-1: store(pt,pt_o,2)
    mmv=lambda l,r: jnp.dot(l,r,preferred_element_type=jnp.float32)
    fcols=w1b.shape[-1]; nf=outs[0].shape[-1]//fcols
    per_z=outs[1].shape[3]*8; zb_rows=per_z//fcols
    lows=4//zb_rows
    a_load=lambda j: copy_now(outs[0].at[:,:,:,:,pl.ds(j*fcols,fcols)],w1b.at[j%2],in_sem.at[0,j%2])
    b_load=lambda j: copy_now(outs[1].at[j//zb_rows,pl.ds(j%zb_rows*lows,lows)],w2b.at[j%2],in_sem.at[1,j%2])
    flight={}
    def u_expand(j):
        if j==0:
            ensure(0); flight["a",0]=a_load(0)
        if j+1<nf: flight["a",j+1]=a_load(j+1)
        flight.pop(("a",j)).wait()
        if j>=2: flight.pop(("o",j-2)).wait()
        hidden=mmv(h1[...],w1b[j%2].reshape(-1,fcols))
        ab[j%2]=hidden
        cols=pl.ds(j*fcols,fcols)
        sb[:,cols]=(hidden*jax.nn.sigmoid(hidden)).astype(jnp.bfloat16)
        flight["o",j]=copy_now(ab.at[j%2],a1_o.at[:,cols],out_sem.at[3+j%2])
        if j==nf-1:
            pending.extend((flight.pop(("o",j-1)),flight.pop(("o",j))))
            store(sb,s1_o,5)
    def u_shrink(j):
        if j==0:
            ensure(1); flight["b",0]=b_load(0)
        if j+1<nf: flight["b",j+1]=b_load(j+1)
        flight.pop(("b",j)).wait()
        acc[...]+=mmv(sb[:,j*fcols:j*fcols+fcols],w2b[j%2].reshape(fcols,-1))
    def u_norm1():
        gain,off=vec(1),vec(7)
        def f(j):
            at_rows=pl.ds(pl.multiple_of(j*quarter_rows,quarter_rows),quarter_rows)
            mid=x0[at_rows,:].astype(jnp.float32)+0.5*acc[at_rows,:]
            acc[at_rows,:]=mid
            ha[at_rows,:]=rows_norm(mid,gain,off).astype(jnp.bfloat16)
        loop(4,f)
        store(acc,x1_o,7); store(ha,ha_o,8)
    qcols=wqb.shape[-1]; nq=outs[2].shape[-1]//qcols
    q_load=lambda j: copy_now(outs[2].at[:,:,:,:,pl.ds(j*qcols,qcols)],wqb.at[j%2],in_sem.at[2,j%2])
    def u_qkv(j):
        if j==0:
            ensure(2); flight["q",0]=q_load(0)
        if j+1<nq: flight["q",j+1]=q_load(j+1)
        flight.pop(("q",j)).wait()
        qkv[:,j*qcols:j*qcols+qcols]=mmv(ha[...],wqb[j%2].reshape(-1,qcols)).astype(jnp.bfloat16)
        if j==nq-1:
            store(qkv,qkv_o,9)
            swap_kv().start()
    dim=x0.shape[1]
    swap_kv=lambda: rc(qkv.at[:,pl.ds(dim,2*dim)],kvo,kv_s.at[0],kv_r.at[0],(k["core"],z))
    def u_head(h):
        if h==0:
            swap_kv().wait()
            store(kvo,kvo_o,10)
        if h>=2: flight.pop(("p",h-2)).wait()
        col=lambda off: pl.ds(off+h*HD,HD)
        attn_head(c==0,length[0],qkv[:,col(0)],qkv[:,col(dim)],qkv[:,col(2*dim)],kvo[:,col(0)],kvo[:,col(dim)],
            pt.at[:,col(0)],pairv[0:2,col(0)],at.at[:,col(0)],pb.at[h%2])
        flight["p",h]=copy_now(pb.at[h%2],p_o.at[h],out_sem.at[11+h%2])
        if h==heads-1:
            store(at,at_o,13)
            pending.extend((flight.pop(("p",h-1)),flight.pop(("p",h))))
    pairv=x1b
    def u_pair():
        pairv[0:1,:]=vec(17); pairv[1:2,:]=vec(18)
    def loop(m,f):
        lax.fori_loop(0,m,lambda j,_: (f(j),0)[1],0)
    last_item=lambda w: max(i for i in range(ni) if items[i][0]==w)
    heads=at.shape[1]//HD
    ready=lambda w: last_item(w)+nz+SLACK
    units=[(nz-1,2,u_norm0),(0,0,u_pair),(0,4,u_table)]
    units+=[(ready(3),1.5,functools.partial(u_ptab,t)) for t in range(nz)]
    units+=[(ready(0),1,functools.partial(u_expand,j)) for j in range(nf)]
    units+=[(ready(1),1,functools.partial(u_shrink,j)) for j in range(nf)]+[(0,2,u_norm1)]
    units+=[(ready(2),1,functools.partial(u_qkv,j)) for j in range(nq)]
    units+=[(ready(2)+2,2.5,functools.partial(u_head,h)) for h in range(heads)]
    def run(s,budget):
        while budget>0 and units and units[0][0]<=s:
            _,cost,unit=units.pop(0)
            unit(); budget-=cost
    go(ni)
    for w in range(AHEAD): go(w)
    for w in order: load(w).start()
    local(nw).start()
    for s in range(ni+nz):
        if s<nw:
            load(order[s]).wait(); local(order[s]).start()
        if s+AHEAD<ni: go(s+AHEAD)
        if s<nz-1: at_(f1,ni,s+1)
        if s==ni-1: moves(1,lambda a,u:move(a,u).start(),lambda a:keep(a).start())
        for f,late in ((f3,1),(f2,0),(f1,-1)):
            for d in range(1,nz):
                if 0<=s-d-late<ni: at_(f,s-d-late,d)
            run(s,BUDGET)
    run(10**6,10**6)
    for cp in pending: cp.wait()
    def away(f):
        for d in range(1,nz):
            @pl.when(z-d>=0)
            def _(): f(z-d,True)
            @pl.when(z+d<nz)
            def _(): f(z+d,False)
    for w in range(nw+1):
        if w not in laid: local(w).wait()
    for w in range(ni+1):
        @pl.when(z<nz-1)
        def _(): zright(w,z,own(w)).wait_send()
        @pl.when(z>0)
        def _(): zleft(w,z,own(w)).wait_send()
        def f(t,fromleft):
            if fromleft:
                @pl.when(z<nz-1)
                def _(): zright(w,t).wait_send()
            else:
                @pl.when(z>0)
                def _(): zleft(w,t).wait_send()
            if w<ni:
                for g in (xsend,ysend,asend,bsend,csend): g(w,t).wait_send()
                if w not in got: csend(w,t).wait_recv()
        away(f)
    for a in range(2):
        moves(a,lambda a,u:move(a,u).wait_send(),lambda a:None)
    landed(1)

ITEM=2**21
BUDGET=1.5
SLACK=1
AHEAD=3
def gather(ws,vecs,fr,ct,length,tables,nz,cid=0):
    nw=len(ws); bf=jnp.bfloat16; f32=jnp.float32
    small=jax.ShapeDtypeStruct((32,vecs[0].shape[1]),bf)
    ins=[w.reshape(4,2,w.shape[0]//8,w.shape[1]) for w in ws]
    order=[3,0,1,2]+list(range(4,nw))
    items=[]
    for w in order:
        q,cc=ins[w].shape[2:]
        parts=max(1,nz*8*q*cc//ITEM)
        for j in range(parts): items.append((w,0,q,j*cc//parts,cc//parts) if q<64 else (w,j*q//parts,q//parts,0,cc))
    ni=len(items)
    rows=2*fr.shape[1]; dim=fr.shape[2]; ff=ws[0].shape[1]; heads=dim//HD; wide=ws[3].shape[1]
    any_=pl.BlockSpec(memory_space=pl.ANY); vm=pl.BlockSpec(memory_space=pltpu.VMEM); sm=pl.BlockSpec(memory_space=pltpu.SMEM)
    sd=jax.ShapeDtypeStruct; V=pltpu.VMEM
    shp=[sd((nz,)+w.shape,w.dtype) for w in ins]+[sd((nz,)+small.shape,small.dtype),sd(fr.shape,fr.dtype),sd(ct.shape,ct.dtype)]
    shp+=[sd((rows,dim),bf),sd((rows,ff),f32),sd((rows,ff),bf),sd((rows,dim),f32),sd((rows,dim),bf),sd((rows,3*dim),bf),sd((rows,2*dim),bf),
        sd((3*rows,dim),bf),sd((3*rows,dim),bf),sd((heads,rows,2*rows),bf),sd((rows,dim),bf)]
    S=pltpu.SemaphoreType.DMA
    cut=512
    q0=ins[0].shape[2]; q2=ins[1].shape[2]
    scratch=[V(w.shape,w.dtype) for w in ins]
    scratch+=[V((rows,dim),bf),V((nz,)+small.shape,bf),V((rows,dim),bf),V((rows,dim),f32),V((rows,dim),bf),V((rows,3*dim),bf),V((rows,2*dim),bf),
        V((3*rows,dim),bf),V((3*rows,dim),bf),V((rows,dim),bf),
        V((2,nz,4,2,q0,cut),bf),V((2,cut//(2*q2),2,q2,dim),bf),V((2,rows,cut),f32),V((rows,ff),bf),V((2,nz,4,2,q0,cut),bf),V((4,2,ins[3].shape[2],wide),bf),
        V((2,rows,2*rows),bf),V((8,dim),f32),V(small.shape,bf),V(small.shape,f32)]
    scratch+=[S((ni+1,nz))]+[S((ni,nz))]*5+[S((ni+1,nz))]*2+[S((ni,nz))]*5+[S((nw+3,)),S((nw,)),S((2,2)),S((2,2)),S((3,)),S((3,2)),S((14,)),S((1,)),S((1,))]
    o=pl.pallas_call(functools.partial(gather_kernel,items,order,nw,nz),out_shape=shp,
        in_specs=[any_]*nw+[vm]*4+[any_]*2+[sm]+[vm]*4,out_specs=[any_]*len(shp),
        scratch_shapes=scratch,
        compiler_params=pltpu.CompilerParams(collective_id=cid,has_side_effects=True,vmem_limit_bytes=60*2**20),
        cost_estimate=pl.CostEstimate(flops=25*10**9,bytes_accessed=2*48*2**20,transcendentals=0),
    )(*ins,*vecs,fr,ct,length,*tables)
    full=[x.reshape(nz*w.shape[0],w.shape[1]) for x,w in zip(o[:nw],ws)]
    return full,o[nw],o[nw+1],o[nw+2],o[nw+3:]

HD=128; SCALE=1.0/math.sqrt(128)
BLK=256
NT=(((1,),(1,)),((),()))
TN=(((0,),(0,)),((),()))
def dot(a,b,dims=(((1,),(0,)),((),()))):
    return lax.dot_general(a,b,dims,preferred_element_type=jnp.float32)

def order(first, own, oth):
    return jnp.concatenate([jnp.where(first, own, oth), jnp.where(first, oth, own)], axis=0)

def attn_head(first,length,q,k,v,ko,vo,pt_ref,pb,o_ref,p_ref):
    T=q.shape[0]; L2=2*T
    q=q.astype(jnp.float32)
    qu=(q+pb[0:1]).astype(jnp.bfloat16); qv=(q+pb[1:2]).astype(jnp.bfloat16)
    k=order(first,k,ko); v=order(first,v,vo)
    W=BLK+L2
    keep=lax.broadcasted_iota(jnp.int32,(BLK,L2),1)<length
    for b in range(T//BLK):
        i0=b*BLK; w0=T-i0-BLK
        s=dot(qu[i0:i0+BLK],k,NT)
        placed=dot(qv[i0:i0+BLK],pt_ref[w0:w0+W,:],NT)
        s=s+pltpu.roll(placed,W-(BLK-1),1,stride=1,stride_axis=0)[:,:L2]
        s=jnp.where(keep,s*SCALE,-1e9)
        m=jnp.max(s,axis=-1,keepdims=True)
        e=jnp.exp(s-m)
        p=(e*(1.0/jnp.sum(e,axis=-1,keepdims=True))).astype(jnp.bfloat16)
        p_ref[i0:i0+BLK,:]=p
        o_ref[i0:i0+BLK,:]=dot(p,v).astype(jnp.bfloat16)

def attn_bwd_kernel(sc_ref, q_ref, k_ref, v_ref, ko_ref, vo_ref, pt_ref, pb_ref, g_ref, at_ref, p_ref,
                    gq_ref, gk_ref, gv_ref, gko_ref, gvo_ref, gpt_ref, gb_ref, gpt_acc):
    T=q_ref.shape[0]; L2=2*T
    first=sc_ref[0]==0
    q=q_ref[...].astype(jnp.float32)
    pb=pb_ref[...].astype(jnp.float32)
    qu=(q+pb[0:1]).astype(jnp.bfloat16); qv=(q+pb[1:2]).astype(jnp.bfloat16)
    k=order(first,k_ref[...],ko_ref[...]); v=order(first,v_ref[...],vo_ref[...])
    W=BLK+L2
    flip=(lax.broadcasted_iota(jnp.int32,(BLK,BLK),0)+lax.broadcasted_iota(jnp.int32,(BLK,BLK),1)==BLK-1).astype(jnp.float32).astype(jnp.bfloat16)
    gpt_acc[...]=jnp.zeros_like(gpt_acc)
    gk=gv=None; su=sv=None
    low=lambda v: v.astype(jnp.bfloat16)
    for b in range(T//BLK):
        i0=b*BLK; w0=T-i0-BLK
        g0=g_ref[i0:i0+BLK,:]
        rows=jnp.concatenate([g0,qu[i0:i0+BLK],qv[i0:i0+BLK],p_ref[0,i0:i0+BLK,:]],axis=1)
        back=dot(flip,rows)
        g=low(back[:,:HD]); qur=low(back[:,HD:2*HD]); qvr=low(back[:,2*HD:3*HD]); p=back[:,3*HD:]
        pbf=low(p)
        delta=jnp.sum(g0.astype(jnp.float32)*at_ref[i0:i0+BLK,:].astype(jnp.float32),axis=-1,keepdims=True)
        delta=lax.dot_general(flip.astype(jnp.float32),jnp.broadcast_to(delta,(BLK,HD)),(((1,),(0,)),((),())),precision=lax.Precision.HIGHEST,preferred_element_type=jnp.float32)[:,:1]
        gr=p*((dot(g,v,NT)-delta)*SCALE)
        grb=low(gr)
        gvb=dot(pbf,g,TN); gkb=dot(grb,qur,TN)
        gv=gvb if gv is None else gv+gvb
        gk=gkb if gk is None else gk+gkb
        gqu=dot(grb,k)
        pad=jnp.concatenate([gr,jnp.zeros((BLK,BLK),jnp.float32)],axis=1)
        gp=low(pltpu.roll(pad,0,1,stride=1,stride_axis=0))
        gpt_acc[w0:w0+W,:]+=dot(gp,qvr,TN)
        gqv=dot(gp,pt_ref[w0:w0+W,:])
        gq_ref[i0:i0+BLK,:]=low(dot(flip,low(gqu+gqv)))
        a=jnp.sum(gqu,axis=0,keepdims=True); c=jnp.sum(gqv,axis=0,keepdims=True)
        su=a if su is None else su+a; sv=c if sv is None else sv+c
    gpt_ref[...]=gpt_acc[...].astype(jnp.bfloat16)
    gk_ref[...]=jnp.where(first,gk[:T],gk[T:]); gv_ref[...]=jnp.where(first,gv[:T],gv[T:])
    gko_ref[...]=jnp.where(first,gk[T:],gk[:T]).astype(jnp.bfloat16); gvo_ref[...]=jnp.where(first,gv[T:],gv[:T]).astype(jnp.bfloat16)
    gb_ref[...]=jnp.concatenate([su,sv,jnp.zeros((6,su.shape[1]),jnp.float32)],axis=0)

def col(rows,off=0): return pl.BlockSpec((rows,HD),lambda h,off=off:(0,h+off))
def attn_bwd(sc,qkv,kvo,pt,pb,g,at,p):
    T=qkv.shape[0]; D=qkv.shape[1]//3; H=D//HD
    f32=jnp.float32; bf=jnp.bfloat16
    return pl.pallas_call(attn_bwd_kernel,grid=(H,),
        in_specs=[pl.BlockSpec(memory_space=pltpu.SMEM),col(T),col(T,H),col(T,2*H),col(T),col(T,H),col(3*T),col(pb.shape[0]),col(T),col(T),pl.BlockSpec((1,T,2*T),lambda h:(h,0,0))],
        out_specs=[col(T)]*5+[col(3*T),col(8)],
        out_shape=[jax.ShapeDtypeStruct((T,D),bf),jax.ShapeDtypeStruct((T,D),f32),jax.ShapeDtypeStruct((T,D),f32),jax.ShapeDtypeStruct((T,D),bf),jax.ShapeDtypeStruct((T,D),bf),jax.ShapeDtypeStruct((3*T,D),bf),jax.ShapeDtypeStruct((8,D),f32)],
        scratch_shapes=[pltpu.VMEM((3*T,HD),f32)],
        compiler_params=pltpu.CompilerParams(vmem_limit_bytes=48*2**20),
        cost_estimate=pl.CostEstimate(flops=H*T*2*T*HD*2*6,bytes_accessed=30*2**20,transcendentals=0),
    )(sc,qkv,qkv,qkv,kvo,kvo,pt,pb,g,at,p)

def reduce_kernel(plan, zfirst, nz, nops, *refs):
    n=len(plan)
    refs=list(refs)
    take=lambda m: [refs.pop(0) for _ in range(m)]
    ops=take(nops); ready,small,gi=take(3)
    out,out_s,gi_o,far,far_s=take(5)
    tw,tsm,sw,ssm,cw,csm,ab,bb=take(8)
    x1=take(n); y1=take(n); x2=take(n); y2=take(n); zb=take(n)
    (cs,cr,x1s,x1r,y1s,y1r,x2s,x2r,y2s,y2r,axs,axr,ays,ayr,aas,aar,abs_,abr,acs,acr,zrs,zrr,zls,zlr,own,cld,loc,opsem,fs,frv,keeps)=refs
    k=place(); dp,z,c=k["dp"],k["z"],k["c"]
    bx=k["p"]%2; by=k["p"]//2
    tcore=z//2; tdp=dp-c+tcore
    bar=pltpu.get_barrier_semaphore()
    def sig(dev): pl.semaphore_signal(bar,inc=1,device_id=dev,device_id_type=MESH)
    for a in ("core","xn","yn"): sig((k[a],z))
    for ok,zz in ((z>0,z-1),(z<nz-1,z+1)):
        @pl.when(ok)
        def _(): sig((dp,zz))
    for u in range(2):
        @pl.when(jnp.logical_or(tcore!=c, 2*c+u!=z))
        def _(): sig((tdp,2*c+u))
    one=lambda b: jnp.where(b,1,0)
    pl.semaphore_wait(bar,3+one(z>0)+one(z<nz-1)+2-one(tcore==c))
    def rc(src,dst,s,r,dev):
        return pltpu.make_async_remote_copy(src_ref=src,dst_ref=dst,send_sem=s,recv_sem=r,device_id=dev,device_id_type=MESH)
    xn=(k["xn"],z); yn=(k["yn"],z); cn=(k["core"],z)
    nt=tw.shape[0]; nsnd=sw.shape[0]; nc=cw.shape[0]
    big=lambda i: len(plan[i])>0
    tb=lambda i: tw.at[i%nt] if big(i) else tsm
    sb=lambda i: sw.at[i%nsnd] if big(i) else ssm
    cb=lambda i: cw.at[i%nc] if big(i) else csm
    fb=lambda i: far.at[i] if big(i) else far_s
    ob=lambda i: out.at[i] if big(i) else out_s
    half=lambda i: 128 if big(i) else 16
    A=lambda i: pl.ds(0,half(i))
    B=lambda i: pl.ds(half(i),half(i))
    send_c=lambda i: rc(sb(i),fb(i),cs.at[i],cr.at[i],cn)
    load_c=lambda i: pltpu.make_async_copy(fb(i),cb(i),cld.at[i])
    zf=lambda i: i in zfirst
    def shard(i,r,*rest):
        return r.at[(z,)+rest] if zf(i) else r.at[(slice(None),)+rest]
    send_x1=lambda i: rc(shard(i,tb(i),slice(None),1-bx,A(i)),x1[i],x1s.at[i],x1r.at[i],xn)
    send_y1=lambda i: rc(shard(i,tb(i),1-by,slice(None),B(i)),y1[i],y1s.at[i],y1r.at[i],yn)
    send_x2=lambda i: rc(shard(i,tb(i),1-by,bx,A(i)),x2[i],x2s.at[i],x2r.at[i],yn)
    send_y2=lambda i: rc(shard(i,tb(i),by,1-bx,B(i)),y2[i],y2s.at[i],y2r.at[i],xn)
    line=lambda i,t: tb(i).at[t] if zf(i) else tb(i).at[t,by,bx]
    send_r=lambda i,t: rc(line(i,t),zb[i].at[t],zrs.at[i,t],zrr.at[i,t],(dp,z+1))
    send_l=lambda i,t,last: rc(line(i,t),zb[i].at[nz if last else t],zls.at[i,t],zlr.at[i,t],(dp,z-1))
    mine=lambda i: tb(i).at[z,by,bx]
    send_ax=lambda i: rc(mine(i),ob(i).at[by,bx,c],axs.at[i],axr.at[i],xn)
    send_ay=lambda i: rc(mine(i),ob(i).at[by,bx,c],ays.at[i],ayr.at[i],yn)
    keep_a=lambda i: pltpu.make_async_copy(mine(i),ob(i).at[by,bx,c],loc.at[i])
    send_aa=lambda i: rc(ob(i).at[by,1-bx,c,A(i)],ob(i).at[by,1-bx,c,A(i)],aas.at[i],aar.at[i],yn)
    send_ab=lambda i: rc(ob(i).at[1-by,bx,c,B(i)],ob(i).at[1-by,bx,c,B(i)],abs_.at[i],abr.at[i],xn)
    send_ac=lambda i: rc(ob(i).at[:,:,c],ob(i).at[:,:,c],acs.at[i],acr.at[i],cn)
    def add(dst,src):
        dst[...]=(dst[...].astype(jnp.float32)+src[...].astype(jnp.float32)).astype(jnp.bfloat16)
    def loop(m,f):
        lax.fori_loop(0,m,lambda j,_: (f(j),0)[1],0)
    def move(u): return rc(gi.at[u],gi_o.at[z%2],fs.at[u],frv.at[z%2],(tdp,2*c+u))
    keep=pltpu.make_async_copy(gi.at[z%2],gi_o.at[z%2],keeps.at[0])
    def operand(i):
        if len(plan[i])==5:
            l,r,zs,lo,ro=plan[i]; s=i%2
            cps=[pltpu.make_async_copy(ops[l].at[:,pl.ds(t*zs+lo,256)],ab.at[s,t],opsem.at[s,t]) for t in range(nz)]
            return cps+[pltpu.make_async_copy(ops[r].at[:,pl.ds(ro,1024)],bb.at[s],opsem.at[s,nz])]
        if big(i):
            q=[(yy,xx) for yy in range(2) for xx in range(2)]
            cols=lambda yy,xx,cc: pl.ds(pl.multiple_of((yy*4+xx*2+cc)*128,128),128)
            return ([pltpu.make_async_copy(ready.at[:,:,cols(yy,xx,c)],tb(i).at[:,yy,xx],opsem.at[i%2,yy*2+xx]) for yy,xx in q]
                +[pltpu.make_async_copy(ready.at[:,:,cols(yy,xx,1-c)],sb(i).at[:,yy,xx],opsem.at[i%2,4+yy*2+xx]) for yy,xx in q])
        return [pltpu.make_async_copy(small.at[:,:,:,c],tb(i),opsem.at[i%2,0]),pltpu.make_async_copy(small.at[:,:,:,1-c],sb(i),opsem.at[i%2,1])]
    def drain(i):
        for f in (send_x1,send_y1,send_x2,send_y2,send_ax,send_ay): f(i).wait_send()
        for t in range(nz):
            @pl.when(z<t)
            def _(): send_r(i,t).wait_send()
            @pl.when(z>t)
            def _(): send_l(i,t,False).wait_send()
    bigs=[i for i in range(n) if big(i)]
    def sl(i):
        if big(i) and i-nt in bigs: drain(i-nt)
        if big(i) and i-nsnd in bigs: send_c(i-nsnd).wait_send()
        for cp in operand(i): cp.start()
    def s0(i):
        for cp in operand(i): cp.wait()
        if len(plan[i])==5:
            s=i%2; T=tb(i); Sb=sb(i)
            cut=lambda cc: jnp.concatenate([bb[s,:,pl.ds(pl.multiple_of((2*q+cc)*128,128),128)] for q in range(4)],axis=1)
            def make(cc,dst):
                right=cut(cc)
                def f(t):
                    tile=lax.dot_general(ab[s,t],right,TN,preferred_element_type=jnp.float32).astype(jnp.bfloat16)
                    for q in range(4): dst[t,q//2,q%2]=tile[:,128*q:128*q+128]
                loop(nz,f)
            make(1-c,Sb)
            send_c(i).start()
            make(c,T)
        else:
            send_c(i).start()
    def s1a(i):
        send_c(i).wait_recv(); load_c(i).start()
    def s1(i):
        load_c(i).wait()
        T=tb(i); C=cb(i)
        loop(nz*4,lambda j: add(T.at[j//4,(j//2)%2,j%2],C.at[j//4,(j//2)%2,j%2]))
        if zf(i): line_start(i)
        else: xy_start(i)
    def xy_start(i):
        send_x1(i).start(); send_y1(i).start()
    def line_start(i):
        @pl.when(z==0)
        def _():
            for t in reversed(range(1,nz)): send_r(i,t).start()
        @pl.when(z==nz-1)
        def _():
            for t in range(nz-1): send_l(i,t,t==nz-2).start()
    def s2(i):
        T=tb(i)
        send_x1(i).wait_recv()
        if zf(i): loop(2,lambda j: add(T.at[z,j,bx,A(i)],x1[i].at[j]))
        else: loop(nz*2,lambda j: add(T.at[j//2,j%2,bx,A(i)],x1[i].at[j//2,j%2]))
        send_x2(i).start()
        send_y1(i).wait_recv()
        if zf(i): loop(2,lambda j: add(T.at[z,by,j,B(i)],y1[i].at[j]))
        else: loop(nz*2,lambda j: add(T.at[j//2,by,j%2,B(i)],y1[i].at[j//2,j%2]))
        send_y2(i).start()
    def s3(i):
        T=tb(i)
        send_x2(i).wait_recv()
        if zf(i): add(T.at[z,by,bx,A(i)],x2[i])
        else: loop(nz,lambda j: add(T.at[j,by,bx,A(i)],x2[i].at[j]))
        send_y2(i).wait_recv()
        if zf(i): add(T.at[z,by,bx,B(i)],y2[i])
        else: loop(nz,lambda j: add(T.at[j,by,bx,B(i)],y2[i].at[j]))
        if zf(i): spread_start(i)
        else: line_start(i)
    def add_line(i,t,slot):
        if zf(i): loop(4,lambda j: add(tb(i).at[t,j//2,j%2],zb[i].at[slot,j//2,j%2]))
        else: add(line(i,t),zb[i].at[slot])
    def hop(h,i):
        @pl.when(z==h)
        def _():
            for t in reversed(range(h+1,nz)):
                send_r(i,t).wait_recv()
                add_line(i,t,t)
                send_r(i,t).start()
        @pl.when(z==nz-1-h)
        def _():
            for t in range(nz-1-h):
                send_l(i,t,False).wait_recv()
                add_line(i,t,t)
                send_l(i,t,t==nz-2-h).start()
    def s6(i):
        @pl.when(z>0)
        def _():
            send_r(i,z).wait_recv()
            add_line(i,z,z)
        @pl.when(z<nz-1)
        def _():
            send_l(i,z,False).wait_recv()
            add_line(i,z,nz)
        if zf(i): xy_start(i)
        else: spread_start(i)
    def spread_start(i):
        send_ax(i).start(); send_ay(i).start(); keep_a(i).start()
    def s7(i):
        send_ax(i).wait_recv(); send_aa(i).start()
        send_ay(i).wait_recv(); send_ab(i).start()
    def s8(i):
        keep_a(i).wait()
        send_aa(i).wait_recv(); send_ab(i).wait_recv(); send_ac(i).start()
    def start_moves():
        for u in range(2):
            @pl.when(jnp.logical_or(tcore!=c,2*c+u!=z))
            def _(): move(u).start()
        @pl.when(tcore==c)
        def _(): keep.start()
    hops=[functools.partial(hop,h) for h in range(1,nz-1)]
    xy_stages=list(zip([sl,s0,s1a,s1,s2,s3]+hops+[s6,s7,s8],XY_LAGS))
    z_stages=list(zip([sl,s0,s1a,s1]+hops+[s6,s2,s3,s7,s8],Z_LAGS))
    for s in range(n+max(XY_LAGS+Z_LAGS)):
        if s==MOVE_AT: start_moves()
        todo=[(d,f,i) for i in range(n) for f,d in (z_stages if zf(i) else xy_stages) if i+d==s]
        for d,f,i in sorted(todo,key=lambda x:-x[0]): f(i)
    for i in range(n):
        if not (big(i) and i+nt in bigs): drain(i)
        if not (big(i) and i+nsnd in bigs): send_c(i).wait_send()
        send_aa(i).wait_send(); send_ab(i).wait_send()
        send_ac(i).wait()
    for u in range(2):
        @pl.when(jnp.logical_or(tcore!=c,2*c+u!=z))
        def _():
            move(u).wait_send()
            rc(gi.at[u],gi_o.at[u],fs.at[u],frv.at[u],(tdp,2*c+u)).wait_recv()
    @pl.when(tcore==c)
    def _(): keep.wait()

XY_LAGS=(0,1,2,3,5,6,7,8,9,10,11)
Z_LAGS=(0,1,2,3,5,6,8,9,10,11,12)
SLOTS=14
MOVE_AT=0
def reduce_call(ops,ready,small,gi,plan,zfirst,nz,cid):
    n=len(plan); nb=sum(len(x)>0 for x in plan); bf=jnp.bfloat16
    rows=ops[0].shape[0]
    any_=pl.BlockSpec(memory_space=pl.ANY)
    sd=jax.ShapeDtypeStruct
    outs=[sd((nb,2,2,2,256,128),bf),sd((2,2,2,32,128),bf),sd(gi.shape,gi.dtype),sd((nb,nz,2,2,256,128),bf),sd((nz,2,2,32,128),bf)]
    V=pltpu.VMEM; S=pltpu.SemaphoreType.DMA
    h=[128 if len(x) else 16 for x in plan]
    lead=lambda i: () if i in zfirst else (nz,)
    scratch=[V((SLOTS,nz,2,2,256,128),bf),V((nz,2,2,32,128),bf),V((2,nz,2,2,256,128),bf),V((nz,2,2,32,128),bf),V((2,nz,2,2,256,128),bf),V((nz,2,2,32,128),bf),
        V((2,nz,rows,256),bf),V((2,rows,1024),bf)]
    scratch+=[V(lead(i)+(2,h[i],128),bf) for i in range(n)]*2+[V(lead(i)+(h[i],128),bf) for i in range(n)]*2
    scratch+=[V((nz+1,)+((2,2) if i in zfirst else ())+(2*h[i],128),bf) for i in range(n)]
    scratch+=[S((n,))]*20+[S((n,nz))]*4+[S((1,)),S((n,)),S((n,)),S((2,8)),S((2,)),S((2,)),S((1,))]
    return pl.pallas_call(functools.partial(reduce_kernel,plan,zfirst,nz,len(ops)),out_shape=outs,in_specs=[any_]*(len(ops)+3),out_specs=[any_]*len(outs),
        scratch_shapes=scratch,
        compiler_params=pltpu.CompilerParams(collective_id=cid,has_side_effects=True,vmem_limit_bytes=58*2**20),
        cost_estimate=pl.CostEstimate(flops=2*n*rows*2**20,bytes_accessed=100*2**20,transcendentals=0),
    )(*ops,ready,small,gi)[:3]

def grad_plan(seq_count):
    plan, names = [], {}
    def weight(name, left, right, blocks, shrink):
        names[name] = len(plan), blocks
        for j in range(blocks):
            plan.append((left, right, 256 * blocks, 256 * j, 0) if shrink else (left, right, 256, 0, 1024 * j))
    weight("w4", 0, 1, 4, True)
    weight("w3", 2, 3, 4, False)
    weight("wco", 4, 5, 1, False)
    weight("wci", 6, 7, 2, False)
    weight("wo", 8, 9, 1, False)
    weight("wqkv", 10, 11, 3, False)
    names["wpos"] = len(plan), 1
    plan.append((0,))
    weight("w2", 12, 13, 4, True)
    weight("w1", 14, 15, 4, False)
    plan.append(())
    return plan, names

WIDEN_SLOTS = 4


def widen_kernel(spots, blocks_ref, *refs):
    outs, (narrow, wide, in_sem, out_sem) = refs[:-4], refs[-4:]
    count = len(spots)

    def fetch(i):
        return pltpu.make_async_copy(blocks_ref.at[i], narrow.at[i % WIDEN_SLOTS], in_sem.at[i % WIDEN_SLOTS])

    def put(i):
        which, row, column = spots[i]
        target = outs[which].at[pl.ds(row, 256), pl.ds(column, 1024)]
        return pltpu.make_async_copy(wide.at[i % WIDEN_SLOTS], target, out_sem.at[i % WIDEN_SLOTS])

    for i in range(WIDEN_SLOTS - 1):
        fetch(i).start()
    for i in range(count):
        if i + WIDEN_SLOTS - 1 < count:
            fetch(i + WIDEN_SLOTS - 1).start()
        fetch(i).wait()
        if i >= WIDEN_SLOTS:
            put(i - WIDEN_SLOTS).wait()
        slot = i % WIDEN_SLOTS

        def cast(piece, _):
            wide[slot, :, pl.ds(pl.multiple_of(128 * piece, 128), 128)] = narrow[slot, piece].astype(jnp.float32)
            return 0

        lax.fori_loop(0, 8, cast, 0, unroll=True)
        put(i).start()
    for i in range(count - WIDEN_SLOTS, count):
        put(i).wait()


def widen(blocks, names):
    spots, shapes = [], []
    for which, (name, (first, length)) in enumerate(names.items()):
        tall = name in ("w2", "w4")
        spots += [(which, 256 * j if tall else 0, 0 if tall else 1024 * j) for j in range(length)]
        shapes.append(jax.ShapeDtypeStruct((256 * length, 1024) if tall else (256, 1024 * length), jnp.float32))
    anywhere = pl.BlockSpec(memory_space=pl.ANY)
    wide = pl.pallas_call(
        functools.partial(widen_kernel, spots),
        in_specs=[anywhere],
        out_specs=[anywhere] * len(shapes),
        out_shape=shapes,
        scratch_shapes=[
            pltpu.VMEM((WIDEN_SLOTS, 8, 256, 128), jnp.bfloat16),
            pltpu.VMEM((WIDEN_SLOTS, 256, 1024), jnp.float32),
            pltpu.SemaphoreType.DMA((WIDEN_SLOTS,)),
            pltpu.SemaphoreType.DMA((WIDEN_SLOTS,)),
        ],
        compiler_params=pltpu.CompilerParams(vmem_limit_bytes=56 * 2**20),
        cost_estimate=pl.CostEstimate(flops=0, bytes_accessed=36 * 2**20, transcendentals=0),
    )(blocks)
    return dict(zip(names, wide))


def reduce_all(ops, ready, g_small, grad_input, seq_count):
    width = D // seq_count
    pieces = width // 128
    small = g_small.reshape(32, seq_count, pieces, 128).transpose(1, 2, 0, 3)
    small = jnp.pad(small, ((0, 0), (0, 8 - pieces), (0, 0), (0, 0))).reshape(seq_count, 2, 2, 2, 32, 128)
    plan, names = grad_plan(seq_count)
    by_line = {i for i in range(1, len(plan) - 1, 3)}
    blocks, small, grad_input = reduce_call(ops, ready, small, grad_input, plan, by_line, seq_count, 1)
    count = lax.axis_size("dp")
    if count > 8:
        groups = [[i + 8 * quad for quad in range(count // 8)] for i in range(8)]
        blocks, small = (lax.psum(x, "dp", axis_index_groups=groups) for x in (blocks, small))
    sums = widen(blocks.reshape(-1, 8, 256, 128), names)
    sums["wpos"] = sums["wpos"].T
    small = small.reshape(8, 32, 128)[:pieces].transpose(1, 0, 2).reshape(32, width).astype(jnp.float32)
    return sums, small, grad_input


def layer_norm(stream, gain, offset):
    average = jnp.mean(stream, axis=-1, keepdims=True)
    centred = stream - average
    spread = jnp.mean(centred * centred, axis=-1, keepdims=True)
    return centred * lax.rsqrt(spread + EPSILON) * gain + offset


def layer_norm_back(stream, gain, grad):
    average = jnp.mean(stream, axis=-1, keepdims=True)
    centred = stream - average
    spread = jnp.mean(centred * centred, axis=-1, keepdims=True)
    inverse = lax.rsqrt(spread + EPSILON)
    unit = centred * inverse
    scaled = grad * gain
    grad_stream = inverse * (
        scaled
        - jnp.mean(scaled, axis=-1, keepdims=True)
        - unit * jnp.mean(scaled * unit, axis=-1, keepdims=True)
    )
    return grad_stream, jnp.sum(grad * unit, axis=0), jnp.sum(grad, axis=0)


def swish(value):
    return value * jax.nn.sigmoid(value)


def swish_back(value, grad):
    gate = jax.nn.sigmoid(value)
    return grad * gate * (1.0 + value * (1.0 - gate))


def position_tables(first_row, rows, length, features):
    fine = 32
    column = lax.broadcasted_iota(jnp.int32, (1, features), 1)
    odd = column % 2 == 1
    frequency = jnp.exp((column // 2).astype(jnp.float32) * (-2.0 * math.log(10000.0) / features))
    coarse_at = (length - 1 - first_row - fine * jnp.arange(rows // fine, dtype=jnp.int32)).astype(jnp.float32)
    fine_at = jnp.arange(fine, dtype=jnp.int32).astype(jnp.float32)
    coarse = coarse_at[:, None] * frequency
    small = fine_at[:, None] * frequency
    coarse_sin, coarse_cos = jnp.sin(coarse), jnp.cos(coarse)
    return jnp.where(odd, coarse_cos, coarse_sin), jnp.where(odd, -coarse_sin, coarse_cos), jnp.cos(small), jnp.sin(small)


def mm(left, right):
    return jnp.dot(left, right, preferred_element_type=jnp.float32)


def mm_nt(left, right):
    return lax.dot_general(left, right, NT, preferred_element_type=jnp.float32)


def mm_tn(left, right):
    return lax.dot_general(left, right, TN, preferred_element_type=jnp.float32).astype(jnp.bfloat16)


def pair_swap(value):
    count = lax.axis_size("dp")
    return lax.ppermute(value, "dp", [(i, i + 1 - 2 * (i % 2)) for i in range(count)])


def redistribute(value):
    dp_count, seq_count = lax.axis_size("dp"), lax.axis_size("seq")
    z = lax.axis_index("seq")
    routes = ([], [])
    for dp in range(dp_count):
        for zz in range(seq_count):
            a, b, c = zz // 2, zz % 2, dp % 2
            for which in range(2):
                routes[which].append(
                    (dp * seq_count + zz, (dp - c + a) * seq_count + 2 * c + (b + which) % 2)
                )
    low = z % 2 == 0
    straight = lax.ppermute(jnp.where(low, value[0], value[1]), ("dp", "seq"), routes[0])
    crossed = lax.ppermute(jnp.where(low, value[1], value[0]), ("dp", "seq"), routes[1])
    return jnp.stack([jnp.where(low, straight, crossed), jnp.where(low, crossed, straight)])


def with_halo(rows, core):
    margin = (KERNEL - 1) // 2
    got = pair_swap(jnp.where(core == 0, rows[-margin:], rows[:margin]))
    none = jnp.zeros_like(got)
    return jnp.concatenate([jnp.where(core == 1, got, none), rows, jnp.where(core == 0, got, none)], axis=0)


def shards(
    frames, cotangent, lengths, assignment, norm_gains, norm_biases, expand_one, shrink_one, qkv_weight,
    pos_weight, pos_biases, attn_out, conv_in, conv_depth, conv_out, expand_two, shrink_two,
):
    seq_count = lax.axis_size("seq")
    dp, z = lax.axis_index("dp"), lax.axis_index("seq")
    core = dp % 2
    own_length = lengths[assignment[dp - core + z // 2], z % 2]
    rows = 2 * frames.shape[2]
    tables = position_tables((1 - core) * rows, 3 * rows, 2 * rows, D)
    weights, small_all, x_in, cot, first_part = gather(
        [expand_one, shrink_one, qkv_weight, pos_weight, attn_out, conv_in, conv_out, expand_two, shrink_two],
        [norm_gains, norm_biases, conv_depth, pos_biases], frames[0], cotangent[0], own_length.reshape(1), tables, seq_count,
    )
    w1, w2, wqkv, _, wo, wci, wco, w3, w4 = weights
    h1, a1, s1, x1, ha, qkv, kv_other, sinusoid, ptab, prob, attn = first_part
    vectors = small_all.transpose(1, 0, 2).reshape(32, D).astype(jnp.float32)
    gains, biases, depth, pos_pair = vectors[0:6], vectors[6:12], vectors[12:17], vectors[16:24]
    pos_pair = jnp.concatenate([vectors[17:19], jnp.zeros((6, D), jnp.float32)], axis=0)
    x0 = x_in.reshape(rows, D).astype(jnp.float32)
    cot = cot.reshape(rows, D).astype(jnp.float32)
    valid = (core * rows + jnp.arange(rows, dtype=jnp.int32) < own_length).astype(jnp.float32)[:, None]

    scalars = jnp.stack([core, own_length]).astype(jnp.int32)
    x2 = x1 + mm(attn, wo)
    hc = layer_norm(x2, gains[2], biases[2]).astype(jnp.bfloat16)
    dbl = mm(hc, wci)
    gate = jax.nn.sigmoid(dbl[:, D:])
    m = (dbl[:, :D] * gate * valid).astype(jnp.bfloat16)
    rim = with_halo(m, core)
    cv = depth[0] * rim[0:rows]
    for tap in range(1, KERNEL):
        cv = cv + depth[tap] * rim[tap : tap + rows]
    sc = swish(layer_norm(cv, gains[3], biases[3])).astype(jnp.bfloat16)
    x3 = x2 + mm(sc, wco)
    h2 = layer_norm(x3, gains[4], biases[4]).astype(jnp.bfloat16)
    a2 = mm(h2, w3)
    s2 = swish(a2).astype(jnp.bfloat16)
    x4 = x3 + 0.5 * mm(s2, w4)
    encoded = layer_norm(x4, gains[5], biases[5]).astype(jnp.bfloat16)
    encoded = redistribute(encoded.reshape(2, rows // 2, D))

    gx4, gg5, gb5 = layer_norm_back(x4, gains[5], cot)
    go2 = (0.5 * gx4).astype(jnp.bfloat16)
    ga2 = swish_back(a2, mm_nt(go2, w4)).astype(jnp.bfloat16)
    back, gg4, gb4 = layer_norm_back(x3, gains[4], mm_nt(ga2, w3))
    gx3 = gx4 + back
    gco = gx3.astype(jnp.bfloat16)
    inner = layer_norm(cv, gains[3], biases[3])
    gcv, gg3, gb3 = layer_norm_back(cv, gains[3], swish_back(inner, mm_nt(gco, wco)))
    gcv = gcv.astype(jnp.bfloat16)
    grim = with_halo(gcv, core)
    gm = depth[0] * grim[KERNEL - 1 : KERNEL - 1 + rows]
    for tap in range(1, KERNEL):
        gm = gm + depth[tap] * grim[KERNEL - 1 - tap : KERNEL - 1 - tap + rows]
    g_depth = jnp.stack([
        jnp.sum(gcv.astype(jnp.float32) * rim[tap : tap + rows].astype(jnp.float32), axis=0) for tap in range(KERNEL)
    ])
    gm = gm * valid
    gdbl = jnp.concatenate(
        [(gm * gate).astype(jnp.bfloat16), (gm * dbl[:, :D] * gate * (1.0 - gate)).astype(jnp.bfloat16)], axis=1
    )
    back, gg2, gb2 = layer_norm_back(x2, gains[2], mm_nt(gdbl, wci))
    gx2 = gx3 + back
    gao = gx2.astype(jnp.bfloat16)
    gattn = mm_nt(gao, wo).astype(jnp.bfloat16)
    gq, gk, gv, gk_other, gv_other, gptab, g_pair = attn_bwd(scalars, qkv, kv_other, ptab, pos_pair, gattn, attn, prob)
    got = pair_swap(jnp.concatenate([gk_other, gv_other], axis=1))
    gk = (gk + got[:, :D]).astype(jnp.bfloat16)
    gv = (gv + got[:, D:]).astype(jnp.bfloat16)
    gqkv = jnp.concatenate([gq, gk, gv], axis=1)
    g_wpos = mm_tn(gptab, sinusoid).reshape(seq_count, D // seq_count, D)
    back, gg1, gb1 = layer_norm_back(x1, gains[1], mm_nt(gqkv, wqkv))
    gx1 = gx2 + back
    go1 = (0.5 * gx1).astype(jnp.bfloat16)
    ga1 = swish_back(a1, mm_nt(go1, w2)).astype(jnp.bfloat16)
    back, gg0, gb0 = layer_norm_back(x0, gains[0], mm_nt(ga1, w1))
    gx0 = gx1 + back
    g_small = jnp.concatenate(
        [jnp.stack([gg0, gg1, gg2, gg3, gg4, gg5, gb0, gb1, gb2, gb3, gb4, gb5]), g_depth, g_pair[:2], jnp.zeros((13, D), jnp.float32)],
        axis=0,
    ).astype(jnp.bfloat16)
    sums, s_small, grad_input = reduce_all(
        [s2, go2, h2, ga2, sc, gco, hc, gdbl, attn, gao, ha, gqkv, s1, go1, h1, ga1],
        g_wpos, g_small, gx0.astype(jnp.bfloat16).reshape(2, rows // 2, D), seq_count,
    )
    grad_input = grad_input.astype(jnp.float32)
    return (
        encoded[None], grad_input[None], s_small[0:6], s_small[6:12], sums["w1"], sums["w2"], sums["wqkv"],
        sums["wpos"], s_small[17:19], sums["wo"], sums["wci"], s_small[12:17], sums["wco"], sums["w3"], sums["w4"],
    )


def solution(mesh):
    rows, columns = P("seq", None), P(None, "seq")
    act = P("dp", None, "seq", None)
    return jax.shard_map(
        shards,
        mesh=mesh,
        in_specs=(act, act, P(), P(), columns, columns, rows, rows, rows, columns, columns, rows, rows, columns, rows, rows, rows),
        out_specs=(act, act, columns, columns, rows, rows, rows, columns, columns, rows, rows, columns, rows, rows, rows),
        check_vma=False,
    )
```
